32 devices in a mesh: segment: 4 (over y, core), ha: 4 (over z), wa: 2 (over x).
Axes of the slice: x: 2, y: 2, z: 4, core: 2. Of those that a mesh axis runs over, the one named last changes fastest.
Arguments:
- latent: bfloat16 [4, 8, 1536], P(None, 'ha', 'wa'), may hold values from -6 to 6
- cache_a: bfloat16 [2, 8, 1536], P(None, 'ha', 'wa'), may hold values from -6 to 6
- cache_b: bfloat16 [2, 16, 1536], P(None, 'ha', 'wa'), may hold values from -4 to 4
- cache_c: bfloat16 [2, 32, 3072], P(None, 'ha', 'wa'), may hold values from -4 to 4
- cache_d: bfloat16 [2, 64, 3072], P(None, 'ha', 'wa'), may hold values from -4 to 4
- conv_pack: bfloat16 [4, 10368, 384], P('segment', 'ha', 'wa'), as said below
- up_pack: bfloat16 [4, 384, 1728], P('segment', 'wa', 'ha'), as said below
Outputs:
- decoded: bfloat16 [4, 128, 6144], P('segment', 'ha', 'wa')
The draws below stay inside these ranges and needn't reach their ends.
Inputs may be any that keep to these rules, and one draw needn't show every extreme that they name: `conv_pack`: rows past 27 cin and columns other than multiples of 384 / cm in a section's row are not read. `up_pack`: rows other than multiples of 384 / cm and columns past 9 co in a section's row are not read.
All inputs are finite; a program needn't handle non-finite values.
Results may differ from the reference program's by a relative error of at most 0.018.
Values may be sent and summed in bfloat16 or wider, within the bound.
No kernel may reach another device: no remote copies, remote signals or barrier semaphores. Data moves between devices by JAX's collectives and lax.ppermute only.
A program may use at most 192 MiB of HBM per device.

```python
import jax
import jax.numpy as jnp
from jax import lax

WIDE = 384
MID = 192
NARROW = 96
FRAMES = 4
H0 = 8
W0 = 4


def draw_conv_pack(key, part):
    fans = jnp.array([27.0 * WIDE, 27.0 * MID, 27.0 * MID, 27.0 * NARROW], jnp.float32)
    values = jax.random.normal(key, (4, 27 * WIDE, WIDE), jnp.float32)
    return (values * lax.rsqrt(fans)[:, None, None]).astype(jnp.bfloat16)


def draw_up_pack(key, part):
    fans = jnp.array([9.0 * WIDE, 9.0 * WIDE, 9.0 * MID, 9.0 * NARROW], jnp.float32)
    values = jax.random.normal(key, (4, WIDE, 9 * MID), jnp.float32)
    return (values * lax.rsqrt(fans)[:, None, None]).astype(jnp.bfloat16)


def block_levels(rng, dims, cuts, low, largest):
    loudness, own = 1.0, jax.random.fold_in(rng, 6)
    for position, parts in cuts:
        draws = jnp.exp(jax.random.uniform(jax.random.fold_in(own, position), (parts,), jnp.float32, low / len(cuts), largest / len(cuts)))
        loudness = loudness * jnp.repeat(draws, dims[position] // parts).reshape([-1 if axis == position else 1 for axis in range(len(dims))])
    return loudness


def gaussian(own_key, shape, spread, reach, split=(), kind=jnp.bfloat16):
    loudness = block_levels(own_key, shape, split, -0.22, 0.18) if split else 1.0
    values = jax.random.normal(own_key, shape, jnp.float32) * spread * loudness
    return jnp.minimum(jnp.maximum(values, -reach), reach).astype(kind)


def setup_inputs(seed: int = 0) -> dict:
    keys = jax.random.split(jax.random.key(seed), 8)
    latent = gaussian(keys[0], (FRAMES, H0, W0 * WIDE), 1.0, 6.0, ((1, 4), (2, 2)))
    cache_a = gaussian(keys[1], (2, H0, W0 * WIDE), 1.0, 6.0, ((1, 4), (2, 2)))
    cache_b = gaussian(keys[2], (2, 2 * H0, 2 * W0 * MID), 0.6, 4.0, ((1, 4), (2, 2)))
    cache_c = gaussian(keys[3], (2, 4 * H0, 4 * W0 * MID), 0.6, 4.0, ((1, 4), (2, 2)))
    cache_d = gaussian(keys[4], (2, 8 * H0, 8 * W0 * NARROW), 0.6, 4.0, ((1, 4), (2, 2)))
    conv_pack = draw_conv_pack(jax.random.fold_in(keys[7], 71), 0)
    up_pack = draw_up_pack(jax.random.fold_in(keys[7], 71), 0)
    return {"latent": latent, "cache_a": cache_a, "cache_b": cache_b, "cache_c": cache_c, "cache_d": cache_d, "conv_pack": conv_pack, "up_pack": up_pack}


EPSILON = 1e-06

def layer_table():
    return ((WIDE, WIDE, MID), (MID, WIDE, MID), (MID, MID, NARROW), (NARROW, NARROW, NARROW))

def causal_conv(stacked, kernel):
    result = lax.conv_general_dilated(stacked.astype(jnp.float32)[None], kernel.astype(jnp.float32), (1, 1, 1), ((0, 0), (1, 1), (1, 1)), dimension_numbers=('NDHWC', 'DHWIO', 'NDHWC'), precision=lax.Precision.HIGHEST)
    return result[0, 0]

def activate(conv_sum):
    inverse = lax.rsqrt(lax.optimization_barrier(jnp.mean(conv_sum * conv_sum, axis=-1, keepdims=True)) + EPSILON)
    return jax.nn.silu(conv_sum * inverse).astype(jnp.bfloat16)

def upsample_conv(hidden, kernel):
    expanded = jnp.repeat(jnp.repeat(hidden, 2, axis=0), 2, axis=1).astype(jnp.float32)
    result = lax.conv_general_dilated(expanded[None], kernel.astype(jnp.float32), (1, 1), ((1, 1), (1, 1)), dimension_numbers=('NHWC', 'HWIO', 'NHWC'), precision=lax.Precision.HIGHEST)
    return result[0].astype(jnp.bfloat16)

def reference(latent, cache_a, cache_b, cache_c, cache_d, conv_pack, up_pack):
    layers = layer_table()
    frames = latent.shape[0]
    caches = (cache_a, cache_b, cache_c, cache_d)
    segment_in = latent.reshape(frames, latent.shape[1], latent.shape[2] // WIDE, WIDE)
    for level in range(4):
        width_in, width_mid, width_out = layers[level]
        stride_step = WIDE // width_mid
        kernel = conv_pack[level, :27 * width_in, ::stride_step].reshape(3, 3, 3, width_in, width_mid)
        up_kernel = up_pack[level, ::stride_step, :9 * width_out].reshape(width_mid, 3, 3, width_out).transpose(1, 2, 0, 3)
        height = segment_in.shape[1]
        width = segment_in.shape[2]
        earlier = caches[level].reshape(2, height, width, width_in)
        history = [earlier[0], earlier[1]]
        results = []
        for moment in range(frames):
            current = segment_in[moment]
            hidden = activate(causal_conv(jnp.stack([history[0], history[1], current]), kernel))
            results.append(upsample_conv(hidden, up_kernel))
            history = [history[1], current]
        segment_in = jnp.stack(results)
    return segment_in.reshape(frames, segment_in.shape[1], -1)
```

```python
from functools import partial

import jax
import jax.numpy as jnp
from jax import lax
from jax.experimental import pallas as pl
from jax.experimental.pallas import tpu as pltpu
from jax.sharding import PartitionSpec as P

WIDE = 384
MID = 192
NARROW = 96


EPSILON = 1e-06


def shortened(array):

    def short(part):
        return part.astype(jnp.bfloat16) if part.dtype == jnp.float32 else part

    return jax.tree.map(short, array)


def passed_along(value, axis, steps):
    count = lax.axis_size(axis)
    initial, last = (max(0, -steps), min(count, count - steps))
    return lax.ppermute(value, axis, [(source, source + steps) for source in range(initial, last)])


def layer_table():
    return ((WIDE, WIDE, MID), (MID, WIDE, MID), (MID, MID, NARROW), (NARROW, NARROW, NARROW))


def round_up(amount):
    return -(-amount // 128) * 128


def volume(target):
    amount = 1
    for extent in target:
        amount = amount * extent
    return amount


def flat_pad(tensor, length):
    leading = tensor.shape[0]
    packed = tensor.reshape(leading, -1)
    return jnp.pad(packed, ((0, 0), (0, length - packed.shape[1])))


def reshaped(packed, target):
    return packed[:, : volume(target)].reshape((packed.shape[0],) + tuple(target))


def add_rows(tensor, from_above, from_below):
    leading, height, width, channels = tensor.shape
    upper = reshaped(from_above, (1, width, channels))
    lower = reshaped(from_below, (1, width, channels))
    return jnp.concatenate([upper, tensor, lower], axis=1)


def add_cols(tensor, from_left, from_right):
    leading, height, width, channels = tensor.shape
    before = reshaped(from_left, (height, 1, channels))
    after = reshaped(from_right, (height, 1, channels))
    return jnp.concatenate([before, tensor, after], axis=2)


def trade_rows(upper_rim, bottom):
    return (
        jax.tree.map(
            lambda part, own: part.astype(own.dtype),
            passed_along(shortened(bottom), "ha", 1),
            bottom,
        ),
        jax.tree.map(
            lambda part, own: part.astype(own.dtype),
            passed_along(shortened(upper_rim), "ha", -1),
            upper_rim,
        ),
    )


def trade_cols(left_rim, right_rim):
    return (
        jax.tree.map(
            lambda part, own: part.astype(own.dtype),
            passed_along(shortened(right_rim), "wa", 1),
            right_rim,
        ),
        jax.tree.map(
            lambda part, own: part.astype(own.dtype),
            passed_along(shortened(left_rim), "wa", -1),
            left_rim,
        ),
    )


def causal_conv(stacked, kernel):
    result = lax.conv_general_dilated(
        stacked[None],
        kernel,
        (1, 1, 1),
        "VALID",
        dimension_numbers=("NDHWC", "DHWIO", "NDHWC"),
        preferred_element_type=jnp.float32,
    )
    return result[0, 0]


def activate(conv_sum):
    inverse = lax.rsqrt(jnp.mean(conv_sum * conv_sum, axis=-1, keepdims=True) + EPSILON)
    return jax.nn.silu(conv_sum * inverse).astype(jnp.bfloat16)


def upsample_conv(hidden_ext, kernel):
    expanded = jnp.repeat(jnp.repeat(hidden_ext, 2, axis=0), 2, axis=1)[1:-1, 1:-1]
    result = lax.conv_general_dilated(
        expanded[None],
        kernel,
        (1, 1),
        "VALID",
        dimension_numbers=("NHWC", "HWIO", "NHWC"),
        preferred_element_type=jnp.float32,
    )
    return result[0].astype(jnp.bfloat16)


def per_device(latent, cache_a, cache_b, cache_c, cache_d, conv_pack, up_pack):
    frames = latent.shape[0]
    tile_rows = latent.shape[1]
    tile_cols = latent.shape[2] // WIDE
    layers = layer_table()
    section = lax.axis_index("segment")
    segments = lax.axis_size("segment")
    final_segment = segments - 1
    input_shapes = [
        (tile_rows << level, tile_cols << level, layers[level][0]) for level in range(4)
    ]
    mid_shapes = [(tile_rows << level, tile_cols << level, layers[level][1]) for level in range(4)]
    out_shapes = [
        (tile_rows << level + 1, tile_cols << level + 1, layers[level][2]) for level in range(4)
    ]
    ext_shapes = [(target[0] + 2, target[1] + 2, target[2]) for target in input_shapes]
    all_shapes = input_shapes + mid_shapes
    row_length = round_up(max((target[1] * target[2] for target in all_shapes)))
    column_length = round_up(max(((target[0] + 2) * target[2] for target in all_shapes)))
    size_input = round_up(max((volume(target) for target in input_shapes)))
    size_middle = round_up(max((volume(target) for target in mid_shapes)))
    size_extended = round_up(max((volume(target) for target in ext_shapes)))
    size_output = round_up(max((volume(target) for target in out_shapes)))
    final_shape = out_shapes[3]
    final_count = volume(final_shape)
    conv_rows, up_rows = (
        lax.all_gather(conv_pack, "ha", axis=1, tiled=True),
        lax.all_gather(up_pack, "ha", axis=2, tiled=True),
    )
    conv_all, up_all = (
        lax.all_gather(conv_rows, "wa", axis=2, tiled=True),
        lax.all_gather(up_rows, "wa", axis=1, tiled=True),
    )

    def conv_kernel(level):
        width_in, width_mid, width_out = layers[level]
        columns = conv_all[0, : 27 * width_in, :: WIDE // width_mid]
        return columns.reshape(3, 3, 3, width_in, columns.shape[1])

    def up_kernel(level):
        width_in, width_mid, width_out = layers[level]
        rows_used = up_all[0, :: WIDE // width_mid, : 9 * width_out]
        return rows_used.reshape(width_mid, 3, 3, width_out).transpose(1, 2, 0, 3)

    conv_kernels = [conv_kernel(level) for level in range(4)]
    up_kernels = [up_kernel(level) for level in range(4)]

    def row_rims(packed, shapes):

        def rows_branch(level, packed):
            tensor = reshaped(packed, shapes[level])
            return (flat_pad(tensor[:, :1], row_length), flat_pad(tensor[:, -1:], row_length))

        upper_rim, bottom = lax.switch(
            section, [partial(rows_branch, level) for level in range(4)], packed
        )
        return trade_rows(upper_rim, bottom)

    def extend(packed, shapes):
        from_above, from_below = row_rims(packed, shapes)

        def cols_branch(level, packed, from_above, from_below):
            tensor = add_rows(reshaped(packed, shapes[level]), from_above, from_below)
            return (
                flat_pad(tensor[:, :, :1], column_length),
                flat_pad(tensor[:, :, -1:], column_length),
            )

        left_rim, right_rim = lax.switch(
            section,
            [partial(cols_branch, level) for level in range(4)],
            packed,
            from_above,
            from_below,
        )
        from_left, from_right = trade_cols(left_rim, right_rim)
        return (from_above, from_below, from_left, from_right)

    def assemble(packed, target, rims):
        tensor = add_rows(reshaped(packed, target), rims[0], rims[1])
        return add_cols(tensor, rims[2], rims[3])

    caches = (cache_a, cache_b, cache_c, cache_d)

    def cache_branch(level):
        return flat_pad(caches[level], size_input)

    cached = lax.switch(section, [partial(cache_branch, level) for level in range(4)])
    cache_rims = extend(cached, input_shapes)

    def store_branch(level, packed, rims):
        return flat_pad(assemble(packed, input_shapes[level], rims), size_extended)

    history = lax.switch(
        section, [partial(store_branch, level) for level in range(4)], cached, cache_rims
    )
    finished = jnp.zeros((frames, final_shape[0], final_shape[1] * final_shape[2]), jnp.bfloat16)
    stream = jnp.zeros((1, size_input), jnp.bfloat16)
    for moment in range(frames + segments - 1):
        if moment == 0:
            incoming = stream
        else:
            incoming = jax.tree.map(
                lambda part, own: part.astype(own.dtype),
                passed_along(shortened(stream), "segment", 1),
                stream,
            )
        frame_id = moment - section
        active = (frame_id >= 0) & (frame_id < frames)
        chosen = jnp.clip(frame_id, 0, frames - 1)
        picked = lax.dynamic_index_in_dim(latent, chosen, 0, keepdims=True)
        current = jnp.where(section == 0, flat_pad(picked, size_input), incoming)
        branch_id = jnp.where(active, section, 4)
        rims = extend(current, input_shapes)

        def conv_branch(level, current, history, rims):
            window = assemble(current, input_shapes[level], rims)
            earlier = reshaped(history, ext_shapes[level])
            hidden = activate(
                causal_conv(jnp.concatenate([earlier, window], axis=0), conv_kernels[level])
            )
            return (flat_pad(hidden[None], size_middle), flat_pad(window, size_extended))

        def spare_conv(current, history, rims):
            return (
                jnp.zeros((1, size_middle), jnp.bfloat16),
                jnp.zeros((1, size_extended), jnp.bfloat16),
            )

        hidden, window = lax.switch(
            branch_id,
            [partial(conv_branch, level) for level in range(4)] + [spare_conv],
            current,
            history,
            rims,
        )
        hidden_rims = extend(hidden, mid_shapes)

        def up_branch(level, hidden, hidden_rims):
            expanded = assemble(hidden, mid_shapes[level], hidden_rims)[0]
            return flat_pad(upsample_conv(expanded, up_kernels[level])[None], size_output)

        def spare_up(hidden, hidden_rims):
            return jnp.zeros((1, size_output), jnp.bfloat16)

        produced = lax.switch(
            branch_id,
            [partial(up_branch, level) for level in range(4)] + [spare_up],
            hidden,
            hidden_rims,
        )
        shifted = jnp.concatenate([history[1:], window], axis=0)
        history = jnp.where(active, shifted, history)
        stream = produced[:, :size_input]
        if moment >= final_segment:
            finished_id = moment - final_segment
            picture = produced[:, :final_count].reshape(
                1, final_shape[0], final_shape[1] * final_shape[2]
            )
            finished = finished.at[finished_id].set(picture[0])
    collected = lax.all_to_all(finished, "segment", split_axis=0, concat_axis=0, tiled=True)
    per_segment = frames // segments
    own_frame = collected[final_segment * per_segment : (final_segment + 1) * per_segment]
    return own_frame


AXES = ("segment", "ha", "wa")
VMEM = 60 * 1024 * 1024


def place(s, h, w):
    return (s * 4 + h) * 2 + w


def send(value, pairs):
    return lax.ppermute(value, AXES, [(place(*a), place(*b)) for a, b in pairs])


def square(segments, dh, dw):
    return [
        ((s, h, w), (s, h ^ dh, w ^ dw)) for s in segments for h in range(2) for w in range(2)
    ]


def kernel_call(body, out_shape, scratch, *args, flops=10**9):
    spec = pl.BlockSpec(memory_space=pltpu.VMEM)
    return pl.pallas_call(
        body,
        out_shape=out_shape,
        in_specs=[pl.BlockSpec(memory_space=pltpu.SMEM)] + [spec] * (len(args) - 1),
        out_specs=jax.tree.map(lambda _: spec, out_shape),
        scratch_shapes=scratch,
        compiler_params=pltpu.CompilerParams(vmem_limit_bytes=VMEM),
        cost_estimate=pl.CostEstimate(flops=flops, bytes_accessed=4 * 10**6, transcendentals=0),
    )(*args)


def dot(a, b):
    return jnp.dot(a, b, preferred_element_type=jnp.float32)


def index_of(shape):
    return lax.broadcasted_iota(jnp.int32, shape, 0)


def silu(v):
    return v / (1.0 + jnp.exp(-v))


def shifts(base, pitch, width):
    n = base.shape[0]
    left, right = pltpu.roll(base, 1, 0), pltpu.roll(base, n - 1, 0)
    if pitch == width:
        column = index_of(base.shape) % pitch
        left = jnp.where(column == 0, 0.0, left)
        right = jnp.where(column == width - 1, 0.0, right)
    return left, base, right


def upsample(p_ref, t_ref, pitch, width, lanes):
    n = p_ref.shape[0]
    blocks = lanes // 128
    column = index_of((n, 128)) % pitch
    for block in range(blocks):

        def tap(dy, dx):
            at = (dy * 3 + dx) * lanes + block * 128
            return p_ref[:, at : at + 128]

        for b in range(2):
            rows = []
            for dy in range(3):
                middle = tap(dy, 1)
                if b == 0:
                    far = pltpu.roll(tap(dy, 0), 1, 0)
                    if pitch == width:
                        far = jnp.where(column == 0, 0.0, far)
                    rows.append(far + middle + tap(dy, 2))
                else:
                    far = pltpu.roll(tap(dy, 2), n - 1, 0)
                    if pitch == width:
                        far = jnp.where(column == width - 1, 0.0, far)
                    rows.append(tap(dy, 0) + middle + far)
            t_ref[block, pl.ds(b, n, stride=2), :] = pltpu.roll(rows[0], pitch, 0) + rows[1] + rows[2]
            t_ref[blocks + block, pl.ds(b, n, stride=2), :] = (
                rows[0] + rows[1] + pltpu.roll(rows[2], n - pitch, 0)
            )


def conv0_body(ids, g_ref, k_ref, out_ref, gf, base, xx, acc, buf):
    s, h = ids[0], ids[1]

    @pl.when(s == 0)
    def _():
        gf[...] = g_ref[...].astype(jnp.float32)
        base[...] = jnp.zeros_like(base)
        for frame in range(6):
            for hh in range(4):
                for ww in range(2):
                    for r in range(2):
                        row = 8 + frame * 2 + r if frame < 2 else (frame - 2) * 2 + r
                        for c in range(2):
                            at = frame * 160 + (1 + 2 * hh + r) * 16 + 2 * ww + c
                            base[at : at + 1, :] = gf[hh * 2 + ww, row : row + 1, c * 384 : (c + 1) * 384]
        for dx, moved in enumerate(shifts(base[...], 16, 4)):
            xx[dx] = moved.astype(jnp.bfloat16)
        for part in range(4):

            @pl.when(h == part)
            def _():
                total = None
                at, end = part * 2592, part * 2592 + 2592
                while at < end:
                    tap, c0 = divmod(at, 384)
                    c1 = min(384, c0 + end - at)
                    dt, dy, dx = tap // 9, tap // 3 % 3, tap % 3
                    start = dt * 160 + dy * 16
                    k0 = at - part * 2592
                    term = dot(xx[dx, start : start + 608, c0:c1], k_ref[k0 : k0 + c1 - c0, :])
                    total = term if total is None else total + term
                    at += c1 - c0
                acc[...] = total

        for frame in range(4):
            for r in range(8):
                to, at = (frame * 8 + r) * 4, frame * 160 + r * 16
                buf[to : to + 4, :] = acc[at : at + 4, :]
        out_ref[...] = buf[...].astype(jnp.bfloat16)


def conv0(ids, gathered, k):
    f32, bf16 = jnp.float32, jnp.bfloat16
    return kernel_call(
        conv0_body,
        jax.ShapeDtypeStruct((128, 192), bf16),
        [
            pltpu.VMEM((8, 20, 768), f32),
            pltpu.VMEM((960, 384), f32),
            pltpu.VMEM((3, 960, 384), bf16),
            pltpu.VMEM((608, 192), f32),
            pltpu.VMEM((128, 192), f32),
        ],
        ids, gathered, k,
    )


def join_taps(h, pieces_own, pieces_z, cat_ref, taps_ref, width, lanes):
    for z in range(2):

        @pl.when(h == z)
        def _():
            for mine, pieces in ((z, pieces_own), (1 - z, pieces_z)):
                for number, piece in enumerate(pieces):
                    at = (mine + 2 * number) * 432
                    cat_ref[:, at : at + 432] = piece

    for tap in range(9):
        taps_ref[:, tap * lanes : tap * lanes + width] = cat_ref[:, tap * width : (tap + 1) * width]


def up0_body(ids, y_ref, own, nz, nx, nd, out_ref, cat, taps, hbuf, hs, p, t):
    s, h, w = ids[0], ids[1], ids[2]

    @pl.when((s == 0) & (h < 2))
    def _():
        halves = []
        for ww in range(2):
            total = y_ref[ww].astype(jnp.float32)
            for hh in range(1, 4):
                total = total + y_ref[hh * 2 + ww].astype(jnp.float32)
            halves.append(total)
        squares = sum(jnp.sum(half * half, axis=1, keepdims=True) for half in halves)
        inverse = lax.rsqrt(squares / 384.0 + EPSILON)
        active = [silu(half * inverse) for half in halves]
        hs[...] = jnp.zeros_like(hs)
        for k in range(2):
            hbuf[...] = jnp.where(w == k, active[0], active[1])
            for frame in range(4):
                for r in range(8):
                    to, at = frame * 72 + r * 8, (frame * 8 + r) * 4
                    hs[k, to : to + 4, :] = hbuf[at : at + 4, :]
        for k, (mine, other) in enumerate(((own, nz), (nx, nd))):
            join_taps(h, (mine[0:192], mine[192:384]), (other[0:192], other[192:384]), cat, taps, 192, 256)
            term = dot(hs[k].astype(jnp.bfloat16), taps[...])
            if k == 0:
                p[...] = term
            else:
                p[...] = p[...] + term
        upsample(p, t, 8, 4, 256)
        column = index_of((16, 192))
        out_ref[...] = jnp.zeros_like(out_ref)
        for z in range(2):

            @pl.when(h == z)
            def _():
                for frame in range(4):
                    for r in range(11):
                        y = r + 5 * z
                        at = frame * 144 + (y // 2) * 16
                        to = frame * 192 + (r + 1 - z) * 16
                        for lane, count in ((0, 128), (128, 64)):
                            row = t[y % 2 * 2 + lane // 128, at : at + 16, 0:count]
                            row = jnp.where(column[:, 0:count] < 8, row, 0.0)
                            out_ref[to : to + 16, lane : lane + count] = row.astype(jnp.bfloat16)


def up0(ids, partials, ups):
    f32, bf16 = jnp.float32, jnp.bfloat16
    return kernel_call(
        up0_body,
        jax.ShapeDtypeStruct((768, 192), bf16),
        [
            pltpu.VMEM((192, 1728), bf16),
            pltpu.VMEM((192, 2304), bf16),
            pltpu.VMEM((128, 192), f32),
            pltpu.VMEM((2, 288, 192), f32),
            pltpu.VMEM((288, 2304), f32),
            pltpu.VMEM((4, 576, 128), f32),
        ],
        ids, partials, *ups,
    )


def tap_rows(first, second, tap):
    parts, at = [], tap * 192
    while at < tap * 192 + 192:
        quarter, row = divmod(at, 1296)
        count = min(1296 - row, tap * 192 + 192 - at)
        source = (first, second)[quarter // 2]
        lane = quarter % 2 * 192
        parts.append(source[row : row + count, lane : lane + 192])
        at += count
    return parts[0] if len(parts) == 1 else jnp.concatenate(parts, axis=0)


def section1_body(ids, x_ref, cache, k_own, k_z, k_x, k_d, own, nz, nx, nd, out_ref, base, xx, acc, hs, cat, taps, p, t):
    s, h, w = ids[0], ids[1], ids[2]

    @pl.when((s == 1) & (h < 2))
    def _():
        @pl.when(w == 0)
        def _():
            base[0:384] = cache[...].astype(jnp.float32)
            base[384:768] = x_ref[0:384].astype(jnp.float32)

        @pl.when(w == 1)
        def _():
            base[...] = x_ref[...].astype(jnp.float32)

        for dx, moved in enumerate(shifts(base[...], 16, 8)):
            xx[dx] = moved.astype(jnp.bfloat16)
        for z in range(2):

            @pl.when(h == z)
            def _():
                for k, (mine, other) in enumerate(((k_own, k_z), (k_x, k_d))):
                    first, second = (mine, other) if z == 0 else (other, mine)
                    total = None
                    for tap in range(27):
                        dt, dy, dx = tap // 9, tap // 3 % 3, tap % 3
                        start = dt * 192 + dy * 16
                        term = dot(xx[dx, start : start + 352, :], tap_rows(first, second, tap))
                        total = term if total is None else total + term
                    acc[k] = total

        squares = sum(jnp.sum(acc[k] * acc[k], axis=1, keepdims=True) for k in range(2))
        inverse = lax.rsqrt(squares / 384.0 + EPSILON)
        index = index_of((352, 192))
        keep = (index % 192 < 160) & (index % 16 < 8)
        for k in range(2):
            hs[k, 0:352] = jnp.where(keep, silu(acc[k] * inverse), 0.0).astype(jnp.bfloat16)
            hs[k, 352:384] = jnp.zeros((32, 192), jnp.bfloat16)
        for k, (mine, other) in enumerate(((own, nz), (nx, nd))):
            join_taps(h, (mine[0:192], mine[192:384]), (other[0:192], other[192:384]), cat, taps, 192, 256)
            term = dot(hs[k], taps[...])
            if k == 0:
                p[...] = term
            else:
                p[...] = p[...] + term
        upsample(p, t, 16, 8, 256)
        out_ref[...] = jnp.zeros_like(out_ref)
        for z in range(2):

            @pl.when(h == z)
            def _():
                for frame in range(2):
                    for r in range(19):
                        y = r + z
                        at = frame * 384 + (y // 2) * 32
                        to = (r + 1 - z) * 16
                        for lane, count in ((0, 128), (128, 64)):
                            row = t[y % 2 * 2 + lane // 128, at : at + 16, 0:count].astype(jnp.bfloat16)
                            lane0 = frame * 192 + lane
                            out_ref[to : to + 16, lane0 : lane0 + count] = row


def section1(ids, frames, cache, kernels, ups):
    f32, bf16 = jnp.float32, jnp.bfloat16
    return kernel_call(
        section1_body,
        jax.ShapeDtypeStruct((320, 384), bf16),
        [
            pltpu.VMEM((768, 192), f32),
            pltpu.VMEM((3, 768, 192), bf16),
            pltpu.VMEM((2, 352, 192), f32),
            pltpu.VMEM((2, 384, 192), bf16),
            pltpu.VMEM((192, 1728), bf16),
            pltpu.VMEM((192, 2304), bf16),
            pltpu.VMEM((384, 2304), f32),
            pltpu.VMEM((4, 768, 128), f32),
        ],
        ids, frames, cache, *kernels, *ups,
    )


def pick(step, count, width, at):
    row = lax.broadcasted_iota(jnp.int32, (192, width), 0)
    column = lax.broadcasted_iota(jnp.int32, (192, width), 1)
    return ((row == (column - at) * step) & (column >= at) & (column < at + count)).astype(jnp.bfloat16)


def pick_rows(step, count, width, at):
    row = lax.broadcasted_iota(jnp.int32, (width, 192), 0)
    column = lax.broadcasted_iota(jnp.int32, (width, 192), 1)
    return ((column == (row - at) * step) & (row >= at) & (row < at + count)).astype(jnp.bfloat16)


def pick_body(ids, *refs):
    kernels, others = refs[0:4], refs[4:8]
    ups, others_up = refs[8:12], refs[12]
    k2, k3, u2, u3, cat, wide = refs[13:19]
    s, h = ids[0], ids[1]
    bf16 = jnp.bfloat16

    @pl.when((s >= 2) & (h < 2))
    def _():
        for z in range(2):
            for segment in range(2, 4):

                @pl.when((h == z) & (s == segment))
                def _():
                    for level in range(2, 4):
                        mine = level == segment
                        own, nz, nx, nd = kernels if mine else others
                        if mine:
                            pieces = [ref[0:192] for ref in ups]
                        else:
                            pieces = [others_up[192 * i : 192 * i + 192] for i in range(4)]
                        first = (own, nx) if z == 0 else (nz, nd)
                        second = (nz, nd) if z == 0 else (own, nx)
                        if level == 2:
                            left, right = pick(2, 96, 192, 0), pick(2, 96, 192, 96)
                            for quarter in range(4):
                                pair = (first, second)[quarter // 2]
                                lane = quarter % 2 * 192
                                rows = dot(pair[0][:, lane : lane + 192], left)
                                rows = rows + dot(pair[1][:, lane : lane + 192], right)
                                k2[quarter * 1296 : (quarter + 1) * 1296] = rows.astype(bf16)
                        else:
                            left, right = pick(4, 48, 96, 0), pick(4, 48, 96, 48)
                            for half in range(2):
                                lane = half * 192
                                rows = dot(first[0][:, lane : lane + 192], left)
                                rows = rows + dot(first[1][:, lane : lane + 192], right)
                                wide[half * 1296 : (half + 1) * 1296] = rows.astype(bf16)
                            k3[...] = jnp.zeros_like(k3)
                            for tap in range(27):
                                k3[tap * 128 : tap * 128 + 96] = wide[tap * 96 : (tap + 1) * 96]
                        step, count = (2, 96) if level == 2 else (4, 48)
                        near = (pieces[0], pieces[2]) if z == 0 else (pieces[1], pieces[3])
                        far = (pieces[1], pieces[3]) if z == 0 else (pieces[0], pieces[2])
                        top, bottom = pick_rows(step, count, 2 * count, 0), pick_rows(step, count, 2 * count, count)
                        for number, pair in enumerate((near, far)):
                            rows = dot(top, pair[0]) + dot(bottom, pair[1])
                            cat[0 : 2 * count, number * 432 : (number + 1) * 432] = rows.astype(bf16)
                        target = u2 if level == 2 else u3
                        for tap in range(9):
                            target[:, tap * 128 : tap * 128 + 96] = cat[0 : 2 * count, tap * 96 : (tap + 1) * 96]


def pick_kernels(ids, kernels, others, ups, others_up):
    bf16 = jnp.bfloat16
    return kernel_call(
        pick_body,
        (
            jax.ShapeDtypeStruct((5184, 192), bf16),
            jax.ShapeDtypeStruct((3456, 96), bf16),
            jax.ShapeDtypeStruct((192, 1152), bf16),
            jax.ShapeDtypeStruct((96, 1152), bf16),
        ),
        [pltpu.VMEM((192, 864), bf16), pltpu.VMEM((2592, 96), bf16)],
        ids, *kernels, *others, *ups, others_up,
    )


def sections23_body(ids, same2, same3, other2, other3, c_ref, d_ref, k2, k3, u2, u3, out_ref,
                    line, base, xx, hs, p, t, base3, xx3, hs3, p3, t3):
    s, h, w = ids[0], ids[1], ids[2]
    f32, bf16 = jnp.float32, jnp.bfloat16

    @pl.when((s >= 2) & (h < 2))
    def _():
        frame = (s - 2) * 2 + w
        line[0:640] = jnp.zeros((640, 192), bf16)
        line[640:1280] = c_ref[...]
        for segment, same, other in ((2, same2, other2), (3, same3, other3)):
            for width in range(2):

                @pl.when((s == segment) & (w == width))
                def _():
                    for number, pair in enumerate((same, other) if width == 0 else (other, same)):
                        for k in range(2):
                            at = 1280 + (2 * number + k) * 320
                            line[at : at + 320] = pair[:, k * 192 : (k + 1) * 192]

        base[...] = line[pl.ds(pl.multiple_of(frame * 320, 320), 1600), :].astype(f32)
        for dx, moved in enumerate(shifts(base[...], 16, 16)):
            xx[dx] = moved.astype(bf16)
        total = None
        for tap in range(27):
            dt, dy, dx = tap // 9, tap // 3 % 3, tap % 3
            start = dt * 320 + dy * 16
            term = dot(xx[dx, start : start + 928, :], k2[tap * 192 : (tap + 1) * 192, :])
            total = term if total is None else total + term
        inverse = lax.rsqrt(jnp.sum(total * total, axis=1, keepdims=True) / 192.0 + EPSILON)
        keep = index_of((928, 192)) % 320 < 288
        hs[0:928] = jnp.where(keep, silu(total * inverse), 0.0).astype(bf16)
        hs[928:960] = jnp.zeros((32, 192), bf16)
        p[...] = dot(hs[...], u2[...])
        upsample(p, t, 16, 16, 128)

        for z in range(2):

            @pl.when(h == z)
            def _():
                blank = 0 if z == 0 else 34
                for moment in range(3):
                    to = moment * 1120 + blank * 32
                    base3[to : to + 32] = jnp.zeros((32, 96), f32)
                    for r in range(34):
                        y = r + 2 * z
                        at = moment * 640 + (y // 2) * 32
                        to = moment * 1120 + (r + 1 - z) * 32
                        base3[to : to + 32] = t[y % 2, at : at + 32, 0:96].astype(bf16).astype(f32)

        @pl.when(frame == 0)
        def _():
            base3[0:2240] = d_ref[...].astype(f32)

        @pl.when(frame == 1)
        def _():
            base3[0:1120] = d_ref[1120:2240].astype(f32)

        xx3[...] = jnp.zeros_like(xx3)
        for dx, moved in enumerate(shifts(base3[...], 32, 32)):
            xx3[:, dx * 128 : dx * 128 + 96] = moved.astype(bf16)
        total = None
        for group in range(9):
            start = group // 3 * 1120 + group % 3 * 32
            term = dot(xx3[start : start + 1056, :], k3[group * 384 : (group + 1) * 384, :])
            total = term if total is None else total + term
        inverse = lax.rsqrt(jnp.sum(total * total, axis=1, keepdims=True) / 96.0 + EPSILON)
        hs3[0:1056] = silu(total * inverse).astype(bf16)
        hs3[1056:1120] = jnp.zeros((64, 96), bf16)
        p3[...] = dot(hs3[...], u3[...])
        upsample(p3, t3, 32, 32, 128)
        for z in range(2):

            @pl.when(h == z)
            def _():
                for r in range(64):
                    y = r + 2 * z
                    row = t3[y % 2, (y // 2) * 64 : (y // 2) * 64 + 64, 0:96].astype(bf16)
                    for half in range(2):
                        at = r % 32 * 32
                        out_ref[r // 32 * 2 + half, at : at + 32, :] = row[half * 32 : half * 32 + 32]


def sections23(ids, received, c, d, kernels):
    f32, bf16 = jnp.float32, jnp.bfloat16
    return kernel_call(
        sections23_body,
        jax.ShapeDtypeStruct((4, 1024, 96), bf16),
        [
            pltpu.VMEM((2560, 192), bf16),
            pltpu.VMEM((1600, 192), f32),
            pltpu.VMEM((3, 1600, 192), bf16),
            pltpu.VMEM((960, 192), bf16),
            pltpu.VMEM((960, 1152), f32),
            pltpu.VMEM((2, 1920, 128), f32),
            pltpu.VMEM((3360, 96), f32),
            pltpu.VMEM((3360, 384), bf16),
            pltpu.VMEM((1120, 96), bf16),
            pltpu.VMEM((1120, 1152), f32),
            pltpu.VMEM((2, 2240, 128), f32),
        ],
        ids, *received, c, d, *kernels,
    )


def window(rows, h, count, first):
    blank = jnp.zeros_like(rows[:, :1])
    top = jnp.concatenate([blank, rows[:, : count - 1]], axis=1)
    low = jnp.concatenate([rows[:, first : first + count - 1], blank], axis=1)
    return jnp.where(h == 0, top, low)


def relay(latent, cache_a, cache_b, cache_c, cache_d, conv_pack, up_pack):
    s, h, w = (lax.axis_index(axis) for axis in AXES)
    ids = jnp.stack([s, h, w]).astype(jnp.int32)
    k, u = conv_pack[0], up_pack[0]

    packed = jnp.concatenate([k[:1296], k[1296:]], axis=1)
    later = (1, 2, 3)
    k_z = send(packed, square(later, 1, 0))
    k_x = send(packed, square(later, 0, 1))
    u_far = send(u, [((s_, h_ + 2, w_), (s_, h_, w_)) for s_ in (0, 1) for h_ in range(2) for w_ in range(2)])
    ups = jnp.concatenate([u, u_far], axis=0)
    u_z = send(ups, square(range(4), 1, 0))
    u_x = send(ups, square(range(4), 0, 1))
    k_d0 = send(k_z[:640], square(later, 0, 1))
    k_d1 = send(k_x[640:], square(later, 1, 0))
    u_d = send(u_z, square(range(4), 0, 1))
    k_d = jnp.concatenate([k_d0, k_d1], axis=0)

    tiles = jnp.concatenate([latent.reshape(8, 768), cache_a.reshape(4, 768), cache_b.reshape(8, 768)], axis=0)
    gathered = lax.all_to_all(
        jnp.broadcast_to(tiles[None], (8, 20, 768)), ("ha", "wa"), split_axis=0, concat_axis=0, tiled=True
    )
    partial_sums = conv0(ids, gathered, k)
    partials = lax.all_to_all(
        jnp.broadcast_to(partial_sums[None], (8, 128, 192)), ("ha", "wa"), split_axis=0, concat_axis=0, tiled=True
    )
    risen = up0(ids, partials, (ups, u_z, u_x, u_d))
    given = send(risen, [((0, h_, w_), (1, h_, w_)) for h_ in range(2) for w_ in range(2)])

    b = gathered[:, 12:20].reshape(4, 2, 2, 4, 4, 192).transpose(2, 0, 3, 1, 4, 5).reshape(2, 16, 8, 192)
    b = jnp.pad(window(b, h, 12, 5), ((0, 0), (0, 0), (0, 8), (0, 0))).reshape(384, 192)
    out1 = section1(ids, given, b, (packed, k_z, k_x, k_d), (ups, u_z, u_x, u_d))
    received = [
        send(out1, [((1, h_, w_), (s_, h_, w_ ^ dw)) for h_ in range(2) for w_ in range(2)])
        for dw in range(2)
        for s_ in (2, 3)
    ]

    cores = [((s_, h_, w_), (s_ ^ 1, h_, w_)) for s_ in (2, 3) for h_ in range(2) for w_ in range(2)]
    others = [send(piece, cores) for piece in (packed, k_z, k_x, k_d)]
    others_up = send(jnp.concatenate([piece[:192] for piece in (ups, u_z, u_x, u_d)], axis=0), cores)
    kernels = pick_kernels(ids, (packed, k_z, k_x, k_d), others, (ups, u_z, u_x, u_d), others_up)
    own = jnp.concatenate([cache_c.reshape(16, 1536), cache_d.reshape(32, 1536)], axis=0)
    beside = send(own, [((s_, h_, w_), (s_, h_, w_ ^ 1)) for s_ in (2, 3) for h_ in range(4) for w_ in range(2)])
    both = jnp.where(w == 0, jnp.concatenate([own, beside], axis=1), jnp.concatenate([beside, own], axis=1))
    bands = [both] + [
        send(both, [((s_, h_ + n, w_), (s_, h_, w_)) for s_ in (2, 3) for h_ in range(2) for w_ in range(2)])
        for n in (1, 2)
    ]
    c = jnp.concatenate([band[:16].reshape(2, 8, 16, 192) for band in bands], axis=1)
    d = jnp.concatenate([band[16:].reshape(2, 16, 32, 96) for band in bands], axis=1)
    c = window(c, h, 20, 5).reshape(640, 192)
    d = window(d, h, 35, 14).reshape(2240, 96)
    blocks = sections23(ids, received, c, d, kernels)

    arrived = [
        send(
            blocks[2 * n + half],
            [((2 + c_, z, x), (2 * c_ + x, 2 * z + n, half)) for c_ in range(2) for z in range(2) for x in range(2)],
        )
        for n in range(2)
        for half in range(2)
    ]
    upper = jnp.where(w == 0, arrived[0], arrived[1])
    lower = jnp.where(w == 0, arrived[2], arrived[3])
    return jnp.where(h % 2 == 0, upper, lower).reshape(1, 32, 3072)


def solution(mesh):
    in_specs = (
        P(None, "ha", "wa"),
        P(None, "ha", "wa"),
        P(None, "ha", "wa"),
        P(None, "ha", "wa"),
        P(None, "ha", "wa"),
        P("segment", "ha", "wa"),
        P("segment", "wa", "ha"),
    )
    out_specs = P("segment", "ha", "wa")
    sizes = tuple(mesh.shape[axis] for axis in AXES)
    program = relay if sizes == (4, 4, 2) else per_device
    return jax.shard_map(
        program, mesh=mesh, in_specs=in_specs, out_specs=out_specs, check_vma=False
    )
```

```python
from functools import partial

import jax
import jax.numpy as jnp
from jax import lax
from jax.experimental import pallas as pl
from jax.experimental.pallas import tpu as pltpu
from jax.sharding import PartitionSpec as P

WIDE = 384
MID = 192
NARROW = 96


EPSILON = 1e-06


def shortened(array):

    def short(part):
        return part.astype(jnp.bfloat16) if part.dtype == jnp.float32 else part

    return jax.tree.map(short, array)


def passed_along(value, axis, steps):
    count = lax.axis_size(axis)
    initial, last = (max(0, -steps), min(count, count - steps))
    return lax.ppermute(value, axis, [(source, source + steps) for source in range(initial, last)])


def layer_table():
    return ((WIDE, WIDE, MID), (MID, WIDE, MID), (MID, MID, NARROW), (NARROW, NARROW, NARROW))


def round_up(amount):
    return -(-amount // 128) * 128


def volume(target):
    amount = 1
    for extent in target:
        amount = amount * extent
    return amount


def flat_pad(tensor, length):
    leading = tensor.shape[0]
    packed = tensor.reshape(leading, -1)
    return jnp.pad(packed, ((0, 0), (0, length - packed.shape[1])))


def reshaped(packed, target):
    return packed[:, : volume(target)].reshape((packed.shape[0],) + tuple(target))


def add_rows(tensor, from_above, from_below):
    leading, height, width, channels = tensor.shape
    upper = reshaped(from_above, (1, width, channels))
    lower = reshaped(from_below, (1, width, channels))
    return jnp.concatenate([upper, tensor, lower], axis=1)


def add_cols(tensor, from_left, from_right):
    leading, height, width, channels = tensor.shape
    before = reshaped(from_left, (height, 1, channels))
    after = reshaped(from_right, (height, 1, channels))
    return jnp.concatenate([before, tensor, after], axis=2)


def trade_rows(upper_rim, bottom):
    return (
        jax.tree.map(
            lambda part, own: part.astype(own.dtype),
            passed_along(shortened(bottom), "ha", 1),
            bottom,
        ),
        jax.tree.map(
            lambda part, own: part.astype(own.dtype),
            passed_along(shortened(upper_rim), "ha", -1),
            upper_rim,
        ),
    )


def trade_cols(left_rim, right_rim):
    return (
        jax.tree.map(
            lambda part, own: part.astype(own.dtype),
            passed_along(shortened(right_rim), "wa", 1),
            right_rim,
        ),
        jax.tree.map(
            lambda part, own: part.astype(own.dtype),
            passed_along(shortened(left_rim), "wa", -1),
            left_rim,
        ),
    )


def causal_conv(stacked, kernel):
    result = lax.conv_general_dilated(
        stacked[None],
        kernel,
        (1, 1, 1),
        "VALID",
        dimension_numbers=("NDHWC", "DHWIO", "NDHWC"),
        preferred_element_type=jnp.float32,
    )
    return result[0, 0]


def activate(conv_sum):
    inverse = lax.rsqrt(jnp.mean(conv_sum * conv_sum, axis=-1, keepdims=True) + EPSILON)
    return jax.nn.silu(conv_sum * inverse).astype(jnp.bfloat16)


def upsample_conv(hidden_ext, kernel):
    expanded = jnp.repeat(jnp.repeat(hidden_ext, 2, axis=0), 2, axis=1)[1:-1, 1:-1]
    result = lax.conv_general_dilated(
        expanded[None],
        kernel,
        (1, 1),
        "VALID",
        dimension_numbers=("NHWC", "HWIO", "NHWC"),
        preferred_element_type=jnp.float32,
    )
    return result[0].astype(jnp.bfloat16)


def per_device(latent, cache_a, cache_b, cache_c, cache_d, conv_pack, up_pack):
    frames = latent.shape[0]
    tile_rows = latent.shape[1]
    tile_cols = latent.shape[2] // WIDE
    layers = layer_table()
    section = lax.axis_index("segment")
    segments = lax.axis_size("segment")
    final_segment = segments - 1
    input_shapes = [
        (tile_rows << level, tile_cols << level, layers[level][0]) for level in range(4)
    ]
    mid_shapes = [(tile_rows << level, tile_cols << level, layers[level][1]) for level in range(4)]
    out_shapes = [
        (tile_rows << level + 1, tile_cols << level + 1, layers[level][2]) for level in range(4)
    ]
    ext_shapes = [(target[0] + 2, target[1] + 2, target[2]) for target in input_shapes]
    all_shapes = input_shapes + mid_shapes
    row_length = round_up(max((target[1] * target[2] for target in all_shapes)))
    column_length = round_up(max(((target[0] + 2) * target[2] for target in all_shapes)))
    size_input = round_up(max((volume(target) for target in input_shapes)))
    size_middle = round_up(max((volume(target) for target in mid_shapes)))
    size_extended = round_up(max((volume(target) for target in ext_shapes)))
    size_output = round_up(max((volume(target) for target in out_shapes)))
    final_shape = out_shapes[3]
    final_count = volume(final_shape)
    conv_rows, up_rows = (
        lax.all_gather(conv_pack, "ha", axis=1, tiled=True),
        lax.all_gather(up_pack, "ha", axis=2, tiled=True),
    )
    conv_all, up_all = (
        lax.all_gather(conv_rows, "wa", axis=2, tiled=True),
        lax.all_gather(up_rows, "wa", axis=1, tiled=True),
    )

    def conv_kernel(level):
        width_in, width_mid, width_out = layers[level]
        columns = conv_all[0, : 27 * width_in, :: WIDE // width_mid]
        return columns.reshape(3, 3, 3, width_in, columns.shape[1])

    def up_kernel(level):
        width_in, width_mid, width_out = layers[level]
        rows_used = up_all[0, :: WIDE // width_mid, : 9 * width_out]
        return rows_used.reshape(width_mid, 3, 3, width_out).transpose(1, 2, 0, 3)

    conv_kernels = [conv_kernel(level) for level in range(4)]
    up_kernels = [up_kernel(level) for level in range(4)]

    def row_rims(packed, shapes):

        def rows_branch(level, packed):
            tensor = reshaped(packed, shapes[level])
            return (flat_pad(tensor[:, :1], row_length), flat_pad(tensor[:, -1:], row_length))

        upper_rim, bottom = lax.switch(
            section, [partial(rows_branch, level) for level in range(4)], packed
        )
        return trade_rows(upper_rim, bottom)

    def extend(packed, shapes):
        from_above, from_below = row_rims(packed, shapes)

        def cols_branch(level, packed, from_above, from_below):
            tensor = add_rows(reshaped(packed, shapes[level]), from_above, from_below)
            return (
                flat_pad(tensor[:, :, :1], column_length),
                flat_pad(tensor[:, :, -1:], column_length),
            )

        left_rim, right_rim = lax.switch(
            section,
            [partial(cols_branch, level) for level in range(4)],
            packed,
            from_above,
            from_below,
        )
        from_left, from_right = trade_cols(left_rim, right_rim)
        return (from_above, from_below, from_left, from_right)

    def assemble(packed, target, rims):
        tensor = add_rows(reshaped(packed, target), rims[0], rims[1])
        return add_cols(tensor, rims[2], rims[3])

    caches = (cache_a, cache_b, cache_c, cache_d)

    def cache_branch(level):
        return flat_pad(caches[level], size_input)

    cached = lax.switch(section, [partial(cache_branch, level) for level in range(4)])
    cache_rims = extend(cached, input_shapes)

    def store_branch(level, packed, rims):
        return flat_pad(assemble(packed, input_shapes[level], rims), size_extended)

    history = lax.switch(
        section, [partial(store_branch, level) for level in range(4)], cached, cache_rims
    )
    finished = jnp.zeros((frames, final_shape[0], final_shape[1] * final_shape[2]), jnp.bfloat16)
    stream = jnp.zeros((1, size_input), jnp.bfloat16)
    for moment in range(frames + segments - 1):
        if moment == 0:
            incoming = stream
        else:
            incoming = jax.tree.map(
                lambda part, own: part.astype(own.dtype),
                passed_along(shortened(stream), "segment", 1),
                stream,
            )
        frame_id = moment - section
        active = (frame_id >= 0) & (frame_id < frames)
        chosen = jnp.clip(frame_id, 0, frames - 1)
        picked = lax.dynamic_index_in_dim(latent, chosen, 0, keepdims=True)
        current = jnp.where(section == 0, flat_pad(picked, size_input), incoming)
        branch_id = jnp.where(active, section, 4)
        rims = extend(current, input_shapes)

        def conv_branch(level, current, history, rims):
            window = assemble(current, input_shapes[level], rims)
            earlier = reshaped(history, ext_shapes[level])
            hidden = activate(
                causal_conv(jnp.concatenate([earlier, window], axis=0), conv_kernels[level])
            )
            return (flat_pad(hidden[None], size_middle), flat_pad(window, size_extended))

        def spare_conv(current, history, rims):
            return (
                jnp.zeros((1, size_middle), jnp.bfloat16),
                jnp.zeros((1, size_extended), jnp.bfloat16),
            )

        hidden, window = lax.switch(
            branch_id,
            [partial(conv_branch, level) for level in range(4)] + [spare_conv],
            current,
            history,
            rims,
        )
        hidden_rims = extend(hidden, mid_shapes)

        def up_branch(level, hidden, hidden_rims):
            expanded = assemble(hidden, mid_shapes[level], hidden_rims)[0]
            return flat_pad(upsample_conv(expanded, up_kernels[level])[None], size_output)

        def spare_up(hidden, hidden_rims):
            return jnp.zeros((1, size_output), jnp.bfloat16)

        produced = lax.switch(
            branch_id,
            [partial(up_branch, level) for level in range(4)] + [spare_up],
            hidden,
            hidden_rims,
        )
        shifted = jnp.concatenate([history[1:], window], axis=0)
        history = jnp.where(active, shifted, history)
        stream = produced[:, :size_input]
        if moment >= final_segment:
            finished_id = moment - final_segment
            picture = produced[:, :final_count].reshape(
                1, final_shape[0], final_shape[1] * final_shape[2]
            )
            finished = finished.at[finished_id].set(picture[0])
    collected = lax.all_to_all(finished, "segment", split_axis=0, concat_axis=0, tiled=True)
    per_segment = frames // segments
    own_frame = collected[final_segment * per_segment : (final_segment + 1) * per_segment]
    return own_frame


AXES = ("segment", "ha", "wa")
VMEM = 60 * 1024 * 1024


def place(s, h, w):
    return (s * 4 + h) * 2 + w


def send(value, pairs):
    return lax.ppermute(value, AXES, [(place(*a), place(*b)) for a, b in pairs])


def square(segments, dh, dw):
    return [
        ((s, h, w), (s, h ^ dh, w ^ dw)) for s in segments for h in range(2) for w in range(2)
    ]


def kernel_call(body, out_shape, scratch, *args, copies=0, flops=10**9):
    return pl.pallas_call(
        body,
        out_shape=out_shape,
        in_specs=[pl.BlockSpec(memory_space=pltpu.SMEM)] + [pl.BlockSpec(memory_space=pl.ANY)] * (len(args) - 1),
        out_specs=jax.tree.map(lambda _: pl.BlockSpec(memory_space=pl.ANY), out_shape),
        scratch_shapes=scratch + [pltpu.SemaphoreType.DMA((copies,))],
        compiler_params=pltpu.CompilerParams(vmem_limit_bytes=VMEM),
        cost_estimate=pl.CostEstimate(flops=flops, bytes_accessed=4 * 10**6, transcendentals=0),
    )(*args)


def start_all(pairs, sems, first=0):
    copies = [pltpu.make_async_copy(a, b, sems.at[first + n]) for n, (a, b) in enumerate(pairs)]
    for copy in copies:
        copy.start()
    return copies


def wait_all(copies):
    for copy in copies:
        copy.wait()


def dot(a, b):
    return jnp.dot(a, b, preferred_element_type=jnp.float32)


def index_of(shape):
    return lax.broadcasted_iota(jnp.int32, shape, 0)


def silu(v):
    return v / (1.0 + jnp.exp(-v))


def shifts(base, pitch, width):
    n = base.shape[0]
    left, right = pltpu.roll(base, 1, 0), pltpu.roll(base, n - 1, 0)
    if pitch == width:
        column = index_of(base.shape) % pitch
        left = jnp.where(column == 0, 0.0, left)
        right = jnp.where(column == width - 1, 0.0, right)
    return left, base, right


def upsample(p_ref, t_ref, pitch, width, lanes):
    n = p_ref.shape[0]
    blocks = lanes // 128
    column = index_of((n, 128)) % pitch
    for block in range(blocks):

        def tap(dy, dx):
            at = (dy * 3 + dx) * lanes + block * 128
            return p_ref[:, at : at + 128]

        for b in range(2):
            rows = []
            for dy in range(3):
                middle = tap(dy, 1)
                if b == 0:
                    far = pltpu.roll(tap(dy, 0), 1, 0)
                    if pitch == width:
                        far = jnp.where(column == 0, 0.0, far)
                    rows.append(far + middle + tap(dy, 2))
                else:
                    far = pltpu.roll(tap(dy, 2), n - 1, 0)
                    if pitch == width:
                        far = jnp.where(column == width - 1, 0.0, far)
                    rows.append(tap(dy, 0) + middle + far)
            t_ref[block, pl.ds(b, n, stride=2), :] = pltpu.roll(rows[0], pitch, 0) + rows[1] + rows[2]
            t_ref[blocks + block, pl.ds(b, n, stride=2), :] = (
                rows[0] + rows[1] + pltpu.roll(rows[2], n - pitch, 0)
            )


def conv0_body(ids, g_any, k_any, out_any, g_ref, k_ref, gf, base, xx, acc, buf, out_ref, sems):
    s, h = ids[0], ids[1]

    @pl.when(s == 0)
    def _():
        coming = start_all([(g_any, g_ref), (k_any, k_ref)], sems)
        base[...] = jnp.zeros_like(base)
        coming[0].wait()
        gf[...] = g_ref[...].astype(jnp.float32)
        for frame in range(6):
            for hh in range(4):
                for ww in range(2):
                    for r in range(2):
                        row = 8 + frame * 2 + r if frame < 2 else (frame - 2) * 2 + r
                        for c in range(2):
                            at = frame * 160 + (1 + 2 * hh + r) * 16 + 2 * ww + c
                            base[at : at + 1, :] = gf[hh * 2 + ww, row : row + 1, c * 384 : (c + 1) * 384]
        for dx, moved in enumerate(shifts(base[...], 16, 4)):
            xx[dx] = moved.astype(jnp.bfloat16)
        coming[1].wait()
        for part in range(4):

            @pl.when(h == part)
            def _():
                total = None
                at, end = part * 2592, part * 2592 + 2592
                while at < end:
                    tap, c0 = divmod(at, 384)
                    c1 = min(384, c0 + end - at)
                    dt, dy, dx = tap // 9, tap // 3 % 3, tap % 3
                    start = dt * 160 + dy * 16
                    k0 = at - part * 2592
                    term = dot(xx[dx, start : start + 608, c0:c1], k_ref[k0 : k0 + c1 - c0, :])
                    total = term if total is None else total + term
                    at += c1 - c0
                acc[...] = total

        for frame in range(4):
            for r in range(8):
                to, at = (frame * 8 + r) * 4, frame * 160 + r * 16
                buf[to : to + 4, :] = acc[at : at + 4, :]
        out_ref[...] = buf[...].astype(jnp.bfloat16)
        wait_all(start_all([(out_ref, out_any)], sems))


def conv0(ids, gathered, k):
    f32, bf16 = jnp.float32, jnp.bfloat16
    return kernel_call(
        conv0_body,
        jax.ShapeDtypeStruct((128, 192), bf16),
        [
            pltpu.VMEM((8, 20, 768), bf16),
            pltpu.VMEM((2592, 192), bf16),
            pltpu.VMEM((8, 20, 768), f32),
            pltpu.VMEM((960, 384), f32),
            pltpu.VMEM((3, 960, 384), bf16),
            pltpu.VMEM((608, 192), f32),
            pltpu.VMEM((128, 192), f32),
            pltpu.VMEM((128, 192), bf16),
        ],
        ids, gathered, k,
        copies=2,
    )


def join_taps(h, pieces_own, pieces_z, cat_ref, taps_ref, width, lanes):
    for z in range(2):

        @pl.when(h == z)
        def _():
            for mine, pieces in ((z, pieces_own), (1 - z, pieces_z)):
                for number, piece in enumerate(pieces):
                    at = (mine + 2 * number) * 432
                    cat_ref[:, at : at + 432] = piece

    for tap in range(9):
        taps_ref[:, tap * lanes : tap * lanes + width] = cat_ref[:, tap * width : (tap + 1) * width]


def up0_body(ids, y_any, own_any, z_any, x_any, d_any, out_any, y_ref, own, nz, nx, nd, cat, taps, hbuf, hs, p, t,
             out_ref, sems):
    s, h, w = ids[0], ids[1], ids[2]

    @pl.when((s == 0) & (h < 2))
    def _():
        coming = start_all([(y_any, y_ref), (own_any, own), (z_any, nz), (x_any, nx), (d_any, nd)], sems)
        coming[0].wait()
        halves = []
        for ww in range(2):
            total = y_ref[ww].astype(jnp.float32)
            for hh in range(1, 4):
                total = total + y_ref[hh * 2 + ww].astype(jnp.float32)
            halves.append(total)
        squares = sum(jnp.sum(half * half, axis=1, keepdims=True) for half in halves)
        inverse = lax.rsqrt(squares / 384.0 + EPSILON)
        active = [silu(half * inverse) for half in halves]
        hs[...] = jnp.zeros_like(hs)
        for k in range(2):
            hbuf[...] = jnp.where(w == k, active[0], active[1])
            for frame in range(4):
                for r in range(8):
                    to, at = frame * 72 + r * 8, (frame * 8 + r) * 4
                    hs[k, to : to + 4, :] = hbuf[at : at + 4, :]
        wait_all(coming[1:])
        for k, (mine, other) in enumerate(((own, nz), (nx, nd))):
            join_taps(h, (mine[0:192], mine[192:384]), (other[0:192], other[192:384]), cat, taps, 192, 256)
            term = dot(hs[k].astype(jnp.bfloat16), taps[...])
            if k == 0:
                p[...] = term
            else:
                p[...] = p[...] + term
        upsample(p, t, 8, 4, 256)
        column = index_of((16, 192))
        out_ref[...] = jnp.zeros_like(out_ref)
        for z in range(2):

            @pl.when(h == z)
            def _():
                for frame in range(4):
                    for r in range(11):
                        y = r + 5 * z
                        at = frame * 144 + (y // 2) * 16
                        to = frame * 192 + (r + 1 - z) * 16
                        for lane, count in ((0, 128), (128, 64)):
                            row = t[y % 2 * 2 + lane // 128, at : at + 16, 0:count]
                            row = jnp.where(column[:, 0:count] < 8, row, 0.0)
                            out_ref[to : to + 16, lane : lane + count] = row.astype(jnp.bfloat16)

        wait_all(start_all([(out_ref, out_any)], sems))


def up0(ids, partials, ups):
    f32, bf16 = jnp.float32, jnp.bfloat16
    return kernel_call(
        up0_body,
        jax.ShapeDtypeStruct((768, 192), bf16),
        [
            pltpu.VMEM((8, 128, 192), bf16),
            *[pltpu.VMEM((384, 432), bf16)] * 4,
            pltpu.VMEM((192, 1728), bf16),
            pltpu.VMEM((192, 2304), bf16),
            pltpu.VMEM((128, 192), f32),
            pltpu.VMEM((2, 288, 192), f32),
            pltpu.VMEM((288, 2304), f32),
            pltpu.VMEM((4, 576, 128), f32),
            pltpu.VMEM((768, 192), bf16),
        ],
        ids, partials, *ups,
        copies=5,
    )


def group_rows(first, second, group):
    parts, at, end = [], group * 576, group * 576 + 576
    while at < end:
        quarter, row = divmod(at, 1296)
        count = min(1296 - row, end - at)
        source = (first, second)[quarter // 2]
        lane = quarter % 2 * 192
        parts.append(source[row : row + count, lane : lane + 192])
        at += count
    return parts[0] if len(parts) == 1 else jnp.concatenate(parts, axis=0)


def section1_body(ids, x_any, g_any, *refs):
    kernels_any, ups_any, out_any = refs[0:8], refs[8:12], refs[12]
    x_ref, g_ref = refs[13:15]
    k_own, k_z, k_x, k_d, own, nz, nx, nd = refs[15:23]
    gf, full, base, xx, acc, hs, cat, taps, p, t, out_ref, sems = refs[23:]
    s, h, w = ids[0], ids[1], ids[2]

    @pl.when((s == 1) & (h < 2))
    def _():
        coming = start_all([(x_any, x_ref), (g_any, g_ref)], sems)
        pairs = []
        for number, piece in enumerate((k_own, k_z, k_x, k_d)):
            pairs.append((kernels_any[2 * number], piece.at[0:640]))
            pairs.append((kernels_any[2 * number + 1], piece.at[640:1296]))
        arriving = start_all(pairs, sems, 2)
        rising = start_all(list(zip(ups_any, (own, nz, nx, nd))), sems, 10)
        wait_all(coming)

        @pl.when(w == 0)
        def _():
            gf[...] = g_ref[...].astype(jnp.float32)
            full[...] = jnp.zeros_like(full)
            for frame in range(2):
                for hh in range(4):
                    for ww in range(2):
                        for r in range(4):
                            for c in range(4):
                                row = 12 + frame * 4 + r
                                at = frame * 288 + (1 + hh * 4 + r) * 16 + ww * 4 + c
                                full[at : at + 1, :] = gf[hh * 2 + ww, row : row + 1, c * 192 : (c + 1) * 192]
            for frame in range(2):
                start = pl.multiple_of(frame * 288 + h * 96, 32)
                base[frame * 192 : (frame + 1) * 192] = full[pl.ds(start, 192), :]
            base[384:768] = x_ref[0:384].astype(jnp.float32)

        @pl.when(w == 1)
        def _():
            base[...] = x_ref[...].astype(jnp.float32)

        for dx, moved in enumerate(shifts(base[...], 16, 8)):
            xx[:, dx * 192 : (dx + 1) * 192] = moved.astype(jnp.bfloat16)
        wait_all(arriving)
        for z in range(2):

            @pl.when(h == z)
            def _():
                for k, (mine, other) in enumerate(((k_own, k_z), (k_x, k_d))):
                    first, second = (mine, other) if z == 0 else (other, mine)
                    total = None
                    for group in range(9):
                        start = group // 3 * 192 + group % 3 * 16
                        term = dot(xx[start : start + 352, :], group_rows(first, second, group))
                        total = term if total is None else total + term
                    acc[k] = total

        squares = sum(jnp.sum(acc[k] * acc[k], axis=1, keepdims=True) for k in range(2))
        inverse = lax.rsqrt(squares / 384.0 + EPSILON)
        index = index_of((352, 192))
        keep = (index % 192 < 160) & (index % 16 < 8)
        for k in range(2):
            hs[k, 0:352] = jnp.where(keep, silu(acc[k] * inverse), 0.0).astype(jnp.bfloat16)
            hs[k, 352:384] = jnp.zeros((32, 192), jnp.bfloat16)
        wait_all(rising)
        for k, (mine, other) in enumerate(((own, nz), (nx, nd))):
            join_taps(h, (mine[0:192], mine[192:384]), (other[0:192], other[192:384]), cat, taps, 192, 256)
            term = dot(hs[k], taps[...])
            if k == 0:
                p[...] = term
            else:
                p[...] = p[...] + term
        upsample(p, t, 16, 8, 256)
        out_ref[...] = jnp.zeros_like(out_ref)
        for z in range(2):

            @pl.when(h == z)
            def _():
                for frame in range(2):
                    for r in range(19):
                        y = r + z
                        at = frame * 384 + (y // 2) * 32
                        to = (r + 1 - z) * 16
                        for lane, count in ((0, 128), (128, 64)):
                            row = t[y % 2 * 2 + lane // 128, at : at + 16, 0:count].astype(jnp.bfloat16)
                            lane0 = frame * 192 + lane
                            out_ref[to : to + 16, lane0 : lane0 + count] = row

        wait_all(start_all([(out_ref, out_any)], sems))


def section1(ids, frames, gathered, kernels, ups):
    f32, bf16 = jnp.float32, jnp.bfloat16
    return kernel_call(
        section1_body,
        jax.ShapeDtypeStruct((320, 384), bf16),
        [
            pltpu.VMEM((768, 192), bf16),
            pltpu.VMEM((8, 20, 768), bf16),
            *[pltpu.VMEM((1296, 384), bf16)] * 4,
            *[pltpu.VMEM((384, 432), bf16)] * 4,
            pltpu.VMEM((8, 20, 768), f32),
            pltpu.VMEM((576, 192), f32),
            pltpu.VMEM((768, 192), f32),
            pltpu.VMEM((768, 576), bf16),
            pltpu.VMEM((2, 352, 192), f32),
            pltpu.VMEM((2, 384, 192), bf16),
            pltpu.VMEM((192, 1728), bf16),
            pltpu.VMEM((192, 2304), bf16),
            pltpu.VMEM((384, 2304), f32),
            pltpu.VMEM((4, 768, 128), f32),
            pltpu.VMEM((320, 384), bf16),
        ],
        ids, frames, gathered, *kernels, *ups,
        copies=14,
    )


def pick(across, step, count, at):
    source = lax.broadcasted_iota(jnp.int32, (192, 192), 1 if across else 0)
    target = lax.broadcasted_iota(jnp.int32, (192, 192), 0 if across else 1) - at
    return ((source == target * step) & (target >= 0) & (target < count)).astype(jnp.bfloat16)


def pack_body(ids, k_any, u_any, upper_any, lower_any, up_any, k, u, upper, lower, up, sems):
    s, w = ids[0], ids[2]
    bf16 = jnp.bfloat16
    coming = start_all([(k_any, k), (u_any, u)], sems)
    wait_all(coming)

    @pl.when(s < 2)
    def _():
        for half in range(2):
            lane = half * 192
            upper[:, lane : lane + 192] = k[half * 1296 : half * 1296 + 640]
            lower[:, lane : lane + 192] = k[half * 1296 + 640 : half * 1296 + 1296]
        up[...] = u[...]

    for level, step, count in ((2, 2, 96), (3, 4, 48)):

        @pl.when(s == level)
        def _():
            columns = pick(False, step, count, w * count)
            for half in range(2):
                lane = half * 192
                upper[:, lane : lane + 192] = dot(k[half * 1296 : half * 1296 + 640], columns).astype(bf16)
                lower[:, lane : lane + 192] = dot(k[half * 1296 + 640 : half * 1296 + 1296], columns).astype(bf16)
            up[...] = dot(pick(True, step, count, w * count), u[...]).astype(bf16)

    wait_all(start_all([(upper, upper_any), (lower, lower_any), (up, up_any)], sems))


def pack(ids, k, u):
    bf16 = jnp.bfloat16
    shapes = ((640, 384), (656, 384), (192, 432))
    return kernel_call(
        pack_body,
        tuple(jax.ShapeDtypeStruct(shape, bf16) for shape in shapes),
        [pltpu.VMEM((2592, 192), bf16), pltpu.VMEM((192, 432), bf16)] + [pltpu.VMEM(shape, bf16) for shape in shapes],
        ids, k, u,
        copies=3,
    )


def merge_body(ids, *refs):
    kernels_any, ups_any, (k2_any, k3_any, up_any) = refs[0:8], refs[8:12], refs[12:15]
    pieces, ups = refs[15:19], refs[19:23]
    k2, wide, k3, cat, up, sems = refs[23:]
    s, h = ids[0], ids[1]

    @pl.when((s >= 2) & (h < 2))
    def _():
        pairs = []
        for number, piece in enumerate(pieces):
            pairs.append((kernels_any[2 * number], piece.at[0:640]))
            pairs.append((kernels_any[2 * number + 1], piece.at[640:1296]))
        coming = start_all(pairs, sems)
        rising = start_all([(a.at[0:192], b) for a, b in zip(ups_any, ups)], sems, 8)
        wait_all(rising)
        for z in range(2):

            @pl.when(h == z)
            def _():
                cat[:, z * 432 : z * 432 + 432] = ups[0][...] + ups[2][...]
                cat[:, (1 - z) * 432 : (1 - z) * 432 + 432] = ups[1][...] + ups[3][...]

        up[...] = jnp.zeros_like(up)
        for tap in range(9):
            up[:, tap * 128 : tap * 128 + 96] = cat[:, tap * 96 : (tap + 1) * 96]
        wait_all(coming)
        own, nz, nx, nd = pieces

        @pl.when(s == 2)
        def _():
            for z in range(2):

                @pl.when(h == z)
                def _():
                    for part, (a, b) in enumerate(((own, nx), (nz, nd))):
                        part = part ^ z
                        for half in range(2):
                            at, lane = (part * 2 + half) * 1296, half * 192
                            k2[at : at + 1296, :] = a[:, lane : lane + 192] + b[:, lane : lane + 192]

            wait_all(start_all([(k2, k2_any)], sems))

        @pl.when(s == 3)
        def _():
            for z in range(2):

                @pl.when(h == z)
                def _():
                    a, b = ((own, nx), (nz, nd))[z]
                    for half in range(2):
                        lane = half * 192
                        rows = a[:, lane : lane + 128] + b[:, lane : lane + 128]
                        wide[half * 1296 : half * 1296 + 1296, :] = rows

            k3[...] = jnp.zeros_like(k3)
            for tap in range(27):
                k3[tap * 128 : tap * 128 + 96, :] = wide[tap * 96 : tap * 96 + 96, :]
            wait_all(start_all([(k3, k3_any)], sems))

        wait_all(start_all([(up, up_any)], sems))


def merge(ids, kernels, ups):
    bf16 = jnp.bfloat16
    shapes = ((5184, 192), (3456, 128), (192, 1152))
    return kernel_call(
        merge_body,
        tuple(jax.ShapeDtypeStruct(shape, bf16) for shape in shapes),
        [
            *[pltpu.VMEM((1296, 384), bf16)] * 4,
            *[pltpu.VMEM((192, 432), bf16)] * 4,
            pltpu.VMEM((5184, 192), bf16),
            pltpu.VMEM((2592, 128), bf16),
            pltpu.VMEM((3456, 128), bf16),
            pltpu.VMEM((192, 864), bf16),
            pltpu.VMEM((192, 1152), bf16),
        ],
        ids, *kernels, *ups,
        copies=12,
    )


def caches_body(ids, b0_any, b1_any, b2_any, c_any, d_any, bands, wide, c_full, d_full, c, d, sems):
    s, h, w = ids[0], ids[1], ids[2]
    f32, bf16 = jnp.float32, jnp.bfloat16

    @pl.when((s >= 2) & (h < 2))
    def _():
        wait_all(start_all([(a, bands.at[n]) for n, a in enumerate((b0_any, b1_any, b2_any))], sems))
        c_full[...] = jnp.zeros_like(c_full)
        d_full[...] = jnp.zeros_like(d_full)
        for band in range(3):
            wide[...] = bands[band].astype(f32)
            for side in range(2):
                swapped = (w + side) % 2
                for frame in range(2):
                    row = side * 48 + frame * 8
                    for column in range(8):
                        at = (frame * 26 + 1 + band * 8) * 16 + swapped * 8 + column
                        lane = column * 192
                        c_full[0, pl.ds(at, 8, stride=16), :] = wide[row : row + 8, lane : lane + 128]
                        tail = jnp.concatenate([wide[row : row + 8, lane + 128 : lane + 192]] * 2, axis=1)
                        c_full[1, pl.ds(at, 8, stride=16), :] = tail
                    row = side * 48 + 16 + frame * 16
                    for column in range(16):
                        at = (frame * 50 + 1 + band * 16) * 32 + swapped * 16 + column
                        lane = column * 96
                        part = wide[row : row + 16, lane : lane + 96]
                        part = jnp.concatenate([part, part[:, 0:32]], axis=1)
                        d_full[pl.ds(at, 16, stride=32), :] = part
        for frame in range(2):
            at = pl.multiple_of((frame * 26 + h * 6) * 16, 32)
            c[frame * 320 : frame * 320 + 320, 0:128] = c_full[0, pl.ds(at, 320), :].astype(bf16)
            c[frame * 320 : frame * 320 + 320, 128:192] = c_full[1, pl.ds(at, 320), 0:64].astype(bf16)
            at = pl.multiple_of((frame * 50 + h * 15) * 32, 32)
            d[frame * 1120 : frame * 1120 + 1120, :] = d_full[pl.ds(at, 1120), 0:96].astype(bf16)
        wait_all(start_all([(c, c_any), (d, d_any)], sems))


def caches(ids, bands):
    f32, bf16 = jnp.float32, jnp.bfloat16
    return kernel_call(
        caches_body,
        (jax.ShapeDtypeStruct((640, 192), bf16), jax.ShapeDtypeStruct((2240, 96), bf16)),
        [
            pltpu.VMEM((3, 96, 1536), bf16),
            pltpu.VMEM((96, 1536), f32),
            pltpu.VMEM((2, 832, 128), f32),
            pltpu.VMEM((3200, 128), f32),
            pltpu.VMEM((640, 192), bf16),
            pltpu.VMEM((2240, 96), bf16),
        ],
        ids, *bands,
        copies=3,
    )


def sections23_body(ids, same2, same3, other2, other3, c_any, d_any, k2_own, k2_sent, k3_own, k3_sent, u_own, u_sent,
                    out0, out1, out2, out3, pairs, d_ref, k2, k3, u2, u3, line, base, xx, hs, p, t, base3, xx3, hs3, p3, t3, out_ref,
                    sems):
    s, h, w = ids[0], ids[1], ids[2]
    f32, bf16 = jnp.float32, jnp.bfloat16

    @pl.when((s >= 2) & (h < 2))
    def _():
        frame = (s - 2) * 2 + w
        line[0:640] = jnp.zeros((640, 192), bf16)
        for segment, same, other in ((2, same2, other2), (3, same3, other3)):

            @pl.when(s == segment)
            def _():
                held2, held3 = (k2_own, k3_sent) if segment == 2 else (k2_sent, k3_own)
                up2, up3 = (u_own, u_sent) if segment == 2 else (u_sent, u_own)
                start_all(
                    [
                        (same, pairs.at[w]),
                        (other, pairs.at[1 - w]),
                        (c_any, line.at[640:1280]),
                        (held2, k2),
                        (up2, u2),
                        (d_any, d_ref),
                        (held3, k3),
                        (up3.at[0:96], u3),
                    ],
                    sems,
                )

        coming = [
            pltpu.make_async_copy(a, b, sems.at[n])
            for n, (a, b) in enumerate(
                [
                    (same2, pairs.at[0]),
                    (other2, pairs.at[1]),
                    (c_any, line.at[640:1280]),
                    (k2_own, k2),
                    (u_own, u2),
                    (d_any, d_ref),
                    (k3_own, k3),
                    (u_own.at[0:96], u3),
                ]
            )
        ]
        wait_all(coming[0:3])
        for number in range(2):
            for k in range(2):
                at = 1280 + (2 * number + k) * 320
                line[at : at + 320] = pairs[number, :, k * 192 : (k + 1) * 192]

        base[...] = line[pl.ds(pl.multiple_of(frame * 320, 320), 1600), :].astype(f32)
        for dx, moved in enumerate(shifts(base[...], 16, 16)):
            xx[:, dx * 192 : (dx + 1) * 192] = moved.astype(bf16)
        coming[3].wait()
        total = None
        for group in range(9):
            start = group // 3 * 320 + group % 3 * 16
            term = dot(xx[start : start + 928, :], k2[group * 576 : (group + 1) * 576, :])
            total = term if total is None else total + term
        inverse = lax.rsqrt(jnp.sum(total * total, axis=1, keepdims=True) / 192.0 + EPSILON)
        keep = index_of((928, 192)) % 320 < 288
        hs[0:928] = jnp.where(keep, silu(total * inverse), 0.0).astype(bf16)
        hs[928:960] = jnp.zeros((32, 192), bf16)
        coming[4].wait()
        p[...] = dot(hs[...], u2[...])
        upsample(p, t, 16, 16, 128)

        for z in range(2):

            @pl.when(h == z)
            def _():
                blank = 0 if z == 0 else 34
                for moment in range(3):
                    to = moment * 1120 + blank * 32
                    base3[to : to + 32] = jnp.zeros((32, 96), f32)
                    for r in range(34):
                        y = r + 2 * z
                        at = moment * 640 + (y // 2) * 32
                        to = moment * 1120 + (r + 1 - z) * 32
                        base3[to : to + 32] = t[y % 2, at : at + 32, 0:96].astype(bf16).astype(f32)

        wait_all(coming[5:8])

        @pl.when(frame == 0)
        def _():
            base3[0:2240] = d_ref[...].astype(f32)

        @pl.when(frame == 1)
        def _():
            base3[0:1120] = d_ref[1120:2240].astype(f32)

        xx3[...] = jnp.zeros_like(xx3)
        for dx, moved in enumerate(shifts(base3[...], 32, 32)):
            xx3[:, dx * 128 : dx * 128 + 96] = moved.astype(bf16)
        total = None
        for group in range(9):
            start = group // 3 * 1120 + group % 3 * 32
            term = dot(xx3[start : start + 1056, :], k3[group * 384 : (group + 1) * 384, 0:96])
            total = term if total is None else total + term
        inverse = lax.rsqrt(jnp.sum(total * total, axis=1, keepdims=True) / 96.0 + EPSILON)
        hs3[0:1056] = silu(total * inverse).astype(bf16)
        hs3[1056:1120] = jnp.zeros((64, 96), bf16)
        p3[...] = dot(hs3[...], u3[...])
        upsample(p3, t3, 32, 32, 128)
        for z in range(2):

            @pl.when(h == z)
            def _():
                for r in range(64):
                    y = r + 2 * z
                    row = t3[y % 2, (y // 2) * 64 : (y // 2) * 64 + 64, 0:96].astype(bf16)
                    for half in range(2):
                        at = r % 32 * 32
                        out_ref[r // 32 * 2 + half, at : at + 32, :] = row[half * 32 : half * 32 + 32]

        wait_all(start_all([(out_ref.at[n], target) for n, target in enumerate((out0, out1, out2, out3))], sems))


def sections23(ids, received, c, d, kernels):
    f32, bf16 = jnp.float32, jnp.bfloat16
    return kernel_call(
        sections23_body,
        tuple([jax.ShapeDtypeStruct((1024, 96), bf16)] * 4),
        [
            pltpu.VMEM((2, 320, 384), bf16),
            pltpu.VMEM((2240, 96), bf16),
            pltpu.VMEM((5184, 192), bf16),
            pltpu.VMEM((3456, 128), bf16),
            pltpu.VMEM((192, 1152), bf16),
            pltpu.VMEM((96, 1152), bf16),
            pltpu.VMEM((2560, 192), bf16),
            pltpu.VMEM((1600, 192), f32),
            pltpu.VMEM((1600, 576), bf16),
            pltpu.VMEM((960, 192), bf16),
            pltpu.VMEM((960, 1152), f32),
            pltpu.VMEM((2, 1920, 128), f32),
            pltpu.VMEM((3360, 96), f32),
            pltpu.VMEM((3360, 384), bf16),
            pltpu.VMEM((1120, 96), bf16),
            pltpu.VMEM((1120, 1152), f32),
            pltpu.VMEM((2, 2240, 128), f32),
            pltpu.VMEM((4, 1024, 96), bf16),
        ],
        ids, *received, c, d, *kernels,
        copies=8,
    )


def relay(latent, cache_a, cache_b, cache_c, cache_d, conv_pack, up_pack):
    s, h, w = (lax.axis_index(axis) for axis in AXES)
    ids = jnp.stack([s, h, w]).astype(jnp.int32)
    k = conv_pack[0]

    upper, lower, u = pack(ids, k, up_pack[0])
    later = (1, 2, 3)
    u_far = send(u, [((s_, h_ + 2, w_), (s_, h_, w_)) for s_ in (0, 1) for h_ in range(2) for w_ in range(2)])
    upper_z, lower_z = (send(part, square(later, 1, 0)) for part in (upper, lower))
    upper_x, lower_x = (send(part, square(later, 0, 1)) for part in (upper, lower))
    ups = jnp.concatenate([u, u_far], axis=0)
    u_z = send(ups, square(range(4), 1, 0))
    u_x = send(ups, square(range(4), 0, 1))
    u_d = send(u_z, square(range(4), 0, 1))
    upper_d = send(upper_z, square(later, 0, 1))
    lower_d = send(lower_x, square(later, 1, 0))
    kernels = (upper, lower, upper_z, lower_z, upper_x, lower_x, upper_d, lower_d)
    risers = (ups, u_z, u_x, u_d)

    tiles = jnp.concatenate([latent.reshape(8, 768), cache_a.reshape(4, 768), cache_b.reshape(8, 768)], axis=0)
    gathered = lax.all_to_all(
        jnp.broadcast_to(tiles[None], (8, 20, 768)), ("ha", "wa"), split_axis=0, concat_axis=0, tiled=True
    )
    partial_sums = conv0(ids, gathered, k)
    partials = lax.all_to_all(
        jnp.broadcast_to(partial_sums[None], (8, 128, 192)), ("ha", "wa"), split_axis=0, concat_axis=0, tiled=True
    )
    risen = up0(ids, partials, risers)
    given = send(risen, [((0, h_, w_), (1, h_, w_)) for h_ in range(2) for w_ in range(2)])

    out1 = section1(ids, given, gathered, kernels, risers)
    received = [
        send(out1, [((1, h_, w_), (s_, h_, w_ ^ dw)) for h_ in range(2) for w_ in range(2)])
        for dw in range(2)
        for s_ in (2, 3)
    ]

    k2, k3, u23 = merge(ids, kernels, risers)
    pairs = [((s_, h_, w_), (s_ ^ 1, h_, w_)) for s_ in (2, 3) for h_ in range(2) for w_ in range(2)]
    k2_sent = send(k2, [pair for pair in pairs if pair[0][0] == 2])
    k3_sent = send(k3, [pair for pair in pairs if pair[0][0] == 3])
    u_sent = send(u23, pairs)
    own = jnp.concatenate([cache_c.reshape(16, 1536), cache_d.reshape(32, 1536)], axis=0)
    beside = send(own, [((s_, h_, w_), (s_, h_, w_ ^ 1)) for s_ in (2, 3) for h_ in range(4) for w_ in range(2)])
    both = jnp.concatenate([own, beside], axis=0)
    bands = [both] + [
        send(both, [((s_, h_ + n, w_), (s_, h_, w_)) for s_ in (2, 3) for h_ in range(2) for w_ in range(2)])
        for n in (1, 2)
    ]
    c, d = caches(ids, bands)
    blocks = sections23(ids, received, c, d, (k2, k2_sent, k3, k3_sent, u23, u_sent))

    arrived = [
        send(
            blocks[2 * n + half],
            [((2 + c_, z, x), (2 * c_ + x, 2 * z + n, half)) for c_ in range(2) for z in range(2) for x in range(2)],
        )
        for n in range(2)
        for half in range(2)
    ]
    lower_half = jnp.where(w == 0, arrived[2], arrived[3])
    upper_half = jnp.where(w == 0, arrived[0], arrived[1])
    return jnp.where(h % 2 == 0, upper_half, lower_half).reshape(1, 32, 3072)


def solution(mesh):
    in_specs = (
        P(None, "ha", "wa"),
        P(None, "ha", "wa"),
        P(None, "ha", "wa"),
        P(None, "ha", "wa"),
        P(None, "ha", "wa"),
        P("segment", "ha", "wa"),
        P("segment", "wa", "ha"),
    )
    out_specs = P("segment", "ha", "wa")
    sizes = tuple(mesh.shape[axis] for axis in AXES)
    program = relay if sizes == (4, 4, 2) else per_device
    return jax.shard_map(
        program, mesh=mesh, in_specs=in_specs, out_specs=out_specs, check_vma=False
    )
```

```python
from functools import partial

import jax
import jax.numpy as jnp
from jax import lax
from jax.experimental import pallas as pl
from jax.experimental.pallas import tpu as pltpu
from jax.sharding import PartitionSpec as P

WIDE = 384
MID = 192
NARROW = 96


EPSILON = 1e-06


def shortened(array):

    def short(part):
        return part.astype(jnp.bfloat16) if part.dtype == jnp.float32 else part

    return jax.tree.map(short, array)


def passed_along(value, axis, steps):
    count = lax.axis_size(axis)
    initial, last = (max(0, -steps), min(count, count - steps))
    return lax.ppermute(value, axis, [(source, source + steps) for source in range(initial, last)])


def layer_table():
    return ((WIDE, WIDE, MID), (MID, WIDE, MID), (MID, MID, NARROW), (NARROW, NARROW, NARROW))


def round_up(amount):
    return -(-amount // 128) * 128


def volume(target):
    amount = 1
    for extent in target:
        amount = amount * extent
    return amount


def flat_pad(tensor, length):
    leading = tensor.shape[0]
    packed = tensor.reshape(leading, -1)
    return jnp.pad(packed, ((0, 0), (0, length - packed.shape[1])))


def reshaped(packed, target):
    return packed[:, : volume(target)].reshape((packed.shape[0],) + tuple(target))


def add_rows(tensor, from_above, from_below):
    leading, height, width, channels = tensor.shape
    upper = reshaped(from_above, (1, width, channels))
    lower = reshaped(from_below, (1, width, channels))
    return jnp.concatenate([upper, tensor, lower], axis=1)


def add_cols(tensor, from_left, from_right):
    leading, height, width, channels = tensor.shape
    before = reshaped(from_left, (height, 1, channels))
    after = reshaped(from_right, (height, 1, channels))
    return jnp.concatenate([before, tensor, after], axis=2)


def trade_rows(upper_rim, bottom):
    return (
        jax.tree.map(
            lambda part, own: part.astype(own.dtype),
            passed_along(shortened(bottom), "ha", 1),
            bottom,
        ),
        jax.tree.map(
            lambda part, own: part.astype(own.dtype),
            passed_along(shortened(upper_rim), "ha", -1),
            upper_rim,
        ),
    )


def trade_cols(left_rim, right_rim):
    return (
        jax.tree.map(
            lambda part, own: part.astype(own.dtype),
            passed_along(shortened(right_rim), "wa", 1),
            right_rim,
        ),
        jax.tree.map(
            lambda part, own: part.astype(own.dtype),
            passed_along(shortened(left_rim), "wa", -1),
            left_rim,
        ),
    )


def causal_conv(stacked, kernel):
    result = lax.conv_general_dilated(
        stacked[None],
        kernel,
        (1, 1, 1),
        "VALID",
        dimension_numbers=("NDHWC", "DHWIO", "NDHWC"),
        preferred_element_type=jnp.float32,
    )
    return result[0, 0]


def activate(conv_sum):
    inverse = lax.rsqrt(jnp.mean(conv_sum * conv_sum, axis=-1, keepdims=True) + EPSILON)
    return jax.nn.silu(conv_sum * inverse).astype(jnp.bfloat16)


def upsample_conv(hidden_ext, kernel):
    expanded = jnp.repeat(jnp.repeat(hidden_ext, 2, axis=0), 2, axis=1)[1:-1, 1:-1]
    result = lax.conv_general_dilated(
        expanded[None],
        kernel,
        (1, 1),
        "VALID",
        dimension_numbers=("NHWC", "HWIO", "NHWC"),
        preferred_element_type=jnp.float32,
    )
    return result[0].astype(jnp.bfloat16)


def per_device(latent, cache_a, cache_b, cache_c, cache_d, conv_pack, up_pack):
    frames = latent.shape[0]
    tile_rows = latent.shape[1]
    tile_cols = latent.shape[2] // WIDE
    layers = layer_table()
    section = lax.axis_index("segment")
    segments = lax.axis_size("segment")
    final_segment = segments - 1
    input_shapes = [
        (tile_rows << level, tile_cols << level, layers[level][0]) for level in range(4)
    ]
    mid_shapes = [(tile_rows << level, tile_cols << level, layers[level][1]) for level in range(4)]
    out_shapes = [
        (tile_rows << level + 1, tile_cols << level + 1, layers[level][2]) for level in range(4)
    ]
    ext_shapes = [(target[0] + 2, target[1] + 2, target[2]) for target in input_shapes]
    all_shapes = input_shapes + mid_shapes
    row_length = round_up(max((target[1] * target[2] for target in all_shapes)))
    column_length = round_up(max(((target[0] + 2) * target[2] for target in all_shapes)))
    size_input = round_up(max((volume(target) for target in input_shapes)))
    size_middle = round_up(max((volume(target) for target in mid_shapes)))
    size_extended = round_up(max((volume(target) for target in ext_shapes)))
    size_output = round_up(max((volume(target) for target in out_shapes)))
    final_shape = out_shapes[3]
    final_count = volume(final_shape)
    conv_rows, up_rows = (
        lax.all_gather(conv_pack, "ha", axis=1, tiled=True),
        lax.all_gather(up_pack, "ha", axis=2, tiled=True),
    )
    conv_all, up_all = (
        lax.all_gather(conv_rows, "wa", axis=2, tiled=True),
        lax.all_gather(up_rows, "wa", axis=1, tiled=True),
    )

    def conv_kernel(level):
        width_in, width_mid, width_out = layers[level]
        columns = conv_all[0, : 27 * width_in, :: WIDE // width_mid]
        return columns.reshape(3, 3, 3, width_in, columns.shape[1])

    def up_kernel(level):
        width_in, width_mid, width_out = layers[level]
        rows_used = up_all[0, :: WIDE // width_mid, : 9 * width_out]
        return rows_used.reshape(width_mid, 3, 3, width_out).transpose(1, 2, 0, 3)

    conv_kernels = [conv_kernel(level) for level in range(4)]
    up_kernels = [up_kernel(level) for level in range(4)]

    def row_rims(packed, shapes):

        def rows_branch(level, packed):
            tensor = reshaped(packed, shapes[level])
            return (flat_pad(tensor[:, :1], row_length), flat_pad(tensor[:, -1:], row_length))

        upper_rim, bottom = lax.switch(
            section, [partial(rows_branch, level) for level in range(4)], packed
        )
        return trade_rows(upper_rim, bottom)

    def extend(packed, shapes):
        from_above, from_below = row_rims(packed, shapes)

        def cols_branch(level, packed, from_above, from_below):
            tensor = add_rows(reshaped(packed, shapes[level]), from_above, from_below)
            return (
                flat_pad(tensor[:, :, :1], column_length),
                flat_pad(tensor[:, :, -1:], column_length),
            )

        left_rim, right_rim = lax.switch(
            section,
            [partial(cols_branch, level) for level in range(4)],
            packed,
            from_above,
            from_below,
        )
        from_left, from_right = trade_cols(left_rim, right_rim)
        return (from_above, from_below, from_left, from_right)

    def assemble(packed, target, rims):
        tensor = add_rows(reshaped(packed, target), rims[0], rims[1])
        return add_cols(tensor, rims[2], rims[3])

    caches = (cache_a, cache_b, cache_c, cache_d)

    def cache_branch(level):
        return flat_pad(caches[level], size_input)

    cached = lax.switch(section, [partial(cache_branch, level) for level in range(4)])
    cache_rims = extend(cached, input_shapes)

    def store_branch(level, packed, rims):
        return flat_pad(assemble(packed, input_shapes[level], rims), size_extended)

    history = lax.switch(
        section, [partial(store_branch, level) for level in range(4)], cached, cache_rims
    )
    finished = jnp.zeros((frames, final_shape[0], final_shape[1] * final_shape[2]), jnp.bfloat16)
    stream = jnp.zeros((1, size_input), jnp.bfloat16)
    for moment in range(frames + segments - 1):
        if moment == 0:
            incoming = stream
        else:
            incoming = jax.tree.map(
                lambda part, own: part.astype(own.dtype),
                passed_along(shortened(stream), "segment", 1),
                stream,
            )
        frame_id = moment - section
        active = (frame_id >= 0) & (frame_id < frames)
        chosen = jnp.clip(frame_id, 0, frames - 1)
        picked = lax.dynamic_index_in_dim(latent, chosen, 0, keepdims=True)
        current = jnp.where(section == 0, flat_pad(picked, size_input), incoming)
        branch_id = jnp.where(active, section, 4)
        rims = extend(current, input_shapes)

        def conv_branch(level, current, history, rims):
            window = assemble(current, input_shapes[level], rims)
            earlier = reshaped(history, ext_shapes[level])
            hidden = activate(
                causal_conv(jnp.concatenate([earlier, window], axis=0), conv_kernels[level])
            )
            return (flat_pad(hidden[None], size_middle), flat_pad(window, size_extended))

        def spare_conv(current, history, rims):
            return (
                jnp.zeros((1, size_middle), jnp.bfloat16),
                jnp.zeros((1, size_extended), jnp.bfloat16),
            )

        hidden, window = lax.switch(
            branch_id,
            [partial(conv_branch, level) for level in range(4)] + [spare_conv],
            current,
            history,
            rims,
        )
        hidden_rims = extend(hidden, mid_shapes)

        def up_branch(level, hidden, hidden_rims):
            expanded = assemble(hidden, mid_shapes[level], hidden_rims)[0]
            return flat_pad(upsample_conv(expanded, up_kernels[level])[None], size_output)

        def spare_up(hidden, hidden_rims):
            return jnp.zeros((1, size_output), jnp.bfloat16)

        produced = lax.switch(
            branch_id,
            [partial(up_branch, level) for level in range(4)] + [spare_up],
            hidden,
            hidden_rims,
        )
        shifted = jnp.concatenate([history[1:], window], axis=0)
        history = jnp.where(active, shifted, history)
        stream = produced[:, :size_input]
        if moment >= final_segment:
            finished_id = moment - final_segment
            picture = produced[:, :final_count].reshape(
                1, final_shape[0], final_shape[1] * final_shape[2]
            )
            finished = finished.at[finished_id].set(picture[0])
    collected = lax.all_to_all(finished, "segment", split_axis=0, concat_axis=0, tiled=True)
    per_segment = frames // segments
    own_frame = collected[final_segment * per_segment : (final_segment + 1) * per_segment]
    return own_frame


AXES = ("segment", "ha", "wa")
VMEM = 60 * 1024 * 1024


def place(s, h, w):
    return (s * 4 + h) * 2 + w


def send(value, pairs):
    return lax.ppermute(value, AXES, [(place(*a), place(*b)) for a, b in pairs])


def square(segments, dh, dw):
    return [
        ((s, h, w), (s, h ^ dh, w ^ dw)) for s in segments for h in range(2) for w in range(2)
    ]


def kernel_call(body, out_shape, scratch, *args, copies=0, flops=10**9):
    return pl.pallas_call(
        body,
        out_shape=out_shape,
        in_specs=[pl.BlockSpec(memory_space=pl.ANY)] * len(args),
        out_specs=jax.tree.map(lambda _: pl.BlockSpec(memory_space=pl.ANY), out_shape),
        scratch_shapes=scratch + [pltpu.SemaphoreType.DMA((copies,))],
        compiler_params=pltpu.CompilerParams(vmem_limit_bytes=VMEM),
        cost_estimate=pl.CostEstimate(flops=flops, bytes_accessed=4 * 10**6, transcendentals=0),
    )(*args)


def start_all(pairs, sems, first=0):
    copies = [pltpu.make_async_copy(a, b, sems.at[first + n]) for n, (a, b) in enumerate(pairs)]
    for copy in copies:
        copy.start()
    return copies


def wait_all(copies):
    for copy in copies:
        copy.wait()


def dot(a, b):
    return jnp.dot(a, b, preferred_element_type=jnp.float32)


def dot_t(a, b):
    return lax.dot_general(a, b, (((1,), (1,)), ((), ())), preferred_element_type=jnp.float32)


def index_of(shape):
    return lax.broadcasted_iota(jnp.int32, shape, 0)


def silu(v):
    return v / (1.0 + jnp.exp(-v))


def shifts(base, pitch, width):
    n = base.shape[0]
    left, right = pltpu.roll(base, 1, 0), pltpu.roll(base, n - 1, 0)
    if pitch == width:
        column = index_of(base.shape) % pitch
        left = jnp.where(column == 0, 0.0, left)
        right = jnp.where(column == width - 1, 0.0, right)
    return left, base, right


def upsample(p_ref, t_ref, pitch, width, lanes):
    n = p_ref.shape[0]
    blocks = lanes // 128
    column = index_of((n, 128)) % pitch
    for block in range(blocks):

        def tap(dy, dx):
            at = (dy * 3 + dx) * lanes + block * 128
            return p_ref[:, at : at + 128]

        for b in range(2):
            rows = []
            for dy in range(3):
                middle = tap(dy, 1)
                if b == 0:
                    far = pltpu.roll(tap(dy, 0), 1, 0)
                    if pitch == width:
                        far = jnp.where(column == 0, 0.0, far)
                    rows.append(far + middle + tap(dy, 2))
                else:
                    far = pltpu.roll(tap(dy, 2), n - 1, 0)
                    if pitch == width:
                        far = jnp.where(column == width - 1, 0.0, far)
                    rows.append(tap(dy, 0) + middle + far)
            t_ref[block, pl.ds(b, n, stride=2), :] = pltpu.roll(rows[0], pitch, 0) + rows[1] + rows[2]
            t_ref[blocks + block, pl.ds(b, n, stride=2), :] = (
                rows[0] + rows[1] + pltpu.roll(rows[2], n - pitch, 0)
            )


def conv0_body(g_any, k_any, out_any, g_ref, k_ref, gf, base, xx, acc, buf, out_ref, sems):
    s, h = lax.axis_index("segment"), lax.axis_index("ha")

    @pl.when(s == 0)
    def _():
        coming = start_all([(g_any, g_ref), (k_any, k_ref)], sems)
        base[...] = jnp.zeros_like(base)
        coming[0].wait()
        gf[...] = g_ref[...].astype(jnp.float32)
        for frame in range(6):
            for hh in range(4):
                for ww in range(2):
                    for r in range(2):
                        row = 8 + frame * 2 + r if frame < 2 else (frame - 2) * 2 + r
                        for c in range(2):
                            at = frame * 160 + (1 + 2 * hh + r) * 16 + 2 * ww + c
                            base[at : at + 1, :] = gf[hh * 2 + ww, row : row + 1, c * 384 : (c + 1) * 384]
        for dx, moved in enumerate(shifts(base[...], 16, 4)):
            xx[dx] = moved.astype(jnp.bfloat16)
        coming[1].wait()
        for part in range(4):

            @pl.when(h == part)
            def _():
                total = None
                at, end = part * 2592, part * 2592 + 2592
                while at < end:
                    tap, c0 = divmod(at, 384)
                    c1 = min(384, c0 + end - at)
                    dt, dy, dx = tap // 9, tap // 3 % 3, tap % 3
                    start = dt * 160 + dy * 16
                    k0 = at - part * 2592
                    term = dot_t(xx[dx, start : start + 608, c0:c1], k_ref[:, k0 : k0 + c1 - c0])
                    total = term if total is None else total + term
                    at += c1 - c0
                acc[...] = total

        for frame in range(4):
            for r in range(8):
                to, at = (frame * 8 + r) * 4, frame * 160 + r * 16
                buf[to : to + 4, :] = acc[at : at + 4, :]
        out_ref[0:128, :] = buf[:, 0:128].astype(jnp.bfloat16)
        tail = jnp.concatenate([buf[0:64, 128:192], buf[64:128, 128:192]], axis=1)
        out_ref[128:192, :] = tail.astype(jnp.bfloat16)
        wait_all(start_all([(out_ref, out_any.at[n]) for n in range(8)], sems))


def conv0(gathered, k):
    f32, bf16 = jnp.float32, jnp.bfloat16
    return kernel_call(
        conv0_body,
        jax.ShapeDtypeStruct((8, 192, 128), bf16),
        [
            pltpu.VMEM((8, 20, 768), bf16),
            pltpu.VMEM((192, 2592), bf16),
            pltpu.VMEM((8, 20, 768), f32),
            pltpu.VMEM((960, 384), f32),
            pltpu.VMEM((3, 960, 384), bf16),
            pltpu.VMEM((608, 192), f32),
            pltpu.VMEM((128, 192), f32),
            pltpu.VMEM((192, 128), bf16),
        ],
        gathered, k,
        copies=8,
    )


def join_taps(h, pieces_own, pieces_z, cat_ref, taps_ref, width, lanes):
    for z in range(2):

        @pl.when(h == z)
        def _():
            for mine, pieces in ((z, pieces_own), (1 - z, pieces_z)):
                for number, piece in enumerate(pieces):
                    at = (mine + 2 * number) * 432
                    cat_ref[:, at : at + 432] = piece

    for tap in range(9):
        taps_ref[:, tap * lanes : tap * lanes + width] = cat_ref[:, tap * width : (tap + 1) * width]


def up0_body(y_any, own_any, z_any, x_any, d_any, out_any, y_ref, own, nz, nx, nd, cat, taps, hbuf, hs, p, t,
             out_ref, sems):
    s, h, w = (lax.axis_index(axis) for axis in AXES)

    @pl.when((s == 0) & (h < 2))
    def _():
        coming = start_all([(y_any, y_ref), (own_any, own), (z_any, nz), (x_any, nx), (d_any, nd)], sems)
        coming[0].wait()
        halves = []
        for ww in range(2):
            total = y_ref[ww].astype(jnp.float32)
            for hh in range(1, 4):
                total = total + y_ref[hh * 2 + ww].astype(jnp.float32)
            tail = jnp.concatenate([total[128:192, 0:64], total[128:192, 64:128]], axis=0)
            halves.append(jnp.concatenate([total[0:128], tail], axis=1))
        squares = sum(jnp.sum(half * half, axis=1, keepdims=True) for half in halves)
        inverse = lax.rsqrt(squares / 384.0 + EPSILON)
        active = [silu(half * inverse) for half in halves]
        hs[...] = jnp.zeros_like(hs)
        for k in range(2):
            hbuf[...] = jnp.where(w == k, active[0], active[1])
            for frame in range(4):
                for r in range(8):
                    to, at = frame * 72 + r * 8, (frame * 8 + r) * 4
                    hs[k, to : to + 4, :] = hbuf[at : at + 4, :]
        wait_all(coming[1:])
        for k, (mine, other) in enumerate(((own, nz), (nx, nd))):
            join_taps(h, (mine[0:192], mine[192:384]), (other[0:192], other[192:384]), cat, taps, 192, 256)
            term = dot(hs[k].astype(jnp.bfloat16), taps[...])
            if k == 0:
                p[...] = term
            else:
                p[...] = p[...] + term
        upsample(p, t, 8, 4, 256)
        column = index_of((16, 192))
        out_ref[...] = jnp.zeros_like(out_ref)
        for z in range(2):

            @pl.when(h == z)
            def _():
                for frame in range(4):
                    for r in range(11):
                        y = r + 5 * z
                        at = frame * 144 + (y // 2) * 16
                        to = frame * 192 + (r + 1 - z) * 16
                        for lane, count in ((0, 128), (128, 64)):
                            row = t[y % 2 * 2 + lane // 128, at : at + 16, 0:count]
                            row = jnp.where(column[:, 0:count] < 8, row, 0.0)
                            out_ref[to : to + 16, lane : lane + count] = row.astype(jnp.bfloat16)

        wait_all(start_all([(out_ref, out_any)], sems))


def up0(partials, ups):
    f32, bf16 = jnp.float32, jnp.bfloat16
    return kernel_call(
        up0_body,
        jax.ShapeDtypeStruct((768, 192), bf16),
        [
            pltpu.VMEM((8, 192, 128), bf16),
            *[pltpu.VMEM((384, 432), bf16)] * 4,
            pltpu.VMEM((192, 1728), bf16),
            pltpu.VMEM((192, 2304), bf16),
            pltpu.VMEM((128, 192), f32),
            pltpu.VMEM((2, 288, 192), f32),
            pltpu.VMEM((288, 2304), f32),
            pltpu.VMEM((4, 576, 128), f32),
            pltpu.VMEM((768, 192), bf16),
        ],
        partials, *ups,
        copies=5,
    )


def group_rows(first, second, group):
    at, end = group * 576, group * 576 + 576
    if end <= 2592:
        return first[:, at:end]
    if at >= 2592:
        return second[:, at - 2592 : end - 2592]
    return jnp.concatenate([first[:, at:2592], second[:, 0 : end - 2592]], axis=1)


def section1_body(x_any, g_any, *refs):
    kernels_any, ups_any, out_any = refs[0:4], refs[4:8], refs[8]
    x_ref, g_ref = refs[9:11]
    k_own, k_z, k_x, k_d, own, nz, nx, nd = refs[11:19]
    gf, full, base, xx, acc, hs, cat, taps, p, t, out_ref, sems = refs[19:]
    s, h, w = (lax.axis_index(axis) for axis in AXES)

    @pl.when((s == 1) & (h < 2))
    def _():
        coming = start_all([(x_any, x_ref), (g_any, g_ref)], sems)
        arriving = start_all(list(zip(kernels_any, (k_own, k_z, k_x, k_d))), sems, 2)
        rising = start_all(list(zip(ups_any, (own, nz, nx, nd))), sems, 6)
        wait_all(coming)

        @pl.when(w == 0)
        def _():
            gf[...] = g_ref[...].astype(jnp.float32)
            full[...] = jnp.zeros_like(full)
            for frame in range(2):
                for hh in range(4):
                    for ww in range(2):
                        for r in range(4):
                            for c in range(4):
                                row = 12 + frame * 4 + r
                                at = frame * 288 + (1 + hh * 4 + r) * 16 + ww * 4 + c
                                full[at : at + 1, :] = gf[hh * 2 + ww, row : row + 1, c * 192 : (c + 1) * 192]
            for frame in range(2):
                start = pl.multiple_of(frame * 288 + h * 96, 32)
                base[frame * 192 : (frame + 1) * 192] = full[pl.ds(start, 192), :]
            base[384:768] = x_ref[0:384].astype(jnp.float32)

        @pl.when(w == 1)
        def _():
            base[...] = x_ref[...].astype(jnp.float32)

        for dx, moved in enumerate(shifts(base[...], 16, 8)):
            xx[:, dx * 192 : (dx + 1) * 192] = moved.astype(jnp.bfloat16)
        wait_all(arriving)
        for z in range(2):

            @pl.when(h == z)
            def _():
                for k, (mine, other) in enumerate(((k_own, k_z), (k_x, k_d))):
                    first, second = (mine, other) if z == 0 else (other, mine)
                    total = None
                    for group in range(9):
                        start = group // 3 * 192 + group % 3 * 16
                        term = dot_t(xx[start : start + 352, :], group_rows(first, second, group))
                        total = term if total is None else total + term
                    acc[k] = total

        squares = sum(jnp.sum(acc[k] * acc[k], axis=1, keepdims=True) for k in range(2))
        inverse = lax.rsqrt(squares / 384.0 + EPSILON)
        index = index_of((352, 192))
        keep = (index % 192 < 160) & (index % 16 < 8)
        for k in range(2):
            hs[k, 0:352] = jnp.where(keep, silu(acc[k] * inverse), 0.0).astype(jnp.bfloat16)
            hs[k, 352:384] = jnp.zeros((32, 192), jnp.bfloat16)
        wait_all(rising)
        for k, (mine, other) in enumerate(((own, nz), (nx, nd))):
            join_taps(h, (mine[0:192], mine[192:384]), (other[0:192], other[192:384]), cat, taps, 192, 256)
            term = dot(hs[k], taps[...])
            if k == 0:
                p[...] = term
            else:
                p[...] = p[...] + term
        upsample(p, t, 16, 8, 256)
        out_ref[...] = jnp.zeros_like(out_ref)
        for z in range(2):

            @pl.when(h == z)
            def _():
                for frame in range(2):
                    for r in range(19):
                        y = r + z
                        at = frame * 384 + (y // 2) * 32
                        to = (r + 1 - z) * 16
                        for lane, count in ((0, 128), (128, 64)):
                            row = t[y % 2 * 2 + lane // 128, at : at + 16, 0:count].astype(jnp.bfloat16)
                            lane0 = frame * 192 + lane
                            out_ref[to : to + 16, lane0 : lane0 + count] = row

        wait_all(start_all([(out_ref, out_any)], sems))


def section1(frames, gathered, kernels, ups):
    f32, bf16 = jnp.float32, jnp.bfloat16
    return kernel_call(
        section1_body,
        jax.ShapeDtypeStruct((320, 384), bf16),
        [
            pltpu.VMEM((768, 192), bf16),
            pltpu.VMEM((8, 20, 768), bf16),
            *[pltpu.VMEM((192, 2592), bf16)] * 4,
            *[pltpu.VMEM((384, 432), bf16)] * 4,
            pltpu.VMEM((8, 20, 768), f32),
            pltpu.VMEM((576, 192), f32),
            pltpu.VMEM((768, 192), f32),
            pltpu.VMEM((768, 576), bf16),
            pltpu.VMEM((2, 352, 192), f32),
            pltpu.VMEM((2, 384, 192), bf16),
            pltpu.VMEM((192, 1728), bf16),
            pltpu.VMEM((192, 2304), bf16),
            pltpu.VMEM((384, 2304), f32),
            pltpu.VMEM((4, 768, 128), f32),
            pltpu.VMEM((320, 384), bf16),
        ],
        frames, gathered, *kernels, *ups,
        copies=10,
    )


def pick(step, count, at):
    source = lax.broadcasted_iota(jnp.int32, (192, 192), 1)
    target = lax.broadcasted_iota(jnp.int32, (192, 192), 0) - at
    return ((source == target * step) & (target >= 0) & (target < count)).astype(jnp.bfloat16)


def merge_body(*refs):
    kernels_any, ups_any, (k2_any, k3_any, up_any) = refs[0:4], refs[4:8], refs[8:11]
    pieces, ups = refs[11:15], refs[15:19]
    k2, wide, k3, cat, up, sems = refs[19:]
    s, h = lax.axis_index("segment"), lax.axis_index("ha")
    bf16 = jnp.bfloat16

    @pl.when((s >= 2) & (h < 2))
    def _():
        coming = start_all(list(zip(kernels_any, pieces)), sems)
        rising = start_all([(a.at[0:192], b) for a, b in zip(ups_any, ups)], sems, 4)
        wait_all(rising)
        step = jnp.where(s == 2, 2, 4)
        count = jnp.where(s == 2, 96, 48)
        mine, theirs = pick(step, count, 0), pick(step, count, count)
        near = (dot(mine, ups[0][...]) + dot(theirs, ups[2][...])).astype(bf16)
        far = (dot(mine, ups[1][...]) + dot(theirs, ups[3][...])).astype(bf16)
        for z in range(2):

            @pl.when(h == z)
            def _():
                cat[:, z * 432 : z * 432 + 432] = near
                cat[:, (1 - z) * 432 : (1 - z) * 432 + 432] = far

        up[...] = jnp.zeros_like(up)
        for tap in range(9):
            up[:, tap * 128 : tap * 128 + 96] = cat[:, tap * 96 : (tap + 1) * 96]
        sending = start_all([(up, up_any)], sems, 4)
        wait_all(coming)
        own, nz, nx, nd = pieces

        @pl.when(s == 2)
        def _():
            for z in range(2):

                @pl.when(h == z)
                def _():
                    for part, (a, b) in enumerate(((own, nx), (nz, nd))):
                        at = (part ^ z) * 2592
                        k2[:, at : at + 2592] = (dot(mine, a[...]) + dot(theirs, b[...])).astype(bf16)

            wait_all(start_all([(k2, k2_any)], sems))

        @pl.when(s == 3)
        def _():
            for z in range(2):

                @pl.when(h == z)
                def _():
                    a, b = ((own, nx), (nz, nd))[z]
                    wide[...] = (dot(mine[0:96], a[...]) + dot(theirs[0:96], b[...])).astype(bf16)

            k3[...] = jnp.zeros_like(k3)
            for tap in range(27):
                k3[:, tap * 128 : tap * 128 + 96] = wide[:, tap * 96 : tap * 96 + 96]
            wait_all(start_all([(k3, k3_any)], sems))

        wait_all(sending)


def merge(kernels, ups):
    bf16 = jnp.bfloat16
    shapes = ((192, 5184), (96, 3456), (192, 1152))
    return kernel_call(
        merge_body,
        tuple(jax.ShapeDtypeStruct(shape, bf16) for shape in shapes),
        [
            *[pltpu.VMEM((192, 2592), bf16)] * 4,
            *[pltpu.VMEM((192, 432), bf16)] * 4,
            pltpu.VMEM((192, 5184), bf16),
            pltpu.VMEM((96, 2592), bf16),
            pltpu.VMEM((96, 3456), bf16),
            pltpu.VMEM((192, 864), bf16),
            pltpu.VMEM((192, 1152), bf16),
        ],
        *kernels, *ups,
        copies=8,
    )


def caches_body(*refs):
    parts, (c_any, d_any) = refs[0:6], refs[6:8]
    bands, wide, c_full, d_full, c, d, sems = refs[8:]
    s, h, w = (lax.axis_index(axis) for axis in AXES)
    f32, bf16 = jnp.float32, jnp.bfloat16

    @pl.when((s >= 2) & (h < 2))
    def _():
        pairs = [(a, bands.at[n // 2, n % 2 * 48 : n % 2 * 48 + 48]) for n, a in enumerate(parts)]
        wait_all(start_all(pairs, sems))
        c_full[...] = jnp.zeros_like(c_full)
        d_full[...] = jnp.zeros_like(d_full)
        for band in range(3):
            wide[...] = bands[band].astype(f32)
            for side in range(2):
                swapped = (w + side) % 2
                for frame in range(2):
                    row = side * 48 + frame * 8
                    for column in range(8):
                        at = (frame * 26 + 1 + band * 8) * 16 + swapped * 8 + column
                        lane = column * 192
                        c_full[0, pl.ds(at, 8, stride=16), :] = wide[row : row + 8, lane : lane + 128]
                        tail = jnp.concatenate([wide[row : row + 8, lane + 128 : lane + 192]] * 2, axis=1)
                        c_full[1, pl.ds(at, 8, stride=16), :] = tail
                    row = side * 48 + 16 + frame * 16
                    for column in range(16):
                        at = (frame * 50 + 1 + band * 16) * 32 + swapped * 16 + column
                        lane = column * 96
                        part = wide[row : row + 16, lane : lane + 96]
                        part = jnp.concatenate([part, part[:, 0:32]], axis=1)
                        d_full[pl.ds(at, 16, stride=32), :] = part
        for frame in range(2):
            at = pl.multiple_of((frame * 26 + h * 6) * 16, 32)
            c[frame * 320 : frame * 320 + 320, 0:128] = c_full[0, pl.ds(at, 320), :].astype(bf16)
            c[frame * 320 : frame * 320 + 320, 128:192] = c_full[1, pl.ds(at, 320), 0:64].astype(bf16)
            at = pl.multiple_of((frame * 50 + h * 15) * 32, 32)
            d[frame * 1120 : frame * 1120 + 1120, :] = d_full[pl.ds(at, 1120), 0:96].astype(bf16)
        wait_all(start_all([(c, c_any), (d, d_any)], sems))


def caches(bands):
    f32, bf16 = jnp.float32, jnp.bfloat16
    return kernel_call(
        caches_body,
        (jax.ShapeDtypeStruct((640, 192), bf16), jax.ShapeDtypeStruct((2240, 96), bf16)),
        [
            pltpu.VMEM((3, 96, 1536), bf16),
            pltpu.VMEM((96, 1536), f32),
            pltpu.VMEM((2, 832, 128), f32),
            pltpu.VMEM((3200, 128), f32),
            pltpu.VMEM((640, 192), bf16),
            pltpu.VMEM((2240, 96), bf16),
        ],
        *bands,
        copies=6,
    )


def sections23_body(same2, same3, other2, other3, c_any, d_any, k2_own, k2_sent, k3_own, k3_sent, u_own, u_sent,
                    out0, out1, out2, out3, pairs, d_ref, k2, k3, u2, u3, line, base, xx, hs, p, t, base3, xx3, hs3, p3, t3, rows3, out_ref,
                    sems):
    s, h, w = (lax.axis_index(axis) for axis in AXES)
    f32, bf16 = jnp.float32, jnp.bfloat16

    @pl.when((s >= 2) & (h < 2))
    def _():
        frame = (s - 2) * 2 + w
        line[0:640] = jnp.zeros((640, 192), bf16)
        for segment, same, other in ((2, same2, other2), (3, same3, other3)):

            @pl.when(s == segment)
            def _():
                held2, held3 = (k2_own, k3_sent) if segment == 2 else (k2_sent, k3_own)
                up2, up3 = (u_own, u_sent) if segment == 2 else (u_sent, u_own)
                start_all(
                    [
                        (same, pairs.at[w]),
                        (other, pairs.at[1 - w]),
                        (c_any, line.at[640:1280]),
                        (held2, k2),
                        (up2, u2),
                        (d_any, d_ref),
                        (held3, k3),
                        (up3.at[0:96], u3),
                    ],
                    sems,
                )

        coming = [
            pltpu.make_async_copy(a, b, sems.at[n])
            for n, (a, b) in enumerate(
                [
                    (same2, pairs.at[0]),
                    (other2, pairs.at[1]),
                    (c_any, line.at[640:1280]),
                    (k2_own, k2),
                    (u_own, u2),
                    (d_any, d_ref),
                    (k3_own, k3),
                    (u_own.at[0:96], u3),
                ]
            )
        ]
        wait_all(coming[0:3])
        for number in range(2):
            for k in range(2):
                at = 1280 + (2 * number + k) * 320
                line[at : at + 320] = pairs[number, :, k * 192 : (k + 1) * 192]

        base[...] = line[pl.ds(pl.multiple_of(frame * 320, 320), 1600), :].astype(f32)
        for dx, moved in enumerate(shifts(base[...], 16, 16)):
            xx[:, dx * 192 : (dx + 1) * 192] = moved.astype(bf16)
        coming[3].wait()
        total = None
        for group in range(9):
            start = group // 3 * 320 + group % 3 * 16
            term = dot_t(xx[start : start + 928, :], k2[:, group * 576 : (group + 1) * 576])
            total = term if total is None else total + term
        inverse = lax.rsqrt(jnp.sum(total * total, axis=1, keepdims=True) / 192.0 + EPSILON)
        keep = index_of((928, 192)) % 320 < 288
        hs[0:928] = jnp.where(keep, silu(total * inverse), 0.0).astype(bf16)
        hs[928:960] = jnp.zeros((32, 192), bf16)
        coming[4].wait()
        p[...] = dot(hs[...], u2[...])
        upsample(p, t, 16, 16, 128)

        for z in range(2):

            @pl.when(h == z)
            def _():
                blank = 0 if z == 0 else 34
                for moment in range(3):
                    to = moment * 1120 + blank * 32
                    base3[to : to + 32] = jnp.zeros((32, 96), f32)
                    for r in range(34):
                        y = r + 2 * z
                        at = moment * 640 + (y // 2) * 32
                        to = moment * 1120 + (r + 1 - z) * 32
                        base3[to : to + 32] = t[y % 2, at : at + 32, 0:96].astype(bf16).astype(f32)

        wait_all(coming[5:8])

        @pl.when(frame == 0)
        def _():
            base3[0:2240] = d_ref[...].astype(f32)

        @pl.when(frame == 1)
        def _():
            base3[0:1120] = d_ref[1120:2240].astype(f32)

        xx3[...] = jnp.zeros_like(xx3)
        for dx, moved in enumerate(shifts(base3[...], 32, 32)):
            xx3[:, dx * 128 : dx * 128 + 96] = moved.astype(bf16)
        total = None
        for group in range(9):
            start = group // 3 * 1120 + group % 3 * 32
            term = dot_t(xx3[start : start + 1056, :], k3[:, group * 384 : (group + 1) * 384])
            total = term if total is None else total + term
        inverse = lax.rsqrt(jnp.sum(total * total, axis=1, keepdims=True) / 96.0 + EPSILON)
        hs3[0:1056] = silu(total * inverse).astype(bf16)
        hs3[1056:1120] = jnp.zeros((64, 96), bf16)
        p3[...] = dot(hs3[...], u3[...])
        upsample(p3, t3, 32, 32, 128)
        for z in range(2):

            @pl.when(h == z)
            def _():
                for a in range(2):
                    for four in range(16):
                        parts = [
                            t3[a, pl.ds(z * 64 + four * 4 + n, 32, stride=64), :][:, 0:96] for n in range(4)
                        ]
                        row = jnp.concatenate(parts, axis=1)
                        for n in range(3):
                            rows3[four * 3 + n, pl.ds(a, 32, stride=2), :] = row[:, n * 128 : (n + 1) * 128]
        for tile in range(48):
            lane = tile % 24 * 128
            for n in range(2):
                part = rows3[tile, n * 32 : n * 32 + 32, :].astype(bf16)
                out_ref[n * 2 + tile // 24, :, lane : lane + 128] = part

        wait_all(start_all([(out_ref.at[n], target) for n, target in enumerate((out0, out1, out2, out3))], sems))


def sections23(received, c, d, kernels):
    f32, bf16 = jnp.float32, jnp.bfloat16
    return kernel_call(
        sections23_body,
        tuple([jax.ShapeDtypeStruct((32, 3072), bf16)] * 4),
        [
            pltpu.VMEM((2, 320, 384), bf16),
            pltpu.VMEM((2240, 96), bf16),
            pltpu.VMEM((192, 5184), bf16),
            pltpu.VMEM((96, 3456), bf16),
            pltpu.VMEM((192, 1152), bf16),
            pltpu.VMEM((96, 1152), bf16),
            pltpu.VMEM((2560, 192), bf16),
            pltpu.VMEM((1600, 192), f32),
            pltpu.VMEM((1600, 576), bf16),
            pltpu.VMEM((960, 192), bf16),
            pltpu.VMEM((960, 1152), f32),
            pltpu.VMEM((2, 1920, 128), f32),
            pltpu.VMEM((3360, 96), f32),
            pltpu.VMEM((3360, 384), bf16),
            pltpu.VMEM((1120, 96), bf16),
            pltpu.VMEM((1120, 1152), f32),
            pltpu.VMEM((2, 2240, 128), f32),
            pltpu.VMEM((48, 64, 128), f32),
            pltpu.VMEM((4, 32, 3072), bf16),
        ],
        *received, c, d, *kernels,
        copies=8,
    )


def relay(latent, cache_a, cache_b, cache_c, cache_d, conv_pack, up_pack):
    h, w = lax.axis_index("ha"), lax.axis_index("wa")
    k, u = conv_pack[0].T, up_pack[0]

    along_z = square((1, 2), 1, 0) + [((3, 0, w_), (3, 1, w_)) for w_ in range(2)]
    along_x = square((1, 2), 0, 1) + [((3, 0, w_), (3, 0, w_ ^ 1)) for w_ in range(2)]
    across = square((1, 2), 0, 1) + [((3, 1, w_), (3, 1, w_ ^ 1)) for w_ in range(2)]
    u_far = send(u, [((s_, h_ + 2, w_), (s_, h_, w_)) for s_ in (0, 1) for h_ in range(2) for w_ in range(2)])
    k_z, k_x = send(k, along_z), send(k, along_x)

    tiles = jnp.concatenate([latent.reshape(8, 768), cache_a.reshape(4, 768), cache_b.reshape(8, 768)], axis=0)
    gathered = lax.all_to_all(
        jnp.broadcast_to(tiles[None], (8, 20, 768)), ("ha", "wa"), split_axis=0, concat_axis=0, tiled=True
    )
    gathered, u_far = lax.optimization_barrier((gathered, u_far))
    ups = jnp.concatenate([u, u_far], axis=0)
    u_z, u_x = send(ups, square(range(4), 1, 0)), send(ups, square(range(4), 0, 1))
    partial_sums = conv0(gathered, k)
    partial_sums, k_z, u_x = lax.optimization_barrier((partial_sums, k_z, u_x))
    k_d = send(k_z, across)
    u_d = send(u_x, square(range(4), 1, 0))
    partials = lax.all_to_all(partial_sums, ("ha", "wa"), split_axis=0, concat_axis=0, tiled=True)
    kernels, risers = (k, k_z, k_x, k_d), (ups, u_z, u_x, u_d)
    risen = up0(partials, risers)
    given = send(risen, [((0, h_, w_), (1, h_, w_)) for h_ in range(2) for w_ in range(2)])

    out1 = section1(given, gathered, kernels, risers)
    received = [
        send(out1, [((1, h_, w_), (s_, h_, w_ ^ dw)) for h_ in range(2) for w_ in range(2)])
        for dw in range(2)
        for s_ in (2, 3)
    ]

    out1, cache_c, cache_d, u_z = lax.optimization_barrier((out1, cache_c, cache_d, u_z))
    own = jnp.concatenate([cache_c.reshape(16, 1536), cache_d.reshape(32, 1536)], axis=0)
    bands = [own] + [
        send(own, [((s_, h_ + n, w_ ^ dw), (s_, h_, w_)) for s_ in (2, 3) for h_ in range(2) for w_ in range(2)])
        for n in range(3)
        for dw in range(2)
        if n + dw
    ]
    k2, k3, u23 = merge(kernels, (ups, u_z, u_x, u_d))
    pairs = [((s_, h_, w_), (s_ ^ 1, h_, w_)) for s_ in (2, 3) for h_ in range(2) for w_ in range(2)]
    k2_sent = send(k2, [pair for pair in pairs if pair[0][0] == 2])
    k3_sent = send(k3, [pair for pair in pairs if pair[0][0] == 3])
    u_sent = send(u23, pairs)
    c, d = caches(bands)
    blocks = sections23(received, c, d, (k2, k2_sent, k3, k3_sent, u23, u_sent))

    arrived = [
        send(
            blocks[2 * n + half],
            [((2 + c_, z, x), (2 * c_ + x, 2 * z + n, half)) for c_ in range(2) for z in range(2) for x in range(2)],
        )
        for n in range(2)
        for half in range(2)
    ]
    lower_half = jnp.where(w == 0, arrived[2], arrived[3])
    upper_half = jnp.where(w == 0, arrived[0], arrived[1])
    return jnp.where(h % 2 == 0, upper_half, lower_half)[None]


def solution(mesh):
    in_specs = (
        P(None, "ha", "wa"),
        P(None, "ha", "wa"),
        P(None, "ha", "wa"),
        P(None, "ha", "wa"),
        P(None, "ha", "wa"),
        P("segment", "ha", "wa"),
        P("segment", "wa", "ha"),
    )
    out_specs = P("segment", "ha", "wa")
    sizes = tuple(mesh.shape[axis] for axis in AXES)
    program = relay if sizes == (4, 4, 2) else per_device
    return jax.shard_map(
        program, mesh=mesh, in_specs=in_specs, out_specs=out_specs, check_vma=False
    )
```

```python
from functools import partial

import jax
import jax.numpy as jnp
from jax import lax
from jax.experimental import pallas as pl
from jax.experimental.pallas import tpu as pltpu
from jax.sharding import PartitionSpec as P

WIDE = 384
MID = 192
NARROW = 96


EPSILON = 1e-06


def shortened(array):

    def short(part):
        return part.astype(jnp.bfloat16) if part.dtype == jnp.float32 else part

    return jax.tree.map(short, array)


def passed_along(value, axis, steps):
    count = lax.axis_size(axis)
    initial, last = (max(0, -steps), min(count, count - steps))
    return lax.ppermute(value, axis, [(source, source + steps) for source in range(initial, last)])


def layer_table():
    return ((WIDE, WIDE, MID), (MID, WIDE, MID), (MID, MID, NARROW), (NARROW, NARROW, NARROW))


def round_up(amount):
    return -(-amount // 128) * 128


def volume(target):
    amount = 1
    for extent in target:
        amount = amount * extent
    return amount


def flat_pad(tensor, length):
    leading = tensor.shape[0]
    packed = tensor.reshape(leading, -1)
    return jnp.pad(packed, ((0, 0), (0, length - packed.shape[1])))


def reshaped(packed, target):
    return packed[:, : volume(target)].reshape((packed.shape[0],) + tuple(target))


def add_rows(tensor, from_above, from_below):
    leading, height, width, channels = tensor.shape
    upper = reshaped(from_above, (1, width, channels))
    lower = reshaped(from_below, (1, width, channels))
    return jnp.concatenate([upper, tensor, lower], axis=1)


def add_cols(tensor, from_left, from_right):
    leading, height, width, channels = tensor.shape
    before = reshaped(from_left, (height, 1, channels))
    after = reshaped(from_right, (height, 1, channels))
    return jnp.concatenate([before, tensor, after], axis=2)


def trade_rows(upper_rim, bottom):
    return (
        jax.tree.map(
            lambda part, own: part.astype(own.dtype),
            passed_along(shortened(bottom), "ha", 1),
            bottom,
        ),
        jax.tree.map(
            lambda part, own: part.astype(own.dtype),
            passed_along(shortened(upper_rim), "ha", -1),
            upper_rim,
        ),
    )


def trade_cols(left_rim, right_rim):
    return (
        jax.tree.map(
            lambda part, own: part.astype(own.dtype),
            passed_along(shortened(right_rim), "wa", 1),
            right_rim,
        ),
        jax.tree.map(
            lambda part, own: part.astype(own.dtype),
            passed_along(shortened(left_rim), "wa", -1),
            left_rim,
        ),
    )


def causal_conv(stacked, kernel):
    result = lax.conv_general_dilated(
        stacked[None],
        kernel,
        (1, 1, 1),
        "VALID",
        dimension_numbers=("NDHWC", "DHWIO", "NDHWC"),
        preferred_element_type=jnp.float32,
    )
    return result[0, 0]


def activate(conv_sum):
    inverse = lax.rsqrt(jnp.mean(conv_sum * conv_sum, axis=-1, keepdims=True) + EPSILON)
    return jax.nn.silu(conv_sum * inverse).astype(jnp.bfloat16)


def upsample_conv(hidden_ext, kernel):
    expanded = jnp.repeat(jnp.repeat(hidden_ext, 2, axis=0), 2, axis=1)[1:-1, 1:-1]
    result = lax.conv_general_dilated(
        expanded[None],
        kernel,
        (1, 1),
        "VALID",
        dimension_numbers=("NHWC", "HWIO", "NHWC"),
        preferred_element_type=jnp.float32,
    )
    return result[0].astype(jnp.bfloat16)


def per_device(latent, cache_a, cache_b, cache_c, cache_d, conv_pack, up_pack):
    frames = latent.shape[0]
    tile_rows = latent.shape[1]
    tile_cols = latent.shape[2] // WIDE
    layers = layer_table()
    section = lax.axis_index("segment")
    segments = lax.axis_size("segment")
    final_segment = segments - 1
    input_shapes = [
        (tile_rows << level, tile_cols << level, layers[level][0]) for level in range(4)
    ]
    mid_shapes = [(tile_rows << level, tile_cols << level, layers[level][1]) for level in range(4)]
    out_shapes = [
        (tile_rows << level + 1, tile_cols << level + 1, layers[level][2]) for level in range(4)
    ]
    ext_shapes = [(target[0] + 2, target[1] + 2, target[2]) for target in input_shapes]
    all_shapes = input_shapes + mid_shapes
    row_length = round_up(max((target[1] * target[2] for target in all_shapes)))
    column_length = round_up(max(((target[0] + 2) * target[2] for target in all_shapes)))
    size_input = round_up(max((volume(target) for target in input_shapes)))
    size_middle = round_up(max((volume(target) for target in mid_shapes)))
    size_extended = round_up(max((volume(target) for target in ext_shapes)))
    size_output = round_up(max((volume(target) for target in out_shapes)))
    final_shape = out_shapes[3]
    final_count = volume(final_shape)
    conv_rows, up_rows = (
        lax.all_gather(conv_pack, "ha", axis=1, tiled=True),
        lax.all_gather(up_pack, "ha", axis=2, tiled=True),
    )
    conv_all, up_all = (
        lax.all_gather(conv_rows, "wa", axis=2, tiled=True),
        lax.all_gather(up_rows, "wa", axis=1, tiled=True),
    )

    def conv_kernel(level):
        width_in, width_mid, width_out = layers[level]
        columns = conv_all[0, : 27 * width_in, :: WIDE // width_mid]
        return columns.reshape(3, 3, 3, width_in, columns.shape[1])

    def up_kernel(level):
        width_in, width_mid, width_out = layers[level]
        rows_used = up_all[0, :: WIDE // width_mid, : 9 * width_out]
        return rows_used.reshape(width_mid, 3, 3, width_out).transpose(1, 2, 0, 3)

    conv_kernels = [conv_kernel(level) for level in range(4)]
    up_kernels = [up_kernel(level) for level in range(4)]

    def row_rims(packed, shapes):

        def rows_branch(level, packed):
            tensor = reshaped(packed, shapes[level])
            return (flat_pad(tensor[:, :1], row_length), flat_pad(tensor[:, -1:], row_length))

        upper_rim, bottom = lax.switch(
            section, [partial(rows_branch, level) for level in range(4)], packed
        )
        return trade_rows(upper_rim, bottom)

    def extend(packed, shapes):
        from_above, from_below = row_rims(packed, shapes)

        def cols_branch(level, packed, from_above, from_below):
            tensor = add_rows(reshaped(packed, shapes[level]), from_above, from_below)
            return (
                flat_pad(tensor[:, :, :1], column_length),
                flat_pad(tensor[:, :, -1:], column_length),
            )

        left_rim, right_rim = lax.switch(
            section,
            [partial(cols_branch, level) for level in range(4)],
            packed,
            from_above,
            from_below,
        )
        from_left, from_right = trade_cols(left_rim, right_rim)
        return (from_above, from_below, from_left, from_right)

    def assemble(packed, target, rims):
        tensor = add_rows(reshaped(packed, target), rims[0], rims[1])
        return add_cols(tensor, rims[2], rims[3])

    caches = (cache_a, cache_b, cache_c, cache_d)

    def cache_branch(level):
        return flat_pad(caches[level], size_input)

    cached = lax.switch(section, [partial(cache_branch, level) for level in range(4)])
    cache_rims = extend(cached, input_shapes)

    def store_branch(level, packed, rims):
        return flat_pad(assemble(packed, input_shapes[level], rims), size_extended)

    history = lax.switch(
        section, [partial(store_branch, level) for level in range(4)], cached, cache_rims
    )
    finished = jnp.zeros((frames, final_shape[0], final_shape[1] * final_shape[2]), jnp.bfloat16)
    stream = jnp.zeros((1, size_input), jnp.bfloat16)
    for moment in range(frames + segments - 1):
        if moment == 0:
            incoming = stream
        else:
            incoming = jax.tree.map(
                lambda part, own: part.astype(own.dtype),
                passed_along(shortened(stream), "segment", 1),
                stream,
            )
        frame_id = moment - section
        active = (frame_id >= 0) & (frame_id < frames)
        chosen = jnp.clip(frame_id, 0, frames - 1)
        picked = lax.dynamic_index_in_dim(latent, chosen, 0, keepdims=True)
        current = jnp.where(section == 0, flat_pad(picked, size_input), incoming)
        branch_id = jnp.where(active, section, 4)
        rims = extend(current, input_shapes)

        def conv_branch(level, current, history, rims):
            window = assemble(current, input_shapes[level], rims)
            earlier = reshaped(history, ext_shapes[level])
            hidden = activate(
                causal_conv(jnp.concatenate([earlier, window], axis=0), conv_kernels[level])
            )
            return (flat_pad(hidden[None], size_middle), flat_pad(window, size_extended))

        def spare_conv(current, history, rims):
            return (
                jnp.zeros((1, size_middle), jnp.bfloat16),
                jnp.zeros((1, size_extended), jnp.bfloat16),
            )

        hidden, window = lax.switch(
            branch_id,
            [partial(conv_branch, level) for level in range(4)] + [spare_conv],
            current,
            history,
            rims,
        )
        hidden_rims = extend(hidden, mid_shapes)

        def up_branch(level, hidden, hidden_rims):
            expanded = assemble(hidden, mid_shapes[level], hidden_rims)[0]
            return flat_pad(upsample_conv(expanded, up_kernels[level])[None], size_output)

        def spare_up(hidden, hidden_rims):
            return jnp.zeros((1, size_output), jnp.bfloat16)

        produced = lax.switch(
            branch_id,
            [partial(up_branch, level) for level in range(4)] + [spare_up],
            hidden,
            hidden_rims,
        )
        shifted = jnp.concatenate([history[1:], window], axis=0)
        history = jnp.where(active, shifted, history)
        stream = produced[:, :size_input]
        if moment >= final_segment:
            finished_id = moment - final_segment
            picture = produced[:, :final_count].reshape(
                1, final_shape[0], final_shape[1] * final_shape[2]
            )
            finished = finished.at[finished_id].set(picture[0])
    collected = lax.all_to_all(finished, "segment", split_axis=0, concat_axis=0, tiled=True)
    per_segment = frames // segments
    own_frame = collected[final_segment * per_segment : (final_segment + 1) * per_segment]
    return own_frame


AXES = ("segment", "ha", "wa")
VMEM = 60 * 1024 * 1024


def place(s, h, w):
    return (s * 4 + h) * 2 + w


def send(value, pairs):
    return lax.ppermute(value, AXES, [(place(*a), place(*b)) for a, b in pairs])


def square(segments, dh, dw):
    return [
        ((s, h, w), (s, h ^ dh, w ^ dw)) for s in segments for h in range(2) for w in range(2)
    ]


def kernel_call(body, out_shape, scratch, *args, copies=0, flops=1000):
    return pl.pallas_call(
        body,
        out_shape=out_shape,
        in_specs=[pl.BlockSpec(memory_space=pl.ANY)] * len(args),
        out_specs=jax.tree.map(lambda _: pl.BlockSpec(memory_space=pl.ANY), out_shape),
        scratch_shapes=scratch + [pltpu.SemaphoreType.DMA((copies,))],
        compiler_params=pltpu.CompilerParams(vmem_limit_bytes=VMEM),
        cost_estimate=pl.CostEstimate(flops=flops, bytes_accessed=1000, transcendentals=0),
    )(*args)


def start_all(pairs, sems, first=0):
    copies = [pltpu.make_async_copy(a, b, sems.at[first + n]) for n, (a, b) in enumerate(pairs)]
    for copy in copies:
        copy.start()
    return copies


def wait_all(copies):
    for copy in copies:
        copy.wait()


def dot(a, b):
    return jnp.dot(a, b, preferred_element_type=jnp.float32)


def dot_t(a, b):
    return lax.dot_general(a, b, (((1,), (1,)), ((), ())), preferred_element_type=jnp.float32)


def index_of(shape):
    return lax.broadcasted_iota(jnp.int32, shape, 0)


def silu(v):
    return v / (1.0 + jnp.exp(-v))


def shifts(base, pitch, width):
    n = base.shape[0]
    left, right = pltpu.roll(base, 1, 0), pltpu.roll(base, n - 1, 0)
    if pitch == width:
        column = index_of(base.shape) % pitch
        left = jnp.where(column == 0, 0.0, left)
        right = jnp.where(column == width - 1, 0.0, right)
    return left, base, right


def upsample(p_ref, t_ref, pitch, width, lanes):
    n = p_ref.shape[0]
    blocks = lanes // 128
    column = index_of((n, 128)) % pitch
    for block in range(blocks):

        def tap(dy, dx):
            at = (dy * 3 + dx) * lanes + block * 128
            return p_ref[:, at : at + 128]

        for b in range(2):
            rows = []
            for dy in range(3):
                middle = tap(dy, 1)
                if b == 0:
                    far = pltpu.roll(tap(dy, 0), 1, 0)
                    if pitch == width:
                        far = jnp.where(column == 0, 0.0, far)
                    rows.append(far + middle + tap(dy, 2))
                else:
                    far = pltpu.roll(tap(dy, 2), n - 1, 0)
                    if pitch == width:
                        far = jnp.where(column == width - 1, 0.0, far)
                    rows.append(tap(dy, 0) + middle + far)
            t_ref[block, pl.ds(b, n, stride=2), :] = pltpu.roll(rows[0], pitch, 0) + rows[1] + rows[2]
            t_ref[blocks + block, pl.ds(b, n, stride=2), :] = (
                rows[0] + rows[1] + pltpu.roll(rows[2], n - pitch, 0)
            )


def tiles_body(latent_any, a_any, b_any, out_any, latent, a, b, rows, out, sems):
    wait_all(start_all([(latent_any, latent), (a_any, a), (b_any, b)], sems))

    @pl.when(lax.axis_index("segment") == 0)
    def _():
        for frame in range(4):
            rows[frame * 2 : frame * 2 + 2] = latent[frame].astype(jnp.float32)
        for frame in range(2):
            rows[8 + frame * 2 : 10 + frame * 2] = a[frame].astype(jnp.float32)

    @pl.when(lax.axis_index("segment") > 0)
    def _():
        for frame in range(2):
            rows[frame * 4 : frame * 4 + 4] = b[frame].astype(jnp.float32)
        rows[8:12] = jnp.zeros((4, 768), jnp.float32)

    out[...] = rows[...].astype(jnp.bfloat16)
    wait_all(start_all([(out, out_any.at[n]) for n in range(8)], sems))


def spread_tiles(latent, cache_a, cache_b):
    bf16 = jnp.bfloat16
    return kernel_call(
        tiles_body,
        jax.ShapeDtypeStruct((8, 12, 768), bf16),
        [
            pltpu.VMEM((4, 2, 768), bf16),
            pltpu.VMEM((2, 2, 768), bf16),
            pltpu.VMEM((2, 4, 768), bf16),
            pltpu.VMEM((12, 768), jnp.float32),
            pltpu.VMEM((12, 768), bf16),
        ],
        latent, cache_a, cache_b,
        copies=8,
    )


def conv0_body(g_any, k_any, out_any, g_ref, k_ref, gf, base, xx, acc, buf, out_ref, sems):
    s, h = lax.axis_index("segment"), lax.axis_index("ha")

    @pl.when(s == 0)
    def _():
        coming = start_all([(g_any, g_ref), (k_any, k_ref)], sems)
        base[...] = jnp.zeros_like(base)
        coming[0].wait()
        gf[...] = g_ref[...].astype(jnp.float32)
        for frame in range(6):
            for hh in range(4):
                for ww in range(2):
                    for r in range(2):
                        row = 8 + frame * 2 + r if frame < 2 else (frame - 2) * 2 + r
                        for c in range(2):
                            at = frame * 160 + (1 + 2 * hh + r) * 16 + 2 * ww + c
                            base[at : at + 1, :] = gf[hh * 2 + ww, row : row + 1, c * 384 : (c + 1) * 384]
        for dx, moved in enumerate(shifts(base[...], 16, 4)):
            xx[dx] = moved.astype(jnp.bfloat16)
        coming[1].wait()
        for part in range(4):

            @pl.when(h == part)
            def _():
                total = None
                at, end = part * 2592, part * 2592 + 2592
                while at < end:
                    tap, c0 = divmod(at, 384)
                    c1 = min(384, c0 + end - at)
                    dt, dy, dx = tap // 9, tap // 3 % 3, tap % 3
                    start = dt * 160 + dy * 16
                    k0 = at - part * 2592
                    term = dot_t(xx[dx, start : start + 608, c0:c1], k_ref[:, k0 : k0 + c1 - c0])
                    total = term if total is None else total + term
                    at += c1 - c0
                acc[...] = total

        for frame in range(4):
            for r in range(8):
                to, at = (frame * 8 + r) * 4, frame * 160 + r * 16
                buf[to : to + 4, :] = acc[at : at + 4, :]
        out_ref[0:128, :] = buf[:, 0:128].astype(jnp.bfloat16)
        tail = jnp.concatenate([buf[0:64, 128:192], buf[64:128, 128:192]], axis=1)
        out_ref[128:192, :] = tail.astype(jnp.bfloat16)
        wait_all(start_all([(out_ref, out_any)], sems))


def conv0(gathered, k):
    f32, bf16 = jnp.float32, jnp.bfloat16
    return kernel_call(
        conv0_body,
        jax.ShapeDtypeStruct((192, 128), bf16),
        [
            pltpu.VMEM((8, 12, 768), bf16),
            pltpu.VMEM((192, 2592), bf16),
            pltpu.VMEM((8, 12, 768), f32),
            pltpu.VMEM((960, 384), f32),
            pltpu.VMEM((3, 960, 384), bf16),
            pltpu.VMEM((608, 192), f32),
            pltpu.VMEM((128, 192), f32),
            pltpu.VMEM((192, 128), bf16),
        ],
        gathered, k,
        copies=8,
    )


def fold_body(own_any, far_any, out_any, own, far, out, sems):
    s, h = lax.axis_index("segment"), lax.axis_index("ha")

    @pl.when((s == 0) & (h < 2))
    def _():
        wait_all(start_all([(own_any, own), (far_any, far)], sems))
        out[...] = (own[...].astype(jnp.float32) + far[...].astype(jnp.float32)).astype(jnp.bfloat16)
        wait_all(start_all([(out, out_any)], sems))


def fold(own, far):
    shape = (192, 128)
    return kernel_call(
        fold_body,
        jax.ShapeDtypeStruct(shape, jnp.bfloat16),
        [pltpu.VMEM(shape, jnp.bfloat16)] * 3,
        own, far,
        copies=2,
    )


def join_taps(h, pieces_own, pieces_z, cat_ref, taps_ref, width, lanes):
    for z in range(2):

        @pl.when(h == z)
        def _():
            for mine, pieces in ((z, pieces_own), (1 - z, pieces_z)):
                for number, piece in enumerate(pieces):
                    at = (mine + 2 * number) * 432
                    cat_ref[:, at : at + 432] = piece

    for tap in range(9):
        taps_ref[:, tap * lanes : tap * lanes + width] = cat_ref[:, tap * width : (tap + 1) * width]


def up0_body(*refs):
    sums_any, ups_any, out_any = refs[0:4], refs[4:8], refs[8]
    y, own, nz, nx, nd = refs[9:14]
    cat, taps, hbuf, hs, p, t, out_ref, sems = refs[14:]
    s, h = lax.axis_index("segment"), lax.axis_index("ha")

    @pl.when((s == 0) & (h < 2))
    def _():
        coming = start_all([(a, y.at[n]) for n, a in enumerate(sums_any)], sems)
        rising = start_all(list(zip(ups_any, (own, nz, nx, nd))), sems, 4)
        wait_all(coming)
        halves = []
        for side in range(2):
            total = y[2 * side].astype(jnp.float32) + y[2 * side + 1].astype(jnp.float32)
            tail = jnp.concatenate([total[128:192, 0:64], total[128:192, 64:128]], axis=0)
            halves.append(jnp.concatenate([total[0:128], tail], axis=1))
        squares = sum(jnp.sum(half * half, axis=1, keepdims=True) for half in halves)
        inverse = lax.rsqrt(squares / 384.0 + EPSILON)
        active = [silu(half * inverse) for half in halves]
        hs[...] = jnp.zeros_like(hs)
        for k in range(2):
            hbuf[...] = active[k]
            for frame in range(4):
                for r in range(8):
                    to, at = frame * 72 + r * 8, (frame * 8 + r) * 4
                    hs[k, to : to + 4, :] = hbuf[at : at + 4, :]
        wait_all(rising)
        for k, (mine, other) in enumerate(((own, nz), (nx, nd))):
            join_taps(h, (mine[0:192], mine[192:384]), (other[0:192], other[192:384]), cat, taps, 192, 256)
            term = dot(hs[k].astype(jnp.bfloat16), taps[...])
            if k == 0:
                p[...] = term
            else:
                p[...] = p[...] + term
        upsample(p, t, 8, 4, 256)
        column = index_of((16, 192))
        out_ref[...] = jnp.zeros_like(out_ref)
        for z in range(2):

            @pl.when(h == z)
            def _():
                for frame in range(4):
                    for r in range(11):
                        y = r + 5 * z
                        at = frame * 144 + (y // 2) * 16
                        to = frame * 192 + (r + 1 - z) * 16
                        for lane, count in ((0, 128), (128, 64)):
                            row = t[y % 2 * 2 + lane // 128, at : at + 16, 0:count]
                            row = jnp.where(column[:, 0:count] < 8, row, 0.0)
                            out_ref[to : to + 16, lane : lane + count] = row.astype(jnp.bfloat16)

        wait_all(start_all([(out_ref, out_any)], sems))


def up0(sums, ups):
    f32, bf16 = jnp.float32, jnp.bfloat16
    return kernel_call(
        up0_body,
        jax.ShapeDtypeStruct((768, 192), bf16),
        [
            pltpu.VMEM((4, 192, 128), bf16),
            *[pltpu.VMEM((384, 432), bf16)] * 4,
            pltpu.VMEM((192, 1728), bf16),
            pltpu.VMEM((192, 2304), bf16),
            pltpu.VMEM((128, 192), f32),
            pltpu.VMEM((2, 288, 192), f32),
            pltpu.VMEM((288, 2304), f32),
            pltpu.VMEM((4, 576, 128), f32),
            pltpu.VMEM((768, 192), bf16),
        ],
        *sums, *ups,
        copies=8,
    )


def group_rows(first, second, group):
    at, end = group * 576, group * 576 + 576
    if end <= 2592:
        return first[:, at:end]
    if at >= 2592:
        return second[:, at - 2592 : end - 2592]
    return jnp.concatenate([first[:, at:2592], second[:, 0 : end - 2592]], axis=1)


def section1_body(x_any, g_any, *refs):
    kernels_any, ups_any, out_any = refs[0:4], refs[4:8], refs[8]
    x_ref, g_ref = refs[9:11]
    k_own, k_z, k_x, k_d, own, nz, nx, nd = refs[11:19]
    gf, full, base, xx, acc, hs, cat, taps, p, t, out_ref, sems = refs[19:]
    s, h, w = (lax.axis_index(axis) for axis in AXES)

    @pl.when((s == 1) & (h < 2))
    def _():
        coming = start_all([(x_any, x_ref), (g_any, g_ref)], sems)
        arriving = start_all(list(zip(kernels_any, (k_own, k_z, k_x, k_d))), sems, 2)
        rising = start_all(list(zip(ups_any, (own, nz, nx, nd))), sems, 6)
        wait_all(coming)

        @pl.when(w == 0)
        def _():
            gf[...] = g_ref[...].astype(jnp.float32)
            full[...] = jnp.zeros_like(full)
            for frame in range(2):
                for hh in range(4):
                    for ww in range(2):
                        for r in range(4):
                            for c in range(4):
                                row = frame * 4 + r
                                at = frame * 288 + (1 + hh * 4 + r) * 16 + ww * 4 + c
                                full[at : at + 1, :] = gf[hh * 2 + ww, row : row + 1, c * 192 : (c + 1) * 192]
            for frame in range(2):
                start = pl.multiple_of(frame * 288 + h * 96, 32)
                base[frame * 192 : (frame + 1) * 192] = full[pl.ds(start, 192), :]
            base[384:768] = x_ref[0:384].astype(jnp.float32)

        @pl.when(w == 1)
        def _():
            base[...] = x_ref[...].astype(jnp.float32)

        for dx, moved in enumerate(shifts(base[...], 16, 8)):
            xx[:, dx * 192 : (dx + 1) * 192] = moved.astype(jnp.bfloat16)
        wait_all(arriving)
        for z in range(2):

            @pl.when(h == z)
            def _():
                for k, (mine, other) in enumerate(((k_own, k_z), (k_x, k_d))):
                    first, second = (mine, other) if z == 0 else (other, mine)
                    total = None
                    for group in range(9):
                        start = group // 3 * 192 + group % 3 * 16
                        term = dot_t(xx[start : start + 352, :], group_rows(first, second, group))
                        total = term if total is None else total + term
                    acc[k] = total

        squares = sum(jnp.sum(acc[k] * acc[k], axis=1, keepdims=True) for k in range(2))
        inverse = lax.rsqrt(squares / 384.0 + EPSILON)
        index = index_of((352, 192))
        keep = (index % 192 < 160) & (index % 16 < 8)
        for k in range(2):
            hs[k, 0:352] = jnp.where(keep, silu(acc[k] * inverse), 0.0).astype(jnp.bfloat16)
            hs[k, 352:384] = jnp.zeros((32, 192), jnp.bfloat16)
        wait_all(rising)
        for k, (mine, other) in enumerate(((own, nz), (nx, nd))):
            join_taps(h, (mine[0:192], mine[192:384]), (other[0:192], other[192:384]), cat, taps, 192, 256)
            term = dot(hs[k], taps[...])
            if k == 0:
                p[...] = term
            else:
                p[...] = p[...] + term
        upsample(p, t, 16, 8, 256)
        out_ref[...] = jnp.zeros_like(out_ref)
        for z in range(2):

            @pl.when(h == z)
            def _():
                for frame in range(2):
                    for r in range(19):
                        y = r + z
                        at = frame * 384 + (y // 2) * 32
                        to = (r + 1 - z) * 16
                        for lane, count in ((0, 128), (128, 64)):
                            row = t[y % 2 * 2 + lane // 128, at : at + 16, 0:count].astype(jnp.bfloat16)
                            lane0 = frame * 192 + lane
                            out_ref[to : to + 16, lane0 : lane0 + count] = row

        wait_all(start_all([(out_ref, out_any)], sems))


def section1(frames, gathered, kernels, ups):
    f32, bf16 = jnp.float32, jnp.bfloat16
    return kernel_call(
        section1_body,
        jax.ShapeDtypeStruct((320, 384), bf16),
        [
            pltpu.VMEM((768, 192), bf16),
            pltpu.VMEM((8, 12, 768), bf16),
            *[pltpu.VMEM((192, 2592), bf16)] * 4,
            *[pltpu.VMEM((384, 432), bf16)] * 4,
            pltpu.VMEM((8, 12, 768), f32),
            pltpu.VMEM((576, 192), f32),
            pltpu.VMEM((768, 192), f32),
            pltpu.VMEM((768, 576), bf16),
            pltpu.VMEM((2, 352, 192), f32),
            pltpu.VMEM((2, 384, 192), bf16),
            pltpu.VMEM((192, 1728), bf16),
            pltpu.VMEM((192, 2304), bf16),
            pltpu.VMEM((384, 2304), f32),
            pltpu.VMEM((4, 768, 128), f32),
            pltpu.VMEM((320, 384), bf16),
        ],
        frames, gathered, *kernels, *ups,
        copies=10,
    )


def pick_body(k_any, u_any, out_any, k, u, out, sems):
    s = lax.axis_index("segment")

    @pl.when(s >= 2)
    def _():
        coming = start_all([(k_any, k), (u_any, u)], sems)
        step = jnp.where(s == 2, 2, 4)
        source = lax.broadcasted_iota(jnp.int32, (96, 192), 1)
        target = lax.broadcasted_iota(jnp.int32, (96, 192), 0)
        picked = ((source == target * step) & (target * step < 192)).astype(jnp.bfloat16)
        wait_all(coming)
        out[:, 0:2592] = dot(picked, k[...]).astype(jnp.bfloat16)
        out[:, 2688:3120] = dot(picked, u[...]).astype(jnp.bfloat16)
        wait_all(start_all([(out, out_any)], sems))


def pick(k, u):
    bf16 = jnp.bfloat16
    return kernel_call(
        pick_body,
        jax.ShapeDtypeStruct((96, 3200), bf16),
        [pltpu.VMEM((192, 2592), bf16), pltpu.VMEM((192, 432), bf16), pltpu.VMEM((96, 3200), bf16)],
        k, u,
        copies=2,
    )


def merge_body(*refs):
    pieces_any, (k2_any, k3_any, up_any) = refs[0:4], refs[4:7]
    pieces = refs[7:11]
    k2, k3, cat, up, sems = refs[11:]
    s, h = lax.axis_index("segment"), lax.axis_index("ha")
    bf16 = jnp.bfloat16

    @pl.when((s >= 2) & (h < 2))
    def _():
        wait_all(start_all(list(zip(pieces_any, pieces)), sems))
        own, nz, nx, nd = pieces
        up[...] = jnp.zeros_like(up)
        for z in range(2):
            for segment, count in ((2, 96), (3, 48)):

                @pl.when((h == z) & (s == segment))
                def _():
                    for part, (a, b) in enumerate(((own, nx), (nz, nd))):
                        at = (part ^ z) * 432
                        cat[0:count, at : at + 432] = a[0:count, 2688:3120]
                        cat[count : 2 * count, at : at + 432] = b[0:count, 2688:3120]
                        if segment == 2:
                            at = (part ^ z) * 2592
                            k2[0:96, at : at + 2592] = a[:, 0:2592]
                            k2[96:192, at : at + 2592] = b[:, 0:2592]
                    if segment == 3:
                        a, b = ((own, nx), (nz, nd))[z]
                        k3[...] = jnp.zeros_like(k3)
                        for tap in range(27):
                            k3[0:48, tap * 128 : tap * 128 + 96] = a[0:48, tap * 96 : tap * 96 + 96]
                            k3[48:96, tap * 128 : tap * 128 + 96] = b[0:48, tap * 96 : tap * 96 + 96]

        for tap in range(9):
            up[:, tap * 128 : tap * 128 + 96] = cat[:, tap * 96 : (tap + 1) * 96]
        wait_all(start_all([(up, up_any), (k2, k2_any), (k3, k3_any)], sems))


def merge(pieces):
    bf16 = jnp.bfloat16
    shapes = ((192, 5184), (96, 3456), (192, 1152))
    return kernel_call(
        merge_body,
        tuple(jax.ShapeDtypeStruct(shape, bf16) for shape in shapes),
        [
            *[pltpu.VMEM((96, 3200), bf16)] * 4,
            pltpu.VMEM((192, 5184), bf16),
            pltpu.VMEM((96, 3456), bf16),
            pltpu.VMEM((192, 864), bf16),
            pltpu.VMEM((192, 1152), bf16),
        ],
        *pieces,
        copies=4,
    )


def caches_body(*refs):
    parts, (c_any, d_any) = refs[0:6], refs[6:8]
    bands, wide, c_full, d_full, c, d, sems = refs[8:]
    s, h, w = (lax.axis_index(axis) for axis in AXES)
    f32, bf16 = jnp.float32, jnp.bfloat16

    @pl.when((s == 2) & (h < 2))
    def _():
        pairs = [(a, bands.at[n // 2, n % 2 * 48 : n % 2 * 48 + 48]) for n, a in enumerate(parts)]
        wait_all(start_all(pairs, sems))
        c_full[...] = jnp.zeros_like(c_full)
        d_full[...] = jnp.zeros_like(d_full)
        for band in range(3):
            wide[...] = bands[band].astype(f32)
            for side in range(2):
                swapped = (w + side) % 2
                for frame in range(2):
                    row = side * 48 + frame * 8
                    for column in range(8):
                        at = (frame * 26 + 1 + band * 8) * 16 + swapped * 8 + column
                        lane = column * 192
                        c_full[0, pl.ds(at, 8, stride=16), :] = wide[row : row + 8, lane : lane + 128]
                        tail = jnp.concatenate([wide[row : row + 8, lane + 128 : lane + 192]] * 2, axis=1)
                        c_full[1, pl.ds(at, 8, stride=16), :] = tail
                    row = side * 48 + 16 + frame * 16
                    for column in range(16):
                        at = (frame * 50 + 1 + band * 16) * 32 + swapped * 16 + column
                        lane = column * 96
                        part = wide[row : row + 16, lane : lane + 96]
                        part = jnp.concatenate([part, part[:, 0:32]], axis=1)
                        d_full[pl.ds(at, 16, stride=32), :] = part
        for frame in range(2):
            at = pl.multiple_of((frame * 26 + h * 6) * 16, 32)
            c[frame * 320 : frame * 320 + 320, 0:128] = c_full[0, pl.ds(at, 320), :].astype(bf16)
            c[frame * 320 : frame * 320 + 320, 128:192] = c_full[1, pl.ds(at, 320), 0:64].astype(bf16)
            at = pl.multiple_of((frame * 50 + h * 15) * 32, 32)
            d[frame * 1120 : frame * 1120 + 1120, :] = d_full[pl.ds(at, 1120), 0:96].astype(bf16)
        wait_all(start_all([(c, c_any), (d, d_any)], sems))


def caches(bands):
    f32, bf16 = jnp.float32, jnp.bfloat16
    return kernel_call(
        caches_body,
        (jax.ShapeDtypeStruct((640, 192), bf16), jax.ShapeDtypeStruct((2240, 96), bf16)),
        [
            pltpu.VMEM((3, 96, 1536), bf16),
            pltpu.VMEM((96, 1536), f32),
            pltpu.VMEM((2, 832, 128), f32),
            pltpu.VMEM((3200, 128), f32),
            pltpu.VMEM((640, 192), bf16),
            pltpu.VMEM((2240, 96), bf16),
        ],
        *bands,
        copies=6,
    )


def sections23_body(same2, same3, other2, other3, c_own, c_sent, d_any, k2_own, k2_sent, k3_own, k3_sent, u_own, u_sent,
                    out0, out1, out2, out3, pairs, d_ref, k2, k3, u2, u3, line, base, xx, hs, p, t, base3, xx3, hs3, p3, t3, rows3, out_ref,
                    sems):
    s, h, w = (lax.axis_index(axis) for axis in AXES)
    f32, bf16 = jnp.float32, jnp.bfloat16

    @pl.when((s >= 2) & (h < 2))
    def _():
        frame = (s - 2) * 2 + w
        line[0:640] = jnp.zeros((640, 192), bf16)
        for segment, same, other in ((2, same2, other2), (3, same3, other3)):

            @pl.when(s == segment)
            def _():
                c_any = c_own if segment == 2 else c_sent
                held2, held3 = (k2_own, k3_sent) if segment == 2 else (k2_sent, k3_own)
                up2, up3 = (u_own, u_sent) if segment == 2 else (u_sent, u_own)
                start_all(
                    [
                        (same, pairs.at[w]),
                        (other, pairs.at[1 - w]),
                        (c_any, line.at[640:1280]),
                        (held2, k2),
                        (up2, u2),
                        (d_any, d_ref),
                        (held3, k3),
                        (up3.at[0:96], u3),
                    ],
                    sems,
                )

        coming = [
            pltpu.make_async_copy(a, b, sems.at[n])
            for n, (a, b) in enumerate(
                [
                    (same2, pairs.at[0]),
                    (other2, pairs.at[1]),
                    (c_own, line.at[640:1280]),
                    (k2_own, k2),
                    (u_own, u2),
                    (d_any, d_ref),
                    (k3_own, k3),
                    (u_own.at[0:96], u3),
                ]
            )
        ]
        wait_all(coming[0:3])
        for number in range(2):
            for k in range(2):
                at = 1280 + (2 * number + k) * 320
                line[at : at + 320] = pairs[number, :, k * 192 : (k + 1) * 192]

        base[...] = line[pl.ds(pl.multiple_of(frame * 320, 320), 1600), :].astype(f32)
        for dx, moved in enumerate(shifts(base[...], 16, 16)):
            xx[:, dx * 192 : (dx + 1) * 192] = moved.astype(bf16)
        coming[3].wait()
        total = None
        for group in range(9):
            start = group // 3 * 320 + group % 3 * 16
            term = dot_t(xx[start : start + 928, :], k2[:, group * 576 : (group + 1) * 576])
            total = term if total is None else total + term
        inverse = lax.rsqrt(jnp.sum(total * total, axis=1, keepdims=True) / 192.0 + EPSILON)
        keep = index_of((928, 192)) % 320 < 288
        hs[0:928] = jnp.where(keep, silu(total * inverse), 0.0).astype(bf16)
        hs[928:960] = jnp.zeros((32, 192), bf16)
        coming[4].wait()
        p[...] = dot(hs[...], u2[...])
        upsample(p, t, 16, 16, 128)

        for z in range(2):

            @pl.when(h == z)
            def _():
                blank = 0 if z == 0 else 34
                for moment in range(3):
                    to = moment * 1120 + blank * 32
                    base3[to : to + 32] = jnp.zeros((32, 96), f32)
                    for r in range(34):
                        y = r + 2 * z
                        at = moment * 640 + (y // 2) * 32
                        to = moment * 1120 + (r + 1 - z) * 32
                        base3[to : to + 32] = t[y % 2, at : at + 32, 0:96].astype(bf16).astype(f32)

        wait_all(coming[5:8])

        @pl.when(frame == 0)
        def _():
            base3[0:2240] = d_ref[...].astype(f32)

        @pl.when(frame == 1)
        def _():
            base3[0:1120] = d_ref[1120:2240].astype(f32)

        xx3[...] = jnp.zeros_like(xx3)
        for dx, moved in enumerate(shifts(base3[...], 32, 32)):
            xx3[:, dx * 128 : dx * 128 + 96] = moved.astype(bf16)
        total = None
        for group in range(9):
            start = group // 3 * 1120 + group % 3 * 32
            term = dot_t(xx3[start : start + 1056, :], k3[:, group * 384 : (group + 1) * 384])
            total = term if total is None else total + term
        inverse = lax.rsqrt(jnp.sum(total * total, axis=1, keepdims=True) / 96.0 + EPSILON)
        hs3[0:1056] = silu(total * inverse).astype(bf16)
        hs3[1056:1120] = jnp.zeros((64, 96), bf16)
        p3[...] = dot(hs3[...], u3[...])
        upsample(p3, t3, 32, 32, 128)
        for z in range(2):

            @pl.when(h == z)
            def _():
                for a in range(2):
                    for four in range(16):
                        parts = [
                            t3[a, pl.ds(z * 64 + four * 4 + n, 32, stride=64), :][:, 0:96] for n in range(4)
                        ]
                        row = jnp.concatenate(parts, axis=1)
                        for n in range(3):
                            rows3[four * 3 + n, pl.ds(a, 32, stride=2), :] = row[:, n * 128 : (n + 1) * 128]
        for tile in range(48):
            lane = tile % 24 * 128
            for n in range(2):
                part = rows3[tile, n * 32 : n * 32 + 32, :].astype(bf16)
                out_ref[n * 2 + tile // 24, :, lane : lane + 128] = part

        wait_all(start_all([(out_ref.at[n], target) for n, target in enumerate((out0, out1, out2, out3))], sems))


def sections23(received, c, c_sent, d, kernels):
    f32, bf16 = jnp.float32, jnp.bfloat16
    return kernel_call(
        sections23_body,
        tuple([jax.ShapeDtypeStruct((32, 3072), bf16)] * 4),
        [
            pltpu.VMEM((2, 320, 384), bf16),
            pltpu.VMEM((2240, 96), bf16),
            pltpu.VMEM((192, 5184), bf16),
            pltpu.VMEM((96, 3456), bf16),
            pltpu.VMEM((192, 1152), bf16),
            pltpu.VMEM((96, 1152), bf16),
            pltpu.VMEM((2560, 192), bf16),
            pltpu.VMEM((1600, 192), f32),
            pltpu.VMEM((1600, 576), bf16),
            pltpu.VMEM((960, 192), bf16),
            pltpu.VMEM((960, 1152), f32),
            pltpu.VMEM((2, 1920, 128), f32),
            pltpu.VMEM((3360, 96), f32),
            pltpu.VMEM((3360, 384), bf16),
            pltpu.VMEM((1120, 96), bf16),
            pltpu.VMEM((1120, 1152), f32),
            pltpu.VMEM((2, 2240, 128), f32),
            pltpu.VMEM((48, 64, 128), f32),
            pltpu.VMEM((4, 32, 3072), bf16),
        ],
        *received, c, c_sent, d, *kernels,
        copies=8,
    )


def blank_body(*refs):
    pass


def blank(some, shapes):
    return kernel_call(blank_body, [jax.ShapeDtypeStruct(shape, jnp.bfloat16) for shape in shapes], [], some, copies=1)


LATER = ((192, 5184), (96, 3456), (192, 1152), (192, 5184), (96, 3456), (192, 1152), (640, 192), (640, 192), (2240, 96))


def sections01(latent, cache_a, cache_b, cache_c, cache_d, k, u):
    u_far = send(u, [((s_, h_ + 2, w_), (s_, h_, w_)) for s_ in (0, 1) for h_ in range(2) for w_ in range(2)])
    k_x, k_z = send(k, square((1,), 0, 1)), send(k, square((1,), 1, 0))
    gathered = lax.all_to_all(
        spread_tiles(latent, cache_a, cache_b), ("ha", "wa"), split_axis=0, concat_axis=0, tiled=True
    )
    ups = jnp.concatenate([u, u_far], axis=0)
    gathered, ups = lax.optimization_barrier((gathered, ups))
    u_z, u_x, u_d = (send(ups, square((0, 1), dh, dw)) for dh, dw in ((1, 0), (0, 1), (1, 1)))
    partial_sums = conv0(gathered, k)
    partial_sums, k_x, k_z = lax.optimization_barrier((partial_sums, k_x, k_z))
    far_sums = send(partial_sums, [((0, h_ + 2, w_), (0, h_, w_)) for h_ in range(2) for w_ in range(2)])
    k_d = send(k_z, square((1,), 0, 1))
    sums = fold(partial_sums, far_sums)
    sums = [sums] + [send(sums, square((0,), dh, dw)) for dh, dw in ((1, 0), (0, 1), (1, 1))]
    risen = up0(sums, (ups, u_z, u_x, u_d))
    given = send(risen, [((0, h_, w_), (1, h_, w_)) for h_ in range(2) for w_ in range(2)])
    out1 = section1(given, gathered, (k, k_z, k_x, k_d), (ups, u_z, u_x, u_d))
    return (out1, *blank(k, LATER))


def before_sections23(latent, cache_a, cache_b, cache_c, cache_d, k, u):
    own = jnp.concatenate([cache_c.reshape(16, 1536), cache_d.reshape(32, 1536)], axis=0)
    bands = [own] + [
        send(own, [((2, h_ + n, w_ ^ dw), (2, h_, w_)) for h_ in range(2) for w_ in range(2)])
        for n in range(3)
        for dw in range(2)
        if n + dw
    ]
    picked = pick(k, u)
    picked_x, picked_z = send(picked, square((2, 3), 0, 1)), send(picked, square((2, 3), 1, 0))
    picked_d = send(picked_z, square((2, 3), 0, 1))
    k2, k3, u23 = merge((picked, picked_z, picked_x, picked_d))
    pairs = [((s_, h_, w_), (s_ ^ 1, h_, w_)) for s_ in (2, 3) for h_ in range(2) for w_ in range(2)]
    rise, fall = [pair for pair in pairs if pair[0][0] == 2], [pair for pair in pairs if pair[0][0] == 3]
    c, d = caches(bands)
    c_sent, k2_sent, k3_sent, u_sent = send(c, rise), send(k2, rise), send(k3, fall), send(u23, pairs)
    return (*blank(k, ((320, 384),)), k2, k3, u23, k2_sent, k3_sent, u_sent, c, c_sent, d)


def relay(latent, cache_a, cache_b, cache_c, cache_d, conv_pack, up_pack):
    s, h, w = (lax.axis_index(axis) for axis in AXES)
    k, u = conv_pack[0].T, up_pack[0]
    out1, k2, k3, u23, k2_sent, k3_sent, u_sent, c, c_sent, d = lax.cond(
        s < 2, sections01, before_sections23, latent, cache_a, cache_b, cache_c, cache_d, k, u
    )
    received = [
        send(out1, [((1, h_, w_), (s_, h_, w_ ^ dw)) for h_ in range(2) for w_ in range(2)])
        for dw in range(2)
        for s_ in (2, 3)
    ]
    blocks = sections23(received, c, c_sent, d, (k2, k2_sent, k3, k3_sent, u23, u_sent))

    arrived = [
        send(
            blocks[2 * n + half],
            [((2 + c_, z, x), (2 * c_ + x, 2 * z + n, half)) for c_ in range(2) for z in range(2) for x in range(2)],
        )
        for n in range(2)
        for half in range(2)
    ]
    lower_half = jnp.where(w == 0, arrived[2], arrived[3])
    upper_half = jnp.where(w == 0, arrived[0], arrived[1])
    return jnp.where(h % 2 == 0, upper_half, lower_half)[None]


def solution(mesh):
    in_specs = (
        P(None, "ha", "wa"),
        P(None, "ha", "wa"),
        P(None, "ha", "wa"),
        P(None, "ha", "wa"),
        P(None, "ha", "wa"),
        P("segment", "ha", "wa"),
        P("segment", "wa", "ha"),
    )
    out_specs = P("segment", "ha", "wa")
    sizes = tuple(mesh.shape[axis] for axis in AXES)
    program = relay if sizes == (4, 4, 2) else per_device
    return jax.shard_map(
        program, mesh=mesh, in_specs=in_specs, out_specs=out_specs, check_vma=False
    )
```

```python
from functools import partial

import jax
import jax.numpy as jnp
from jax import lax
from jax.experimental import pallas as pl
from jax.experimental.pallas import tpu as pltpu
from jax.sharding import PartitionSpec as P

WIDE = 384
MID = 192
NARROW = 96


EPSILON = 1e-06


def shortened(array):

    def short(part):
        return part.astype(jnp.bfloat16) if part.dtype == jnp.float32 else part

    return jax.tree.map(short, array)


def passed_along(value, axis, steps):
    count = lax.axis_size(axis)
    initial, last = (max(0, -steps), min(count, count - steps))
    return lax.ppermute(value, axis, [(source, source + steps) for source in range(initial, last)])


def layer_table():
    return ((WIDE, WIDE, MID), (MID, WIDE, MID), (MID, MID, NARROW), (NARROW, NARROW, NARROW))


def round_up(amount):
    return -(-amount // 128) * 128


def volume(target):
    amount = 1
    for extent in target:
        amount = amount * extent
    return amount


def flat_pad(tensor, length):
    leading = tensor.shape[0]
    packed = tensor.reshape(leading, -1)
    return jnp.pad(packed, ((0, 0), (0, length - packed.shape[1])))


def reshaped(packed, target):
    return packed[:, : volume(target)].reshape((packed.shape[0],) + tuple(target))


def add_rows(tensor, from_above, from_below):
    leading, height, width, channels = tensor.shape
    upper = reshaped(from_above, (1, width, channels))
    lower = reshaped(from_below, (1, width, channels))
    return jnp.concatenate([upper, tensor, lower], axis=1)


def add_cols(tensor, from_left, from_right):
    leading, height, width, channels = tensor.shape
    before = reshaped(from_left, (height, 1, channels))
    after = reshaped(from_right, (height, 1, channels))
    return jnp.concatenate([before, tensor, after], axis=2)


def trade_rows(upper_rim, bottom):
    return (
        jax.tree.map(
            lambda part, own: part.astype(own.dtype),
            passed_along(shortened(bottom), "ha", 1),
            bottom,
        ),
        jax.tree.map(
            lambda part, own: part.astype(own.dtype),
            passed_along(shortened(upper_rim), "ha", -1),
            upper_rim,
        ),
    )


def trade_cols(left_rim, right_rim):
    return (
        jax.tree.map(
            lambda part, own: part.astype(own.dtype),
            passed_along(shortened(right_rim), "wa", 1),
            right_rim,
        ),
        jax.tree.map(
            lambda part, own: part.astype(own.dtype),
            passed_along(shortened(left_rim), "wa", -1),
            left_rim,
        ),
    )


def causal_conv(stacked, kernel):
    result = lax.conv_general_dilated(
        stacked[None],
        kernel,
        (1, 1, 1),
        "VALID",
        dimension_numbers=("NDHWC", "DHWIO", "NDHWC"),
        preferred_element_type=jnp.float32,
    )
    return result[0, 0]


def activate(conv_sum):
    inverse = lax.rsqrt(jnp.mean(conv_sum * conv_sum, axis=-1, keepdims=True) + EPSILON)
    return jax.nn.silu(conv_sum * inverse).astype(jnp.bfloat16)


def upsample_conv(hidden_ext, kernel):
    expanded = jnp.repeat(jnp.repeat(hidden_ext, 2, axis=0), 2, axis=1)[1:-1, 1:-1]
    result = lax.conv_general_dilated(
        expanded[None],
        kernel,
        (1, 1),
        "VALID",
        dimension_numbers=("NHWC", "HWIO", "NHWC"),
        preferred_element_type=jnp.float32,
    )
    return result[0].astype(jnp.bfloat16)


def per_device(latent, cache_a, cache_b, cache_c, cache_d, conv_pack, up_pack):
    frames = latent.shape[0]
    tile_rows = latent.shape[1]
    tile_cols = latent.shape[2] // WIDE
    layers = layer_table()
    section = lax.axis_index("segment")
    segments = lax.axis_size("segment")
    final_segment = segments - 1
    input_shapes = [
        (tile_rows << level, tile_cols << level, layers[level][0]) for level in range(4)
    ]
    mid_shapes = [(tile_rows << level, tile_cols << level, layers[level][1]) for level in range(4)]
    out_shapes = [
        (tile_rows << level + 1, tile_cols << level + 1, layers[level][2]) for level in range(4)
    ]
    ext_shapes = [(target[0] + 2, target[1] + 2, target[2]) for target in input_shapes]
    all_shapes = input_shapes + mid_shapes
    row_length = round_up(max((target[1] * target[2] for target in all_shapes)))
    column_length = round_up(max(((target[0] + 2) * target[2] for target in all_shapes)))
    size_input = round_up(max((volume(target) for target in input_shapes)))
    size_middle = round_up(max((volume(target) for target in mid_shapes)))
    size_extended = round_up(max((volume(target) for target in ext_shapes)))
    size_output = round_up(max((volume(target) for target in out_shapes)))
    final_shape = out_shapes[3]
    final_count = volume(final_shape)
    conv_rows, up_rows = (
        lax.all_gather(conv_pack, "ha", axis=1, tiled=True),
        lax.all_gather(up_pack, "ha", axis=2, tiled=True),
    )
    conv_all, up_all = (
        lax.all_gather(conv_rows, "wa", axis=2, tiled=True),
        lax.all_gather(up_rows, "wa", axis=1, tiled=True),
    )

    def conv_kernel(level):
        width_in, width_mid, width_out = layers[level]
        columns = conv_all[0, : 27 * width_in, :: WIDE // width_mid]
        return columns.reshape(3, 3, 3, width_in, columns.shape[1])

    def up_kernel(level):
        width_in, width_mid, width_out = layers[level]
        rows_used = up_all[0, :: WIDE // width_mid, : 9 * width_out]
        return rows_used.reshape(width_mid, 3, 3, width_out).transpose(1, 2, 0, 3)

    conv_kernels = [conv_kernel(level) for level in range(4)]
    up_kernels = [up_kernel(level) for level in range(4)]

    def row_rims(packed, shapes):

        def rows_branch(level, packed):
            tensor = reshaped(packed, shapes[level])
            return (flat_pad(tensor[:, :1], row_length), flat_pad(tensor[:, -1:], row_length))

        upper_rim, bottom = lax.switch(
            section, [partial(rows_branch, level) for level in range(4)], packed
        )
        return trade_rows(upper_rim, bottom)

    def extend(packed, shapes):
        from_above, from_below = row_rims(packed, shapes)

        def cols_branch(level, packed, from_above, from_below):
            tensor = add_rows(reshaped(packed, shapes[level]), from_above, from_below)
            return (
                flat_pad(tensor[:, :, :1], column_length),
                flat_pad(tensor[:, :, -1:], column_length),
            )

        left_rim, right_rim = lax.switch(
            section,
            [partial(cols_branch, level) for level in range(4)],
            packed,
            from_above,
            from_below,
        )
        from_left, from_right = trade_cols(left_rim, right_rim)
        return (from_above, from_below, from_left, from_right)

    def assemble(packed, target, rims):
        tensor = add_rows(reshaped(packed, target), rims[0], rims[1])
        return add_cols(tensor, rims[2], rims[3])

    caches = (cache_a, cache_b, cache_c, cache_d)

    def cache_branch(level):
        return flat_pad(caches[level], size_input)

    cached = lax.switch(section, [partial(cache_branch, level) for level in range(4)])
    cache_rims = extend(cached, input_shapes)

    def store_branch(level, packed, rims):
        return flat_pad(assemble(packed, input_shapes[level], rims), size_extended)

    history = lax.switch(
        section, [partial(store_branch, level) for level in range(4)], cached, cache_rims
    )
    finished = jnp.zeros((frames, final_shape[0], final_shape[1] * final_shape[2]), jnp.bfloat16)
    stream = jnp.zeros((1, size_input), jnp.bfloat16)
    for moment in range(frames + segments - 1):
        if moment == 0:
            incoming = stream
        else:
            incoming = jax.tree.map(
                lambda part, own: part.astype(own.dtype),
                passed_along(shortened(stream), "segment", 1),
                stream,
            )
        frame_id = moment - section
        active = (frame_id >= 0) & (frame_id < frames)
        chosen = jnp.clip(frame_id, 0, frames - 1)
        picked = lax.dynamic_index_in_dim(latent, chosen, 0, keepdims=True)
        current = jnp.where(section == 0, flat_pad(picked, size_input), incoming)
        branch_id = jnp.where(active, section, 4)
        rims = extend(current, input_shapes)

        def conv_branch(level, current, history, rims):
            window = assemble(current, input_shapes[level], rims)
            earlier = reshaped(history, ext_shapes[level])
            hidden = activate(
                causal_conv(jnp.concatenate([earlier, window], axis=0), conv_kernels[level])
            )
            return (flat_pad(hidden[None], size_middle), flat_pad(window, size_extended))

        def spare_conv(current, history, rims):
            return (
                jnp.zeros((1, size_middle), jnp.bfloat16),
                jnp.zeros((1, size_extended), jnp.bfloat16),
            )

        hidden, window = lax.switch(
            branch_id,
            [partial(conv_branch, level) for level in range(4)] + [spare_conv],
            current,
            history,
            rims,
        )
        hidden_rims = extend(hidden, mid_shapes)

        def up_branch(level, hidden, hidden_rims):
            expanded = assemble(hidden, mid_shapes[level], hidden_rims)[0]
            return flat_pad(upsample_conv(expanded, up_kernels[level])[None], size_output)

        def spare_up(hidden, hidden_rims):
            return jnp.zeros((1, size_output), jnp.bfloat16)

        produced = lax.switch(
            branch_id,
            [partial(up_branch, level) for level in range(4)] + [spare_up],
            hidden,
            hidden_rims,
        )
        shifted = jnp.concatenate([history[1:], window], axis=0)
        history = jnp.where(active, shifted, history)
        stream = produced[:, :size_input]
        if moment >= final_segment:
            finished_id = moment - final_segment
            picture = produced[:, :final_count].reshape(
                1, final_shape[0], final_shape[1] * final_shape[2]
            )
            finished = finished.at[finished_id].set(picture[0])
    collected = lax.all_to_all(finished, "segment", split_axis=0, concat_axis=0, tiled=True)
    per_segment = frames // segments
    own_frame = collected[final_segment * per_segment : (final_segment + 1) * per_segment]
    return own_frame


AXES = ("segment", "ha", "wa")
MIB = 1024 * 1024


def place(s, h, w):
    return (s * 4 + h) * 2 + w


def send(value, pairs):
    return lax.ppermute(value, AXES, [(place(*a), place(*b)) for a, b in pairs])


def square(segments, dh, dw):
    return [
        ((s, h, w), (s, h ^ dh, w ^ dw)) for s in segments for h in range(2) for w in range(2)
    ]


def kernel_call(body, out_shape, scratch, *args, copies=0, vmem=16, cost=1000, place=pl.ANY):
    return pl.pallas_call(
        body,
        out_shape=out_shape,
        in_specs=[pl.BlockSpec(memory_space=place)] * len(args),
        out_specs=jax.tree.map(lambda _: pl.BlockSpec(memory_space=pl.ANY), out_shape),
        scratch_shapes=scratch + [pltpu.SemaphoreType.DMA((copies,))],
        compiler_params=pltpu.CompilerParams(vmem_limit_bytes=vmem * MIB),
        cost_estimate=pl.CostEstimate(flops=1000 * cost, bytes_accessed=1000, transcendentals=0),
    )(*args)


def start_all(pairs, sems, first=0):
    copies = [pltpu.make_async_copy(a, b, sems.at[first + n]) for n, (a, b) in enumerate(pairs)]
    for copy in copies:
        copy.start()
    return copies


def wait_all(copies):
    for copy in copies:
        copy.wait()


def dot(a, b):
    return jnp.dot(a, b, preferred_element_type=jnp.float32)


def dot_t(a, b):
    return lax.dot_general(a, b, (((1,), (1,)), ((), ())), preferred_element_type=jnp.float32)


def index_of(shape):
    return lax.broadcasted_iota(jnp.int32, shape, 0)


def silu(v):
    return v / (1.0 + jnp.exp(-v))


def shifts(base, pitch, width):
    n = base.shape[0]
    left, right = pltpu.roll(base, 1, 0), pltpu.roll(base, n - 1, 0)
    if pitch == width:
        column = index_of(base.shape) % pitch
        left = jnp.where(column == 0, 0.0, left)
        right = jnp.where(column == width - 1, 0.0, right)
    return left, base, right


def upsample(p_ref, t_ref, pitch, width, lanes):
    n = p_ref.shape[0]
    blocks = lanes // 128
    column = index_of((n, 128)) % pitch
    for block in range(blocks):

        def tap(dy, dx):
            at = (dy * 3 + dx) * lanes + block * 128
            return p_ref[:, at : at + 128]

        for b in range(2):
            rows = []
            for dy in range(3):
                middle = tap(dy, 1)
                if b == 0:
                    far = pltpu.roll(tap(dy, 0), 1, 0)
                    if pitch == width:
                        far = jnp.where(column == 0, 0.0, far)
                    rows.append(far + middle + tap(dy, 2))
                else:
                    far = pltpu.roll(tap(dy, 2), n - 1, 0)
                    if pitch == width:
                        far = jnp.where(column == width - 1, 0.0, far)
                    rows.append(tap(dy, 0) + middle + far)
            t_ref[block, pl.ds(b, n, stride=2), :] = pltpu.roll(rows[0], pitch, 0) + rows[1] + rows[2]
            t_ref[blocks + block, pl.ds(b, n, stride=2), :] = (
                rows[0] + rows[1] + pltpu.roll(rows[2], n - pitch, 0)
            )


def tiles_body(latent_any, a_any, b_any, out_any, latent, a, b, rows, out, sems):
    wait_all(start_all([(latent_any, latent), (a_any, a), (b_any, b)], sems))

    @pl.when(lax.axis_index("segment") == 0)
    def _():
        for frame in range(4):
            rows[frame * 2 : frame * 2 + 2] = latent[frame].astype(jnp.float32)
        for frame in range(2):
            rows[8 + frame * 2 : 10 + frame * 2] = a[frame].astype(jnp.float32)

    @pl.when(lax.axis_index("segment") > 0)
    def _():
        for frame in range(2):
            rows[frame * 4 : frame * 4 + 4] = b[frame].astype(jnp.float32)
        rows[8:12] = jnp.zeros((4, 768), jnp.float32)

    out[...] = rows[...].astype(jnp.bfloat16)
    wait_all(start_all([(out, out_any.at[n]) for n in range(8)], sems))


def spread_tiles(latent, cache_a, cache_b):
    bf16 = jnp.bfloat16
    return kernel_call(
        tiles_body,
        jax.ShapeDtypeStruct((8, 12, 768), bf16),
        [
            pltpu.VMEM((4, 2, 768), bf16),
            pltpu.VMEM((2, 2, 768), bf16),
            pltpu.VMEM((2, 4, 768), bf16),
            pltpu.VMEM((12, 768), jnp.float32),
            pltpu.VMEM((12, 768), bf16),
        ],
        latent, cache_a, cache_b,
        copies=8,
    )


def conv0_body(g_any, k_any, out_any, g_ref, k_ref, gf, base, xx, acc, buf, out_ref, sems):
    s, h = lax.axis_index("segment"), lax.axis_index("ha")

    @pl.when(s == 0)
    def _():
        coming = start_all([(g_any, g_ref), (k_any, k_ref)], sems)
        base[...] = jnp.zeros_like(base)
        coming[0].wait()
        gf[...] = g_ref[...].astype(jnp.float32)
        for frame in range(6):
            for hh in range(4):
                for ww in range(2):
                    for r in range(2):
                        row = 8 + frame * 2 + r if frame < 2 else (frame - 2) * 2 + r
                        for c in range(2):
                            at = frame * 160 + (1 + 2 * hh + r) * 16 + 2 * ww + c
                            base[at : at + 1, :] = gf[hh * 2 + ww, row : row + 1, c * 384 : (c + 1) * 384]
        for dx, moved in enumerate(shifts(base[...], 16, 4)):
            xx[dx] = moved.astype(jnp.bfloat16)
        coming[1].wait()
        for part in range(4):

            @pl.when(h == part)
            def _():
                total = None
                at, end = part * 2592, part * 2592 + 2592
                while at < end:
                    tap, c0 = divmod(at, 384)
                    c1 = min(384, c0 + end - at)
                    dt, dy, dx = tap // 9, tap // 3 % 3, tap % 3
                    start = dt * 160 + dy * 16
                    k0 = at - part * 2592
                    term = dot_t(xx[dx, start : start + 608, c0:c1], k_ref[:, k0 : k0 + c1 - c0])
                    total = term if total is None else total + term
                    at += c1 - c0
                acc[...] = total

        for frame in range(4):
            for r in range(8):
                to, at = (frame * 8 + r) * 4, frame * 160 + r * 16
                buf[to : to + 4, :] = acc[at : at + 4, :]
        out_ref[0:128, :] = buf[:, 0:128].astype(jnp.bfloat16)
        tail = jnp.concatenate([buf[0:64, 128:192], buf[64:128, 128:192]], axis=1)
        out_ref[128:192, :] = tail.astype(jnp.bfloat16)
        wait_all(start_all([(out_ref, out_any.at[n]) for n in range(8)], sems))


def conv0(gathered, k):
    f32, bf16 = jnp.float32, jnp.bfloat16
    return kernel_call(
        conv0_body,
        jax.ShapeDtypeStruct((8, 192, 128), bf16),
        [
            pltpu.VMEM((8, 12, 768), bf16),
            pltpu.VMEM((192, 2592), bf16),
            pltpu.VMEM((8, 12, 768), f32),
            pltpu.VMEM((960, 384), f32),
            pltpu.VMEM((3, 960, 384), bf16),
            pltpu.VMEM((608, 192), f32),
            pltpu.VMEM((128, 192), f32),
            pltpu.VMEM((192, 128), bf16),
        ],
        gathered, k,
        copies=8,
        cost=20 * 10**6,
    )


def join_body(own, nz, nx, nd, mine_any, other_any, cat, taps, sems):
    s, h = lax.axis_index("segment"), lax.axis_index("ha")

    @pl.when((s < 2) & (h < 2))
    def _():
        sending = []
        for half, (near, far, target) in enumerate(((own, nz, mine_any), (nx, nd, other_any))):
            for z in range(2):

                @pl.when(h == z)
                def _():
                    for first, pieces in ((z, near), (1 - z, far)):
                        for n in range(2):
                            at = (first + 2 * n) * 432
                            cat[:, at : at + 432] = pieces[:, n * 432 : (n + 1) * 432]

            for tap in range(9):
                taps[half, :, tap * 256 : tap * 256 + 192] = cat[:, tap * 192 : (tap + 1) * 192]
                taps[half, :, tap * 256 + 192 : (tap + 1) * 256] = jnp.zeros((192, 64), jnp.bfloat16)
            sending += start_all([(taps.at[half], target)], sems, half)
        wait_all(sending)


def join(pieces):
    bf16 = jnp.bfloat16
    return kernel_call(
        join_body,
        (jax.ShapeDtypeStruct((192, 2304), bf16), jax.ShapeDtypeStruct((192, 2304), bf16)),
        [pltpu.VMEM((192, 1728), bf16), pltpu.VMEM((2, 192, 2304), bf16)],
        *pieces,
        copies=2,
        vmem=8,
        cost=20 * 10**6,
        place=pltpu.VMEM,
    )


def up0_body(*refs):
    y_any, taps_any, out_any = refs[0], refs[1:3], refs[3]
    y, taps, hbuf, hs, p, t, out_ref, sems = refs[4:]
    s, h, w = (lax.axis_index(axis) for axis in AXES)

    @pl.when((s == 0) & (h < 2))
    def _():
        coming = start_all([(y_any, y)], sems)
        rising = start_all([(a, taps.at[n]) for n, a in enumerate(taps_any)], sems, 1)
        wait_all(coming)
        halves = []
        for side in range(2):
            total = y[side].astype(jnp.float32)
            for hh in range(1, 4):
                total = total + y[hh * 2 + side].astype(jnp.float32)
            tail = jnp.concatenate([total[128:192, 0:64], total[128:192, 64:128]], axis=0)
            halves.append(jnp.concatenate([total[0:128], tail], axis=1))
        squares = sum(jnp.sum(half * half, axis=1, keepdims=True) for half in halves)
        inverse = lax.rsqrt(squares / 384.0 + EPSILON)
        active = [silu(half * inverse) for half in halves]
        hs[...] = jnp.zeros_like(hs)
        for k in range(2):
            hbuf[...] = jnp.where(w == k, active[0], active[1])
            for frame in range(4):
                for r in range(8):
                    to, at = frame * 72 + r * 8, (frame * 8 + r) * 4
                    hs[k, to : to + 4, :] = hbuf[at : at + 4, :]
        wait_all(rising)
        p[...] = dot(hs[0].astype(jnp.bfloat16), taps[0]) + dot(hs[1].astype(jnp.bfloat16), taps[1])
        upsample(p, t, 8, 4, 256)
        column = index_of((16, 192))
        out_ref[...] = jnp.zeros_like(out_ref)
        for z in range(2):

            @pl.when(h == z)
            def _():
                for frame in range(4):
                    for r in range(11):
                        y = r + 5 * z
                        at = frame * 144 + (y // 2) * 16
                        to = frame * 192 + (r + 1 - z) * 16
                        for lane, count in ((0, 128), (128, 64)):
                            row = t[y % 2 * 2 + lane // 128, at : at + 16, 0:count]
                            row = jnp.where(column[:, 0:count] < 8, row, 0.0)
                            out_ref[to : to + 16, lane : lane + count] = row.astype(jnp.bfloat16)

        wait_all(start_all([(out_ref, out_any)], sems))


def up0(partials, ups):
    f32, bf16 = jnp.float32, jnp.bfloat16
    return kernel_call(
        up0_body,
        jax.ShapeDtypeStruct((768, 192), bf16),
        [
            pltpu.VMEM((8, 192, 128), bf16),
            pltpu.VMEM((2, 192, 2304), bf16),
            pltpu.VMEM((128, 192), f32),
            pltpu.VMEM((2, 288, 192), f32),
            pltpu.VMEM((288, 2304), f32),
            pltpu.VMEM((4, 576, 128), f32),
            pltpu.VMEM((768, 192), bf16),
        ],
        partials, *ups,
        copies=3,
    )


def group_rows(first, second, group):
    at, end = group * 576, group * 576 + 576
    if end <= 2592:
        return first[:, at:end]
    if at >= 2592:
        return second[:, at - 2592 : end - 2592]
    return jnp.concatenate([first[:, at:2592], second[:, 0 : end - 2592]], axis=1)


def section1_body(x_any, g_any, *refs):
    kernels_any, taps_any, out_any = refs[0:4], refs[4:6], refs[6]
    x_ref, g_ref = refs[7:9]
    k_own, k_z, k_x, k_d = refs[9:13]
    gf, full, base, xx, acc, hs, taps, p, t, out_ref, sems = refs[13:]
    s, h, w = (lax.axis_index(axis) for axis in AXES)

    @pl.when((s == 1) & (h < 2))
    def _():
        coming = start_all([(x_any, x_ref), (g_any, g_ref)], sems)
        arriving = start_all(list(zip(kernels_any, (k_own, k_z, k_x, k_d))), sems, 2)
        rising = start_all([(a, taps.at[n]) for n, a in enumerate(taps_any)], sems, 6)
        wait_all(coming)

        @pl.when(w == 0)
        def _():
            gf[...] = g_ref[...].astype(jnp.float32)
            full[...] = jnp.zeros_like(full)
            for frame in range(2):
                for hh in range(4):
                    for ww in range(2):
                        for r in range(4):
                            for c in range(4):
                                row = frame * 4 + r
                                at = frame * 288 + (1 + hh * 4 + r) * 16 + ww * 4 + c
                                full[at : at + 1, :] = gf[hh * 2 + ww, row : row + 1, c * 192 : (c + 1) * 192]
            for frame in range(2):
                start = pl.multiple_of(frame * 288 + h * 96, 32)
                base[frame * 192 : (frame + 1) * 192] = full[pl.ds(start, 192), :]
            base[384:768] = x_ref[0:384].astype(jnp.float32)

        @pl.when(w == 1)
        def _():
            base[...] = x_ref[...].astype(jnp.float32)

        for dx, moved in enumerate(shifts(base[...], 16, 8)):
            xx[:, dx * 192 : (dx + 1) * 192] = moved.astype(jnp.bfloat16)
        wait_all(arriving)
        for z in range(2):

            @pl.when(h == z)
            def _():
                for k, (mine, other) in enumerate(((k_own, k_z), (k_x, k_d))):
                    first, second = (mine, other) if z == 0 else (other, mine)
                    total = None
                    for group in range(9):
                        start = group // 3 * 192 + group % 3 * 16
                        term = dot_t(xx[start : start + 352, :], group_rows(first, second, group))
                        total = term if total is None else total + term
                    acc[k] = total

        squares = sum(jnp.sum(acc[k] * acc[k], axis=1, keepdims=True) for k in range(2))
        inverse = lax.rsqrt(squares / 384.0 + EPSILON)
        index = index_of((352, 192))
        keep = (index % 192 < 160) & (index % 16 < 8)
        for k in range(2):
            hs[k, 0:352] = jnp.where(keep, silu(acc[k] * inverse), 0.0).astype(jnp.bfloat16)
            hs[k, 352:384] = jnp.zeros((32, 192), jnp.bfloat16)
        wait_all(rising)
        p[...] = dot(hs[0], taps[0]) + dot(hs[1], taps[1])
        upsample(p, t, 16, 8, 256)
        out_ref[...] = jnp.zeros_like(out_ref)
        for z in range(2):

            @pl.when(h == z)
            def _():
                for frame in range(2):
                    for r in range(19):
                        y = r + z
                        at = frame * 384 + (y // 2) * 32
                        to = (r + 1 - z) * 16
                        for lane, count in ((0, 128), (128, 64)):
                            row = t[y % 2 * 2 + lane // 128, at : at + 16, 0:count].astype(jnp.bfloat16)
                            lane0 = frame * 192 + lane
                            out_ref[to : to + 16, lane0 : lane0 + count] = row

        wait_all(start_all([(out_ref, out_any)], sems))


def section1(frames, gathered, kernels, ups):
    f32, bf16 = jnp.float32, jnp.bfloat16
    return kernel_call(
        section1_body,
        jax.ShapeDtypeStruct((320, 384), bf16),
        [
            pltpu.VMEM((768, 192), bf16),
            pltpu.VMEM((8, 12, 768), bf16),
            *[pltpu.VMEM((192, 2592), bf16)] * 4,
            pltpu.VMEM((8, 12, 768), f32),
            pltpu.VMEM((576, 192), f32),
            pltpu.VMEM((768, 192), f32),
            pltpu.VMEM((768, 576), bf16),
            pltpu.VMEM((2, 352, 192), f32),
            pltpu.VMEM((2, 384, 192), bf16),
            pltpu.VMEM((2, 192, 2304), bf16),
            pltpu.VMEM((384, 2304), f32),
            pltpu.VMEM((4, 768, 128), f32),
            pltpu.VMEM((320, 384), bf16),
        ],
        frames, gathered, *kernels, *ups,
        copies=8,
        vmem=26,
    )


def pick_body(k_any, u_any, out_any, k, u, out, sems):
    s = lax.axis_index("segment")

    @pl.when(s >= 2)
    def _():
        coming = start_all([(k_any, k), (u_any, u)], sems)
        step = jnp.where(s == 2, 2, 4)
        source = lax.broadcasted_iota(jnp.int32, (96, 192), 1)
        target = lax.broadcasted_iota(jnp.int32, (96, 192), 0)
        picked = ((source == target * step) & (target * step < 192)).astype(jnp.bfloat16)
        wait_all(coming)
        out[:, 0:2592] = dot(picked, k[...]).astype(jnp.bfloat16)
        out[:, 2688:3120] = dot(picked, u[...]).astype(jnp.bfloat16)
        wait_all(start_all([(out, out_any)], sems))


def pick(k, u):
    bf16 = jnp.bfloat16
    return kernel_call(
        pick_body,
        jax.ShapeDtypeStruct((96, 3200), bf16),
        [pltpu.VMEM((192, 2592), bf16), pltpu.VMEM((192, 432), bf16), pltpu.VMEM((96, 3200), bf16)],
        k, u,
        copies=2,
    )


def merge_body(*refs):
    pieces_any, (k2_any, k3_any, up_any) = refs[0:4], refs[4:7]
    pieces = refs[7:11]
    k2, k3, cat, up, sems = refs[11:]
    s, h = lax.axis_index("segment"), lax.axis_index("ha")
    bf16 = jnp.bfloat16

    @pl.when((s >= 2) & (h < 2))
    def _():
        wait_all(start_all(list(zip(pieces_any, pieces)), sems))
        own, nz, nx, nd = pieces
        up[...] = jnp.zeros_like(up)
        for z in range(2):
            for segment, count in ((2, 96), (3, 48)):

                @pl.when((h == z) & (s == segment))
                def _():
                    for part, (a, b) in enumerate(((own, nx), (nz, nd))):
                        at = (part ^ z) * 432
                        cat[0:count, at : at + 432] = a[0:count, 2688:3120]
                        cat[count : 2 * count, at : at + 432] = b[0:count, 2688:3120]
                        if segment == 2:
                            at = (part ^ z) * 2592
                            k2[0:96, at : at + 2592] = a[:, 0:2592]
                            k2[96:192, at : at + 2592] = b[:, 0:2592]
                    if segment == 3:
                        a, b = ((own, nx), (nz, nd))[z]
                        k3[...] = jnp.zeros_like(k3)
                        for tap in range(27):
                            k3[0:48, tap * 128 : tap * 128 + 96] = a[0:48, tap * 96 : tap * 96 + 96]
                            k3[48:96, tap * 128 : tap * 128 + 96] = b[0:48, tap * 96 : tap * 96 + 96]

        for tap in range(9):
            up[:, tap * 128 : tap * 128 + 96] = cat[:, tap * 96 : (tap + 1) * 96]
        wait_all(start_all([(up, up_any), (k2, k2_any), (k3, k3_any)], sems))


def merge(pieces):
    bf16 = jnp.bfloat16
    shapes = ((192, 5184), (96, 3456), (192, 1152))
    return kernel_call(
        merge_body,
        tuple(jax.ShapeDtypeStruct(shape, bf16) for shape in shapes),
        [
            *[pltpu.VMEM((96, 3200), bf16)] * 4,
            pltpu.VMEM((192, 5184), bf16),
            pltpu.VMEM((96, 3456), bf16),
            pltpu.VMEM((192, 864), bf16),
            pltpu.VMEM((192, 1152), bf16),
        ],
        *pieces,
        copies=4,
        vmem=12,
    )


def caches_body(*refs):
    parts, (c_any, d_any) = refs[0:6], refs[6:8]
    bands, wide, c_full, d_full, c, d, sems = refs[8:]
    s, h, w = (lax.axis_index(axis) for axis in AXES)
    f32, bf16 = jnp.float32, jnp.bfloat16

    @pl.when((s == 2) & (h < 2))
    def _():
        pairs = [(a, bands.at[n // 2, n % 2 * 48 : n % 2 * 48 + 48]) for n, a in enumerate(parts)]
        wait_all(start_all(pairs, sems))
        c_full[...] = jnp.zeros_like(c_full)
        d_full[...] = jnp.zeros_like(d_full)
        for band in range(3):
            wide[...] = bands[band].astype(f32)
            for side in range(2):
                swapped = (w + side) % 2
                for frame in range(2):
                    row = side * 48 + frame * 8
                    for column in range(8):
                        at = (frame * 26 + 1 + band * 8) * 16 + swapped * 8 + column
                        lane = column * 192
                        c_full[0, pl.ds(at, 8, stride=16), :] = wide[row : row + 8, lane : lane + 128]
                        tail = jnp.concatenate([wide[row : row + 8, lane + 128 : lane + 192]] * 2, axis=1)
                        c_full[1, pl.ds(at, 8, stride=16), :] = tail
                    row = side * 48 + 16 + frame * 16
                    for column in range(16):
                        at = (frame * 50 + 1 + band * 16) * 32 + swapped * 16 + column
                        lane = column * 96
                        part = wide[row : row + 16, lane : lane + 96]
                        part = jnp.concatenate([part, part[:, 0:32]], axis=1)
                        d_full[pl.ds(at, 16, stride=32), :] = part
        for frame in range(2):
            at = pl.multiple_of((frame * 26 + h * 6) * 16, 32)
            c[frame * 320 : frame * 320 + 320, 0:128] = c_full[0, pl.ds(at, 320), :].astype(bf16)
            c[frame * 320 : frame * 320 + 320, 128:192] = c_full[1, pl.ds(at, 320), 0:64].astype(bf16)
            at = pl.multiple_of((frame * 50 + h * 15) * 32, 32)
            d[frame * 1120 : frame * 1120 + 1120, :] = d_full[pl.ds(at, 1120), 0:96].astype(bf16)
        wait_all(start_all([(c, c_any), (d, d_any)], sems))


def caches(bands):
    f32, bf16 = jnp.float32, jnp.bfloat16
    return kernel_call(
        caches_body,
        (jax.ShapeDtypeStruct((640, 192), bf16), jax.ShapeDtypeStruct((2240, 96), bf16)),
        [
            pltpu.VMEM((3, 96, 1536), bf16),
            pltpu.VMEM((96, 1536), f32),
            pltpu.VMEM((2, 832, 128), f32),
            pltpu.VMEM((3200, 128), f32),
            pltpu.VMEM((640, 192), bf16),
            pltpu.VMEM((2240, 96), bf16),
        ],
        *bands,
        copies=6,
        vmem=16,
        cost=60 * 10**6,
    )


def sections23_body(same2, same3, other2, other3, c_own, c_sent, d_any, k2_own, k2_sent, k3_own, k3_sent, u_own, u_sent,
                    out0, out1, out2, out3, pairs, d_ref, k2, k3, u2, u3, line, base, xx, hs, p, t, base3, xx3, hs3, p3, t3, rows3, out_ref,
                    sems):
    s, h, w = (lax.axis_index(axis) for axis in AXES)
    f32, bf16 = jnp.float32, jnp.bfloat16

    @pl.when((s >= 2) & (h < 2))
    def _():
        frame = (s - 2) * 2 + w
        line[0:640] = jnp.zeros((640, 192), bf16)
        for segment, same, other in ((2, same2, other2), (3, same3, other3)):

            @pl.when(s == segment)
            def _():
                c_any = c_own if segment == 2 else c_sent
                held2, held3 = (k2_own, k3_sent) if segment == 2 else (k2_sent, k3_own)
                up2, up3 = (u_own, u_sent) if segment == 2 else (u_sent, u_own)
                start_all(
                    [
                        (same, pairs.at[w]),
                        (other, pairs.at[1 - w]),
                        (c_any, line.at[640:1280]),
                        (held2, k2),
                        (up2, u2),
                        (d_any, d_ref),
                        (held3, k3),
                        (up3.at[0:96], u3),
                    ],
                    sems,
                )

        coming = [
            pltpu.make_async_copy(a, b, sems.at[n])
            for n, (a, b) in enumerate(
                [
                    (same2, pairs.at[0]),
                    (other2, pairs.at[1]),
                    (c_own, line.at[640:1280]),
                    (k2_own, k2),
                    (u_own, u2),
                    (d_any, d_ref),
                    (k3_own, k3),
                    (u_own.at[0:96], u3),
                ]
            )
        ]
        wait_all(coming[0:3])
        for number in range(2):
            for k in range(2):
                at = 1280 + (2 * number + k) * 320
                line[at : at + 320] = pairs[number, :, k * 192 : (k + 1) * 192]

        base[...] = line[pl.ds(pl.multiple_of(frame * 320, 320), 1600), :].astype(f32)
        for dx, moved in enumerate(shifts(base[...], 16, 16)):
            xx[:, dx * 192 : (dx + 1) * 192] = moved.astype(bf16)
        coming[3].wait()
        total = None
        for group in range(9):
            start = group // 3 * 320 + group % 3 * 16
            term = dot_t(xx[start : start + 928, :], k2[:, group * 576 : (group + 1) * 576])
            total = term if total is None else total + term
        inverse = lax.rsqrt(jnp.sum(total * total, axis=1, keepdims=True) / 192.0 + EPSILON)
        keep = index_of((928, 192)) % 320 < 288
        hs[0:928] = jnp.where(keep, silu(total * inverse), 0.0).astype(bf16)
        hs[928:960] = jnp.zeros((32, 192), bf16)
        coming[4].wait()
        p[...] = dot(hs[...], u2[...])
        upsample(p, t, 16, 16, 128)

        for z in range(2):

            @pl.when(h == z)
            def _():
                blank = 0 if z == 0 else 34
                for moment in range(3):
                    to = moment * 1120 + blank * 32
                    base3[to : to + 32] = jnp.zeros((32, 96), f32)
                    for r in range(34):
                        y = r + 2 * z
                        at = moment * 640 + (y // 2) * 32
                        to = moment * 1120 + (r + 1 - z) * 32
                        base3[to : to + 32] = t[y % 2, at : at + 32, 0:96].astype(bf16).astype(f32)

        wait_all(coming[5:8])

        @pl.when(frame == 0)
        def _():
            base3[0:2240] = d_ref[...].astype(f32)

        @pl.when(frame == 1)
        def _():
            base3[0:1120] = d_ref[1120:2240].astype(f32)

        xx3[...] = jnp.zeros_like(xx3)
        for dx, moved in enumerate(shifts(base3[...], 32, 32)):
            xx3[:, dx * 128 : dx * 128 + 96] = moved.astype(bf16)
        total = None
        for group in range(9):
            start = group // 3 * 1120 + group % 3 * 32
            term = dot_t(xx3[start : start + 1056, :], k3[:, group * 384 : (group + 1) * 384])
            total = term if total is None else total + term
        inverse = lax.rsqrt(jnp.sum(total * total, axis=1, keepdims=True) / 96.0 + EPSILON)
        hs3[0:1056] = silu(total * inverse).astype(bf16)
        hs3[1056:1120] = jnp.zeros((64, 96), bf16)
        p3[...] = dot(hs3[...], u3[...])
        upsample(p3, t3, 32, 32, 128)
        for z in range(2):

            @pl.when(h == z)
            def _():
                for a in range(2):
                    for four in range(16):
                        parts = [
                            t3[a, pl.ds(z * 64 + four * 4 + n, 32, stride=64), :][:, 0:96] for n in range(4)
                        ]
                        row = jnp.concatenate(parts, axis=1)
                        for n in range(3):
                            rows3[four * 3 + n, pl.ds(a, 32, stride=2), :] = row[:, n * 128 : (n + 1) * 128]
        for tile in range(48):
            lane = tile % 24 * 128
            for n in range(2):
                part = rows3[tile, n * 32 : n * 32 + 32, :].astype(bf16)
                out_ref[n * 2 + tile // 24, :, lane : lane + 128] = part

        wait_all(start_all([(out_ref.at[n], target) for n, target in enumerate((out0, out1, out2, out3))], sems))


def sections23(received, c, c_sent, d, kernels):
    f32, bf16 = jnp.float32, jnp.bfloat16
    return kernel_call(
        sections23_body,
        tuple([jax.ShapeDtypeStruct((32, 3072), bf16)] * 4),
        [
            pltpu.VMEM((2, 320, 384), bf16),
            pltpu.VMEM((2240, 96), bf16),
            pltpu.VMEM((192, 5184), bf16),
            pltpu.VMEM((96, 3456), bf16),
            pltpu.VMEM((192, 1152), bf16),
            pltpu.VMEM((96, 1152), bf16),
            pltpu.VMEM((2560, 192), bf16),
            pltpu.VMEM((1600, 192), f32),
            pltpu.VMEM((1600, 576), bf16),
            pltpu.VMEM((960, 192), bf16),
            pltpu.VMEM((960, 1152), f32),
            pltpu.VMEM((2, 1920, 128), f32),
            pltpu.VMEM((3360, 96), f32),
            pltpu.VMEM((3360, 384), bf16),
            pltpu.VMEM((1120, 96), bf16),
            pltpu.VMEM((1120, 1152), f32),
            pltpu.VMEM((2, 2240, 128), f32),
            pltpu.VMEM((48, 64, 128), f32),
            pltpu.VMEM((4, 32, 3072), bf16),
        ],
        *received, c, c_sent, d, *kernels,
        copies=8,
        vmem=44,
    )


def beside_body(near_any, far_any, out_any, near, far, out, sems):
    wait_all(start_all([(near_any, near), (far_any, far)], sems))
    out[:, 0:432] = near[...]
    out[:, 432:864] = far[...]
    wait_all(start_all([(out, out_any)], sems))


def beside(near, far):
    shape, bf16 = (192, 864), jnp.bfloat16
    return kernel_call(
        beside_body,
        jax.ShapeDtypeStruct(shape, bf16),
        [pltpu.VMEM((192, 432), bf16), pltpu.VMEM((192, 432), bf16), pltpu.VMEM(shape, bf16)],
        near, far,
        copies=2,
        cost=15000000,
    )


def blank_body(*refs):
    pass


def blank(some, shapes):
    return kernel_call(blank_body, [jax.ShapeDtypeStruct(shape, jnp.bfloat16) for shape in shapes], [], some, copies=1)


LATER = ((192, 5184), (96, 3456), (192, 1152), (192, 5184), (96, 3456), (192, 1152), (640, 192), (640, 192), (2240, 96))


def sections01(latent, cache_a, cache_b, cache_c, cache_d, k, u):
    u_far = send(u, [((s_, h_ + 2, w_), (s_, h_, w_)) for s_ in (0, 1) for h_ in range(2) for w_ in range(2)])
    k_x, k_z = send(k, square((1,), 0, 1)), send(k, square((1,), 1, 0))
    gathered = lax.all_to_all(
        spread_tiles(latent, cache_a, cache_b), ("ha", "wa"), split_axis=0, concat_axis=0, tiled=True
    )
    ups = beside(u, u_far)
    u_z, u_x, u_d = (send(ups, square((0, 1), dh, dw)) for dh, dw in ((1, 0), (0, 1), (1, 1)))
    partial_sums = conv0(gathered, k)
    partial_sums, k_x, k_z = lax.optimization_barrier((partial_sums, k_x, k_z))
    k_d = send(k_z, square((1,), 0, 1))
    partials = lax.all_to_all(partial_sums, ("ha", "wa"), split_axis=0, concat_axis=0, tiled=True)
    taps = join((ups, u_z, u_x, u_d))
    risen = up0(partials, taps)
    given = send(risen, [((0, h_, w_), (1, h_, w_)) for h_ in range(2) for w_ in range(2)])
    out1 = section1(given, gathered, (k, k_z, k_x, k_d), taps)
    return (out1, *blank(k, LATER))


def before_sections23(latent, cache_a, cache_b, cache_c, cache_d, k, u):
    own = jnp.concatenate([cache_c.reshape(16, 1536), cache_d.reshape(32, 1536)], axis=0)
    bands = [own] + [
        send(own, [((2, h_ + n, w_ ^ dw), (2, h_, w_)) for h_ in range(2) for w_ in range(2)])
        for n in range(3)
        for dw in range(2)
        if n + dw
    ]
    picked = pick(k, u)
    picked_x, picked_z, picked_d = (send(picked, square((2, 3), dh, dw)) for dh, dw in ((0, 1), (1, 0), (1, 1)))
    k2, k3, u23 = merge((picked, picked_z, picked_x, picked_d))
    pairs = [((s_, h_, w_), (s_ ^ 1, h_, w_)) for s_ in (2, 3) for h_ in range(2) for w_ in range(2)]
    rise, fall = [pair for pair in pairs if pair[0][0] == 2], [pair for pair in pairs if pair[0][0] == 3]
    c, d = caches(bands)
    c_sent, k2_sent, k3_sent, u_sent = send(c, rise), send(k2, rise), send(k3, fall), send(u23, pairs)
    return (*blank(k, ((320, 384),)), k2, k3, u23, k2_sent, k3_sent, u_sent, c, c_sent, d)


def relay(latent, cache_a, cache_b, cache_c, cache_d, conv_pack, up_pack):
    s, h, w = (lax.axis_index(axis) for axis in AXES)
    k, u = conv_pack[0].T, up_pack[0]
    out1, k2, k3, u23, k2_sent, k3_sent, u_sent, c, c_sent, d = lax.cond(
        s < 2, sections01, before_sections23, latent, cache_a, cache_b, cache_c, cache_d, k, u
    )
    received = [
        send(out1, [((1, h_, w_), (s_, h_, w_ ^ dw)) for h_ in range(2) for w_ in range(2)])
        for dw in range(2)
        for s_ in (2, 3)
    ]
    blocks = sections23(received, c, c_sent, d, (k2, k2_sent, k3, k3_sent, u23, u_sent))

    arrived = [
        send(
            blocks[2 * n + half],
            [((2 + c_, z, x), (2 * c_ + x, 2 * z + n, half)) for c_ in range(2) for z in range(2) for x in range(2)],
        )
        for n in range(2)
        for half in range(2)
    ]
    lower_half = jnp.where(w == 0, arrived[2], arrived[3])
    upper_half = jnp.where(w == 0, arrived[0], arrived[1])
    return jnp.where(h % 2 == 0, upper_half, lower_half)[None]


def solution(mesh):
    in_specs = (
        P(None, "ha", "wa"),
        P(None, "ha", "wa"),
        P(None, "ha", "wa"),
        P(None, "ha", "wa"),
        P(None, "ha", "wa"),
        P("segment", "ha", "wa"),
        P("segment", "wa", "ha"),
    )
    out_specs = P("segment", "ha", "wa")
    sizes = tuple(mesh.shape[axis] for axis in AXES)
    program = relay if sizes == (4, 4, 2) else per_device
    return jax.shard_map(
        program, mesh=mesh, in_specs=in_specs, out_specs=out_specs, check_vma=False
    )
```

```python
from functools import partial

import jax
import jax.numpy as jnp
from jax import lax
from jax.experimental import pallas as pl
from jax.experimental.pallas import tpu as pltpu
from jax.sharding import PartitionSpec as P

WIDE = 384
MID = 192
NARROW = 96


EPSILON = 1e-06


def shortened(array):

    def short(part):
        return part.astype(jnp.bfloat16) if part.dtype == jnp.float32 else part

    return jax.tree.map(short, array)


def passed_along(value, axis, steps):
    count = lax.axis_size(axis)
    initial, last = (max(0, -steps), min(count, count - steps))
    return lax.ppermute(value, axis, [(source, source + steps) for source in range(initial, last)])


def layer_table():
    return ((WIDE, WIDE, MID), (MID, WIDE, MID), (MID, MID, NARROW), (NARROW, NARROW, NARROW))


def round_up(amount):
    return -(-amount // 128) * 128


def volume(target):
    amount = 1
    for extent in target:
        amount = amount * extent
    return amount


def flat_pad(tensor, length):
    leading = tensor.shape[0]
    packed = tensor.reshape(leading, -1)
    return jnp.pad(packed, ((0, 0), (0, length - packed.shape[1])))


def reshaped(packed, target):
    return packed[:, : volume(target)].reshape((packed.shape[0],) + tuple(target))


def add_rows(tensor, from_above, from_below):
    leading, height, width, channels = tensor.shape
    upper = reshaped(from_above, (1, width, channels))
    lower = reshaped(from_below, (1, width, channels))
    return jnp.concatenate([upper, tensor, lower], axis=1)


def add_cols(tensor, from_left, from_right):
    leading, height, width, channels = tensor.shape
    before = reshaped(from_left, (height, 1, channels))
    after = reshaped(from_right, (height, 1, channels))
    return jnp.concatenate([before, tensor, after], axis=2)


def trade_rows(upper_rim, bottom):
    return (
        jax.tree.map(
            lambda part, own: part.astype(own.dtype),
            passed_along(shortened(bottom), "ha", 1),
            bottom,
        ),
        jax.tree.map(
            lambda part, own: part.astype(own.dtype),
            passed_along(shortened(upper_rim), "ha", -1),
            upper_rim,
        ),
    )


def trade_cols(left_rim, right_rim):
    return (
        jax.tree.map(
            lambda part, own: part.astype(own.dtype),
            passed_along(shortened(right_rim), "wa", 1),
            right_rim,
        ),
        jax.tree.map(
            lambda part, own: part.astype(own.dtype),
            passed_along(shortened(left_rim), "wa", -1),
            left_rim,
        ),
    )


def causal_conv(stacked, kernel):
    result = lax.conv_general_dilated(
        stacked[None],
        kernel,
        (1, 1, 1),
        "VALID",
        dimension_numbers=("NDHWC", "DHWIO", "NDHWC"),
        preferred_element_type=jnp.float32,
    )
    return result[0, 0]


def activate(conv_sum):
    inverse = lax.rsqrt(jnp.mean(conv_sum * conv_sum, axis=-1, keepdims=True) + EPSILON)
    return jax.nn.silu(conv_sum * inverse).astype(jnp.bfloat16)


def upsample_conv(hidden_ext, kernel):
    expanded = jnp.repeat(jnp.repeat(hidden_ext, 2, axis=0), 2, axis=1)[1:-1, 1:-1]
    result = lax.conv_general_dilated(
        expanded[None],
        kernel,
        (1, 1),
        "VALID",
        dimension_numbers=("NHWC", "HWIO", "NHWC"),
        preferred_element_type=jnp.float32,
    )
    return result[0].astype(jnp.bfloat16)


def per_device(latent, cache_a, cache_b, cache_c, cache_d, conv_pack, up_pack):
    frames = latent.shape[0]
    tile_rows = latent.shape[1]
    tile_cols = latent.shape[2] // WIDE
    layers = layer_table()
    section = lax.axis_index("segment")
    segments = lax.axis_size("segment")
    final_segment = segments - 1
    input_shapes = [
        (tile_rows << level, tile_cols << level, layers[level][0]) for level in range(4)
    ]
    mid_shapes = [(tile_rows << level, tile_cols << level, layers[level][1]) for level in range(4)]
    out_shapes = [
        (tile_rows << level + 1, tile_cols << level + 1, layers[level][2]) for level in range(4)
    ]
    ext_shapes = [(target[0] + 2, target[1] + 2, target[2]) for target in input_shapes]
    all_shapes = input_shapes + mid_shapes
    row_length = round_up(max((target[1] * target[2] for target in all_shapes)))
    column_length = round_up(max(((target[0] + 2) * target[2] for target in all_shapes)))
    size_input = round_up(max((volume(target) for target in input_shapes)))
    size_middle = round_up(max((volume(target) for target in mid_shapes)))
    size_extended = round_up(max((volume(target) for target in ext_shapes)))
    size_output = round_up(max((volume(target) for target in out_shapes)))
    final_shape = out_shapes[3]
    final_count = volume(final_shape)
    conv_rows, up_rows = (
        lax.all_gather(conv_pack, "ha", axis=1, tiled=True),
        lax.all_gather(up_pack, "ha", axis=2, tiled=True),
    )
    conv_all, up_all = (
        lax.all_gather(conv_rows, "wa", axis=2, tiled=True),
        lax.all_gather(up_rows, "wa", axis=1, tiled=True),
    )

    def conv_kernel(level):
        width_in, width_mid, width_out = layers[level]
        columns = conv_all[0, : 27 * width_in, :: WIDE // width_mid]
        return columns.reshape(3, 3, 3, width_in, columns.shape[1])

    def up_kernel(level):
        width_in, width_mid, width_out = layers[level]
        rows_used = up_all[0, :: WIDE // width_mid, : 9 * width_out]
        return rows_used.reshape(width_mid, 3, 3, width_out).transpose(1, 2, 0, 3)

    conv_kernels = [conv_kernel(level) for level in range(4)]
    up_kernels = [up_kernel(level) for level in range(4)]

    def row_rims(packed, shapes):

        def rows_branch(level, packed):
            tensor = reshaped(packed, shapes[level])
            return (flat_pad(tensor[:, :1], row_length), flat_pad(tensor[:, -1:], row_length))

        upper_rim, bottom = lax.switch(
            section, [partial(rows_branch, level) for level in range(4)], packed
        )
        return trade_rows(upper_rim, bottom)

    def extend(packed, shapes):
        from_above, from_below = row_rims(packed, shapes)

        def cols_branch(level, packed, from_above, from_below):
            tensor = add_rows(reshaped(packed, shapes[level]), from_above, from_below)
            return (
                flat_pad(tensor[:, :, :1], column_length),
                flat_pad(tensor[:, :, -1:], column_length),
            )

        left_rim, right_rim = lax.switch(
            section,
            [partial(cols_branch, level) for level in range(4)],
            packed,
            from_above,
            from_below,
        )
        from_left, from_right = trade_cols(left_rim, right_rim)
        return (from_above, from_below, from_left, from_right)

    def assemble(packed, target, rims):
        tensor = add_rows(reshaped(packed, target), rims[0], rims[1])
        return add_cols(tensor, rims[2], rims[3])

    caches = (cache_a, cache_b, cache_c, cache_d)

    def cache_branch(level):
        return flat_pad(caches[level], size_input)

    cached = lax.switch(section, [partial(cache_branch, level) for level in range(4)])
    cache_rims = extend(cached, input_shapes)

    def store_branch(level, packed, rims):
        return flat_pad(assemble(packed, input_shapes[level], rims), size_extended)

    history = lax.switch(
        section, [partial(store_branch, level) for level in range(4)], cached, cache_rims
    )
    finished = jnp.zeros((frames, final_shape[0], final_shape[1] * final_shape[2]), jnp.bfloat16)
    stream = jnp.zeros((1, size_input), jnp.bfloat16)
    for moment in range(frames + segments - 1):
        if moment == 0:
            incoming = stream
        else:
            incoming = jax.tree.map(
                lambda part, own: part.astype(own.dtype),
                passed_along(shortened(stream), "segment", 1),
                stream,
            )
        frame_id = moment - section
        active = (frame_id >= 0) & (frame_id < frames)
        chosen = jnp.clip(frame_id, 0, frames - 1)
        picked = lax.dynamic_index_in_dim(latent, chosen, 0, keepdims=True)
        current = jnp.where(section == 0, flat_pad(picked, size_input), incoming)
        branch_id = jnp.where(active, section, 4)
        rims = extend(current, input_shapes)

        def conv_branch(level, current, history, rims):
            window = assemble(current, input_shapes[level], rims)
            earlier = reshaped(history, ext_shapes[level])
            hidden = activate(
                causal_conv(jnp.concatenate([earlier, window], axis=0), conv_kernels[level])
            )
            return (flat_pad(hidden[None], size_middle), flat_pad(window, size_extended))

        def spare_conv(current, history, rims):
            return (
                jnp.zeros((1, size_middle), jnp.bfloat16),
                jnp.zeros((1, size_extended), jnp.bfloat16),
            )

        hidden, window = lax.switch(
            branch_id,
            [partial(conv_branch, level) for level in range(4)] + [spare_conv],
            current,
            history,
            rims,
        )
        hidden_rims = extend(hidden, mid_shapes)

        def up_branch(level, hidden, hidden_rims):
            expanded = assemble(hidden, mid_shapes[level], hidden_rims)[0]
            return flat_pad(upsample_conv(expanded, up_kernels[level])[None], size_output)

        def spare_up(hidden, hidden_rims):
            return jnp.zeros((1, size_output), jnp.bfloat16)

        produced = lax.switch(
            branch_id,
            [partial(up_branch, level) for level in range(4)] + [spare_up],
            hidden,
            hidden_rims,
        )
        shifted = jnp.concatenate([history[1:], window], axis=0)
        history = jnp.where(active, shifted, history)
        stream = produced[:, :size_input]
        if moment >= final_segment:
            finished_id = moment - final_segment
            picture = produced[:, :final_count].reshape(
                1, final_shape[0], final_shape[1] * final_shape[2]
            )
            finished = finished.at[finished_id].set(picture[0])
    collected = lax.all_to_all(finished, "segment", split_axis=0, concat_axis=0, tiled=True)
    per_segment = frames // segments
    own_frame = collected[final_segment * per_segment : (final_segment + 1) * per_segment]
    return own_frame


AXES = ("segment", "ha", "wa")
MIB = 1024 * 1024


def place(s, h, w):
    return (s * 4 + h) * 2 + w


def send(value, pairs):
    return lax.ppermute(value, AXES, [(place(*a), place(*b)) for a, b in pairs])


def square(segments, dh, dw):
    return [
        ((s, h, w), (s, h ^ dh, w ^ dw)) for s in segments for h in range(2) for w in range(2)
    ]


def kernel_call(body, out_shape, scratch, *args, copies=0, vmem=16, cost=1000, place=pl.ANY):
    return pl.pallas_call(
        body,
        out_shape=out_shape,
        in_specs=[pl.BlockSpec(memory_space=place)] * len(args),
        out_specs=jax.tree.map(lambda _: pl.BlockSpec(memory_space=pl.ANY), out_shape),
        scratch_shapes=scratch + [pltpu.SemaphoreType.DMA((copies,))],
        compiler_params=pltpu.CompilerParams(vmem_limit_bytes=vmem * MIB),
        cost_estimate=pl.CostEstimate(flops=1000 * cost, bytes_accessed=1000, transcendentals=0),
    )(*args)


def start_all(pairs, sems, first=0):
    copies = [pltpu.make_async_copy(a, b, sems.at[first + n]) for n, (a, b) in enumerate(pairs)]
    for copy in copies:
        copy.start()
    return copies


def wait_all(copies):
    for copy in copies:
        copy.wait()


def dot(a, b):
    return jnp.dot(a, b, preferred_element_type=jnp.float32)


def dot_t(a, b):
    return lax.dot_general(a, b, (((1,), (1,)), ((), ())), preferred_element_type=jnp.float32)


def index_of(shape):
    return lax.broadcasted_iota(jnp.int32, shape, 0)


def silu(v):
    return v / (1.0 + jnp.exp(-v))


def shifts(base, pitch, width):
    n = base.shape[0]
    left, right = pltpu.roll(base, 1, 0), pltpu.roll(base, n - 1, 0)
    if pitch == width:
        column = index_of(base.shape) % pitch
        left = jnp.where(column == 0, 0.0, left)
        right = jnp.where(column == width - 1, 0.0, right)
    return left, base, right


def upsample(p_ref, t_ref, pitch, width, lanes):
    n = p_ref.shape[0]
    blocks = lanes // 128
    column = index_of((n, 128)) % pitch
    for block in range(blocks):

        def tap(dy, dx):
            at = (dy * 3 + dx) * lanes + block * 128
            return p_ref[:, at : at + 128]

        for b in range(2):
            rows = []
            for dy in range(3):
                middle = tap(dy, 1)
                if b == 0:
                    far = pltpu.roll(tap(dy, 0), 1, 0)
                    if pitch == width:
                        far = jnp.where(column == 0, 0.0, far)
                    rows.append(far + middle + tap(dy, 2))
                else:
                    far = pltpu.roll(tap(dy, 2), n - 1, 0)
                    if pitch == width:
                        far = jnp.where(column == width - 1, 0.0, far)
                    rows.append(tap(dy, 0) + middle + far)
            t_ref[block, pl.ds(b, n, stride=2), :] = pltpu.roll(rows[0], pitch, 0) + rows[1] + rows[2]
            t_ref[blocks + block, pl.ds(b, n, stride=2), :] = (
                rows[0] + rows[1] + pltpu.roll(rows[2], n - pitch, 0)
            )


def tiles_body(latent_any, a_any, b_any, out_any, latent, a, b, rows, out, sems):
    wait_all(start_all([(latent_any, latent), (a_any, a), (b_any, b)], sems))

    @pl.when(lax.axis_index("segment") == 0)
    def _():
        for frame in range(4):
            rows[frame * 2 : frame * 2 + 2] = latent[frame].astype(jnp.float32)
        for frame in range(2):
            rows[8 + frame * 2 : 10 + frame * 2] = a[frame].astype(jnp.float32)

    @pl.when(lax.axis_index("segment") > 0)
    def _():
        for frame in range(2):
            rows[frame * 4 : frame * 4 + 4] = b[frame].astype(jnp.float32)
        rows[8:12] = jnp.zeros((4, 768), jnp.float32)

    out[...] = rows[...].astype(jnp.bfloat16)
    wait_all(start_all([(out, out_any.at[n]) for n in range(8)], sems))


def spread_tiles(latent, cache_a, cache_b):
    bf16 = jnp.bfloat16
    return kernel_call(
        tiles_body,
        jax.ShapeDtypeStruct((8, 12, 768), bf16),
        [
            pltpu.VMEM((4, 2, 768), bf16),
            pltpu.VMEM((2, 2, 768), bf16),
            pltpu.VMEM((2, 4, 768), bf16),
            pltpu.VMEM((12, 768), jnp.float32),
            pltpu.VMEM((12, 768), bf16),
        ],
        latent, cache_a, cache_b,
        copies=8,
    )


def conv0_body(g_any, k_any, out_any, g_ref, k_ref, gf, base, xx, acc, buf, out_ref, sems):
    s, h = lax.axis_index("segment"), lax.axis_index("ha")

    @pl.when(s == 0)
    def _():
        coming = start_all([(g_any, g_ref), (k_any, k_ref)], sems)
        base[...] = jnp.zeros_like(base)
        coming[0].wait()
        gf[...] = g_ref[...].astype(jnp.float32)
        for frame in range(6):
            for hh in range(4):
                for ww in range(2):
                    for r in range(2):
                        row = 8 + frame * 2 + r if frame < 2 else (frame - 2) * 2 + r
                        for c in range(2):
                            at = frame * 160 + (1 + 2 * hh + r) * 16 + 2 * ww + c
                            base[at : at + 1, :] = gf[hh * 2 + ww, row : row + 1, c * 384 : (c + 1) * 384]
        for dx, moved in enumerate(shifts(base[...], 16, 4)):
            xx[dx] = moved.astype(jnp.bfloat16)
        coming[1].wait()
        for part in range(4):

            @pl.when(h == part)
            def _():
                total = None
                at, end = part * 2592, part * 2592 + 2592
                while at < end:
                    tap, c0 = divmod(at, 384)
                    c1 = min(384, c0 + end - at)
                    dt, dy, dx = tap // 9, tap // 3 % 3, tap % 3
                    start = dt * 160 + dy * 16
                    k0 = at - part * 2592
                    term = dot_t(xx[dx, start : start + 608, c0:c1], k_ref[:, k0 : k0 + c1 - c0])
                    total = term if total is None else total + term
                    at += c1 - c0
                acc[...] = total

        for frame in range(4):
            for r in range(8):
                to, at = (frame * 8 + r) * 4, frame * 160 + r * 16
                buf[to : to + 4, :] = acc[at : at + 4, :]
        out_ref[0:128, :] = buf[:, 0:128].astype(jnp.bfloat16)
        tail = jnp.concatenate([buf[0:64, 128:192], buf[64:128, 128:192]], axis=1)
        out_ref[128:192, :] = tail.astype(jnp.bfloat16)
        wait_all(start_all([(out_ref, out_any.at[n]) for n in range(8)], sems))


def conv0(gathered, k):
    f32, bf16 = jnp.float32, jnp.bfloat16
    return kernel_call(
        conv0_body,
        jax.ShapeDtypeStruct((8, 192, 128), bf16),
        [
            pltpu.VMEM((8, 12, 768), bf16),
            pltpu.VMEM((192, 2592), bf16),
            pltpu.VMEM((8, 12, 768), f32),
            pltpu.VMEM((960, 384), f32),
            pltpu.VMEM((3, 960, 384), bf16),
            pltpu.VMEM((608, 192), f32),
            pltpu.VMEM((128, 192), f32),
            pltpu.VMEM((192, 128), bf16),
        ],
        gathered, k,
        copies=8,
        cost=20 * 10**6,
    )


def join_body(own, nz, nx, nd, mine_any, other_any, cat, taps, sems):
    s, h = lax.axis_index("segment"), lax.axis_index("ha")

    @pl.when((s < 2) & (h < 2))
    def _():
        sending = []
        for half, (near, far, target) in enumerate(((own, nz, mine_any), (nx, nd, other_any))):
            for z in range(2):

                @pl.when(h == z)
                def _():
                    for first, pieces in ((z, near), (1 - z, far)):
                        for n in range(2):
                            at = (first + 2 * n) * 432
                            cat[:, at : at + 432] = pieces[:, n * 432 : (n + 1) * 432]

            for tap in range(9):
                taps[half, :, tap * 256 : tap * 256 + 192] = cat[:, tap * 192 : (tap + 1) * 192]
                taps[half, :, tap * 256 + 192 : (tap + 1) * 256] = jnp.zeros((192, 64), jnp.bfloat16)
            sending += start_all([(taps.at[half], target)], sems, half)
        wait_all(sending)


def join(pieces):
    bf16 = jnp.bfloat16
    return kernel_call(
        join_body,
        (jax.ShapeDtypeStruct((192, 2304), bf16), jax.ShapeDtypeStruct((192, 2304), bf16)),
        [pltpu.VMEM((192, 1728), bf16), pltpu.VMEM((2, 192, 2304), bf16)],
        *pieces,
        copies=2,
        vmem=8,
        cost=20 * 10**6,
        place=pltpu.VMEM,
    )


def up0_body(*refs):
    y_any, taps_any, out_any = refs[0], refs[1:3], refs[3]
    y, taps, hbuf, hs, p, t, out_ref, sems = refs[4:]
    s, h, w = (lax.axis_index(axis) for axis in AXES)

    @pl.when((s == 0) & (h < 2))
    def _():
        coming = start_all([(y_any, y)], sems)
        rising = start_all([(a, taps.at[n]) for n, a in enumerate(taps_any)], sems, 1)
        wait_all(coming)
        halves = []
        for side in range(2):
            total = y[side].astype(jnp.float32)
            for hh in range(1, 4):
                total = total + y[hh * 2 + side].astype(jnp.float32)
            tail = jnp.concatenate([total[128:192, 0:64], total[128:192, 64:128]], axis=0)
            halves.append(jnp.concatenate([total[0:128], tail], axis=1))
        squares = sum(jnp.sum(half * half, axis=1, keepdims=True) for half in halves)
        inverse = lax.rsqrt(squares / 384.0 + EPSILON)
        active = [silu(half * inverse) for half in halves]
        hs[...] = jnp.zeros_like(hs)
        for k in range(2):
            hbuf[...] = jnp.where(w == k, active[0], active[1])
            for frame in range(4):
                for r in range(8):
                    to, at = frame * 72 + r * 8, (frame * 8 + r) * 4
                    hs[k, to : to + 4, :] = hbuf[at : at + 4, :]
        wait_all(rising)
        p[...] = dot(hs[0].astype(jnp.bfloat16), taps[0]) + dot(hs[1].astype(jnp.bfloat16), taps[1])
        upsample(p, t, 8, 4, 256)
        column = index_of((16, 192))
        out_ref[...] = jnp.zeros_like(out_ref)
        for z in range(2):

            @pl.when(h == z)
            def _():
                for frame in range(4):
                    for r in range(11):
                        y = r + 5 * z
                        at = frame * 144 + (y // 2) * 16
                        to = frame * 192 + (r + 1 - z) * 16
                        for lane, count in ((0, 128), (128, 64)):
                            row = t[y % 2 * 2 + lane // 128, at : at + 16, 0:count]
                            row = jnp.where(column[:, 0:count] < 8, row, 0.0)
                            out_ref[to : to + 16, lane : lane + count] = row.astype(jnp.bfloat16)

        wait_all(start_all([(out_ref, out_any)], sems))


def up0(partials, ups):
    f32, bf16 = jnp.float32, jnp.bfloat16
    return kernel_call(
        up0_body,
        jax.ShapeDtypeStruct((768, 192), bf16),
        [
            pltpu.VMEM((8, 192, 128), bf16),
            pltpu.VMEM((2, 192, 2304), bf16),
            pltpu.VMEM((128, 192), f32),
            pltpu.VMEM((2, 288, 192), f32),
            pltpu.VMEM((288, 2304), f32),
            pltpu.VMEM((4, 576, 128), f32),
            pltpu.VMEM((768, 192), bf16),
        ],
        partials, *ups,
        copies=3,
    )


def group_rows(first, second, group):
    at, end = group * 576, group * 576 + 576
    if end <= 2592:
        return first[:, at:end]
    if at >= 2592:
        return second[:, at - 2592 : end - 2592]
    return jnp.concatenate([first[:, at:2592], second[:, 0 : end - 2592]], axis=1)


def section1_body(x_any, g_any, *refs):
    kernels_any, taps_any, out_any = refs[0:4], refs[4:6], refs[6]
    x_ref, g_ref = refs[7:9]
    k_own, k_z, k_x, k_d = refs[9:13]
    gf, full, base, xx, acc, hs, taps, p, t, out_ref, sems = refs[13:]
    s, h, w = (lax.axis_index(axis) for axis in AXES)

    @pl.when((s == 1) & (h < 2))
    def _():
        coming = start_all([(x_any, x_ref), (g_any, g_ref)], sems)
        arriving = start_all(list(zip(kernels_any, (k_own, k_z, k_x, k_d))), sems, 2)
        rising = start_all([(a, taps.at[n]) for n, a in enumerate(taps_any)], sems, 6)
        wait_all(coming)

        @pl.when(w == 0)
        def _():
            gf[...] = g_ref[...].astype(jnp.float32)
            full[...] = jnp.zeros_like(full)
            for frame in range(2):
                for hh in range(4):
                    for ww in range(2):
                        for r in range(4):
                            for c in range(4):
                                row = frame * 4 + r
                                at = frame * 288 + (1 + hh * 4 + r) * 16 + ww * 4 + c
                                full[at : at + 1, :] = gf[hh * 2 + ww, row : row + 1, c * 192 : (c + 1) * 192]
            for frame in range(2):
                start = pl.multiple_of(frame * 288 + h * 96, 32)
                base[frame * 192 : (frame + 1) * 192] = full[pl.ds(start, 192), :]
            base[384:768] = x_ref[0:384].astype(jnp.float32)

        @pl.when(w == 1)
        def _():
            base[...] = x_ref[...].astype(jnp.float32)

        for dx, moved in enumerate(shifts(base[...], 16, 8)):
            xx[:, dx * 192 : (dx + 1) * 192] = moved.astype(jnp.bfloat16)
        wait_all(arriving)
        for z in range(2):

            @pl.when(h == z)
            def _():
                for k, (mine, other) in enumerate(((k_own, k_z), (k_x, k_d))):
                    first, second = (mine, other) if z == 0 else (other, mine)
                    total = None
                    for group in range(9):
                        start = group // 3 * 192 + group % 3 * 16
                        term = dot_t(xx[start : start + 352, :], group_rows(first, second, group))
                        total = term if total is None else total + term
                    acc[k] = total

        squares = sum(jnp.sum(acc[k] * acc[k], axis=1, keepdims=True) for k in range(2))
        inverse = lax.rsqrt(squares / 384.0 + EPSILON)
        index = index_of((352, 192))
        keep = (index % 192 < 160) & (index % 16 < 8)
        for k in range(2):
            hs[k, 0:352] = jnp.where(keep, silu(acc[k] * inverse), 0.0).astype(jnp.bfloat16)
            hs[k, 352:384] = jnp.zeros((32, 192), jnp.bfloat16)
        wait_all(rising)
        p[...] = dot(hs[0], taps[0]) + dot(hs[1], taps[1])
        upsample(p, t, 16, 8, 256)
        out_ref[...] = jnp.zeros_like(out_ref)
        for z in range(2):

            @pl.when(h == z)
            def _():
                for frame in range(2):
                    for r in range(19):
                        y = r + z
                        at = frame * 384 + (y // 2) * 32
                        to = (r + 1 - z) * 16
                        for lane, count in ((0, 128), (128, 64)):
                            row = t[y % 2 * 2 + lane // 128, at : at + 16, 0:count].astype(jnp.bfloat16)
                            lane0 = frame * 192 + lane
                            out_ref[to : to + 16, lane0 : lane0 + count] = row

        wait_all(start_all([(out_ref, out_any)], sems))


def section1(frames, gathered, kernels, ups):
    f32, bf16 = jnp.float32, jnp.bfloat16
    return kernel_call(
        section1_body,
        jax.ShapeDtypeStruct((320, 384), bf16),
        [
            pltpu.VMEM((768, 192), bf16),
            pltpu.VMEM((8, 12, 768), bf16),
            *[pltpu.VMEM((192, 2592), bf16)] * 4,
            pltpu.VMEM((8, 12, 768), f32),
            pltpu.VMEM((576, 192), f32),
            pltpu.VMEM((768, 192), f32),
            pltpu.VMEM((768, 576), bf16),
            pltpu.VMEM((2, 352, 192), f32),
            pltpu.VMEM((2, 384, 192), bf16),
            pltpu.VMEM((2, 192, 2304), bf16),
            pltpu.VMEM((384, 2304), f32),
            pltpu.VMEM((4, 768, 128), f32),
            pltpu.VMEM((320, 384), bf16),
        ],
        frames, gathered, *kernels, *ups,
        copies=8,
        vmem=26,
    )


def pick_body(k_any, u_any, out_any, k, u, out, sems):
    s = lax.axis_index("segment")

    @pl.when(s >= 2)
    def _():
        coming = start_all([(k_any, k), (u_any, u)], sems)
        step = jnp.where(s == 2, 2, 4)
        source = lax.broadcasted_iota(jnp.int32, (96, 192), 1)
        target = lax.broadcasted_iota(jnp.int32, (96, 192), 0)
        picked = ((source == target * step) & (target * step < 192)).astype(jnp.bfloat16)
        wait_all(coming)
        out[:, 0:2592] = dot(picked, k[...]).astype(jnp.bfloat16)
        out[:, 2688:3120] = dot(picked, u[...]).astype(jnp.bfloat16)
        wait_all(start_all([(out, out_any)], sems))


def pick(k, u):
    bf16 = jnp.bfloat16
    return kernel_call(
        pick_body,
        jax.ShapeDtypeStruct((96, 3200), bf16),
        [pltpu.VMEM((192, 2592), bf16), pltpu.VMEM((192, 432), bf16), pltpu.VMEM((96, 3200), bf16)],
        k, u,
        copies=2,
    )


def merge_body(*refs):
    pieces_any, (k2_any, k3_any, up_any) = refs[0:4], refs[4:7]
    pieces = refs[7:11]
    k2, k3, cat, up, sems = refs[11:]
    s, h = lax.axis_index("segment"), lax.axis_index("ha")
    bf16 = jnp.bfloat16

    @pl.when((s >= 2) & (h < 2))
    def _():
        wait_all(start_all(list(zip(pieces_any, pieces)), sems))
        own, nz, nx, nd = pieces
        up[...] = jnp.zeros_like(up)
        for z in range(2):
            for segment, count in ((2, 96), (3, 48)):

                @pl.when((h == z) & (s == segment))
                def _():
                    for part, (a, b) in enumerate(((own, nx), (nz, nd))):
                        at = (part ^ z) * 432
                        cat[0:count, at : at + 432] = a[0:count, 2688:3120]
                        cat[count : 2 * count, at : at + 432] = b[0:count, 2688:3120]
                        if segment == 2:
                            at = (part ^ z) * 2592
                            k2[0:96, at : at + 2592] = a[:, 0:2592]
                            k2[96:192, at : at + 2592] = b[:, 0:2592]
                    if segment == 3:
                        a, b = ((own, nx), (nz, nd))[z]
                        k3[...] = jnp.zeros_like(k3)
                        for tap in range(27):
                            k3[0:48, tap * 128 : tap * 128 + 96] = a[0:48, tap * 96 : tap * 96 + 96]
                            k3[48:96, tap * 128 : tap * 128 + 96] = b[0:48, tap * 96 : tap * 96 + 96]

        for tap in range(9):
            up[:, tap * 128 : tap * 128 + 96] = cat[:, tap * 96 : (tap + 1) * 96]
        wait_all(start_all([(up, up_any), (k2, k2_any), (k3, k3_any)], sems))


def merge(pieces):
    bf16 = jnp.bfloat16
    shapes = ((192, 5184), (96, 3456), (192, 1152))
    return kernel_call(
        merge_body,
        tuple(jax.ShapeDtypeStruct(shape, bf16) for shape in shapes),
        [
            *[pltpu.VMEM((96, 3200), bf16)] * 4,
            pltpu.VMEM((192, 5184), bf16),
            pltpu.VMEM((96, 3456), bf16),
            pltpu.VMEM((192, 864), bf16),
            pltpu.VMEM((192, 1152), bf16),
        ],
        *pieces,
        copies=4,
        vmem=12,
    )


def caches_body(*refs):
    parts, (c_any, d_any) = refs[0:6], refs[6:8]
    bands, wide, c_full, d_full, c, d, sems = refs[8:]
    s, h, w = (lax.axis_index(axis) for axis in AXES)
    f32, bf16 = jnp.float32, jnp.bfloat16

    @pl.when((s == 2) & (h < 2))
    def _():
        pairs = [(a, bands.at[n // 2, n % 2 * 48 : n % 2 * 48 + 48]) for n, a in enumerate(parts)]
        wait_all(start_all(pairs, sems))
        c_full[...] = jnp.zeros_like(c_full)
        d_full[...] = jnp.zeros_like(d_full)
        for band in range(3):
            wide[...] = bands[band].astype(f32)
            for side in range(2):
                swapped = (w + side) % 2
                for frame in range(2):
                    row = side * 48 + frame * 8
                    for column in range(8):
                        at = (frame * 26 + 1 + band * 8) * 16 + swapped * 8 + column
                        lane = column * 192
                        c_full[0, pl.ds(at, 8, stride=16), :] = wide[row : row + 8, lane : lane + 128]
                        tail = jnp.concatenate([wide[row : row + 8, lane + 128 : lane + 192]] * 2, axis=1)
                        c_full[1, pl.ds(at, 8, stride=16), :] = tail
                    row = side * 48 + 16 + frame * 16
                    for column in range(16):
                        at = (frame * 50 + 1 + band * 16) * 32 + swapped * 16 + column
                        lane = column * 96
                        part = wide[row : row + 16, lane : lane + 96]
                        part = jnp.concatenate([part, part[:, 0:32]], axis=1)
                        d_full[pl.ds(at, 16, stride=32), :] = part
        for frame in range(2):
            at = pl.multiple_of((frame * 26 + h * 6) * 16, 32)
            c[frame * 320 : frame * 320 + 320, 0:128] = c_full[0, pl.ds(at, 320), :].astype(bf16)
            c[frame * 320 : frame * 320 + 320, 128:192] = c_full[1, pl.ds(at, 320), 0:64].astype(bf16)
            at = pl.multiple_of((frame * 50 + h * 15) * 32, 32)
            d[frame * 1120 : frame * 1120 + 1120, :] = d_full[pl.ds(at, 1120), 0:96].astype(bf16)
        wait_all(start_all([(c, c_any), (d, d_any)], sems))


def caches(bands):
    f32, bf16 = jnp.float32, jnp.bfloat16
    return kernel_call(
        caches_body,
        (jax.ShapeDtypeStruct((640, 192), bf16), jax.ShapeDtypeStruct((2240, 96), bf16)),
        [
            pltpu.VMEM((3, 96, 1536), bf16),
            pltpu.VMEM((96, 1536), f32),
            pltpu.VMEM((2, 832, 128), f32),
            pltpu.VMEM((3200, 128), f32),
            pltpu.VMEM((640, 192), bf16),
            pltpu.VMEM((2240, 96), bf16),
        ],
        *bands,
        copies=6,
        vmem=16,
        cost=60 * 10**6,
    )


def sections23_body(same2, same3, other2, other3, c_own, c_sent, d_any, k2_own, k2_sent, k3_own, k3_sent, u_own, u_sent,
                    out0, out1, out2, out3, pairs, d_ref, k2, k3, u2, u3, line, base, xx, hs, p, t, base3, xx3, hs3, p3, t3, rows3, out_ref,
                    sems):
    s, h, w = (lax.axis_index(axis) for axis in AXES)
    f32, bf16 = jnp.float32, jnp.bfloat16

    @pl.when((s >= 2) & (h < 2))
    def _():
        frame = (s - 2) * 2 + w
        line[0:640] = jnp.zeros((640, 192), bf16)
        for segment, same, other in ((2, same2, other2), (3, same3, other3)):

            @pl.when(s == segment)
            def _():
                c_any = c_own if segment == 2 else c_sent
                held2, held3 = (k2_own, k3_sent) if segment == 2 else (k2_sent, k3_own)
                up2, up3 = (u_own, u_sent) if segment == 2 else (u_sent, u_own)
                start_all(
                    [
                        (same, pairs.at[w]),
                        (other, pairs.at[1 - w]),
                        (c_any, line.at[640:1280]),
                        (held2, k2),
                        (up2, u2),
                        (d_any, d_ref),
                        (held3, k3),
                        (up3.at[0:96], u3),
                    ],
                    sems,
                )

        coming = [
            pltpu.make_async_copy(a, b, sems.at[n])
            for n, (a, b) in enumerate(
                [
                    (same2, pairs.at[0]),
                    (other2, pairs.at[1]),
                    (c_own, line.at[640:1280]),
                    (k2_own, k2),
                    (u_own, u2),
                    (d_any, d_ref),
                    (k3_own, k3),
                    (u_own.at[0:96], u3),
                ]
            )
        ]
        wait_all(coming[0:3])
        for number in range(2):
            for k in range(2):
                at = 1280 + (2 * number + k) * 320
                line[at : at + 320] = pairs[number, :, k * 192 : (k + 1) * 192]

        base[...] = line[pl.ds(pl.multiple_of(frame * 320, 320), 1600), :].astype(f32)
        for dx, moved in enumerate(shifts(base[...], 16, 16)):
            xx[:, dx * 192 : (dx + 1) * 192] = moved.astype(bf16)
        coming[3].wait()
        for moment in range(3):
            total = None
            for group in range(9):
                start = (group // 3 + moment) * 320 + group % 3 * 16
                term = dot_t(xx[start : start + 288, :], k2[:, group * 576 : (group + 1) * 576])
                total = term if total is None else total + term
            inverse = lax.rsqrt(jnp.sum(total * total, axis=1, keepdims=True) / 192.0 + EPSILON)
            at = moment * 320
            hs[at : at + 288] = silu(total * inverse).astype(bf16)
            hs[moment * 320 + 288 : moment * 320 + 320] = jnp.zeros((32, 192), bf16)
        coming[4].wait()
        p[...] = dot(hs[...], u2[...])
        upsample(p, t, 16, 16, 128)

        for z in range(2):

            @pl.when(h == z)
            def _():
                blank = 0 if z == 0 else 34
                for moment in range(3):
                    to = moment * 1120 + blank * 32
                    base3[to : to + 32] = jnp.zeros((32, 96), f32)
                    for r in range(34):
                        y = r + 2 * z
                        at = moment * 640 + (y // 2) * 32
                        to = moment * 1120 + (r + 1 - z) * 32
                        base3[to : to + 32] = t[y % 2, at : at + 32, 0:96].astype(bf16).astype(f32)

        wait_all(coming[5:8])

        @pl.when(frame == 0)
        def _():
            base3[0:2240] = d_ref[...].astype(f32)

        @pl.when(frame == 1)
        def _():
            base3[0:1120] = d_ref[1120:2240].astype(f32)

        xx3[...] = jnp.zeros_like(xx3)
        for dx, moved in enumerate(shifts(base3[...], 32, 32)):
            xx3[:, dx * 128 : dx * 128 + 96] = moved.astype(bf16)
        total = None
        for group in range(9):
            start = group // 3 * 1120 + group % 3 * 32
            term = dot_t(xx3[start : start + 1056, :], k3[:, group * 384 : (group + 1) * 384])
            total = term if total is None else total + term
        inverse = lax.rsqrt(jnp.sum(total * total, axis=1, keepdims=True) / 96.0 + EPSILON)
        hs3[0:1056] = silu(total * inverse).astype(bf16)
        hs3[1056:1120] = jnp.zeros((64, 96), bf16)
        p3[...] = dot(hs3[...], u3[...])
        upsample(p3, t3, 32, 32, 128)
        for z in range(2):

            @pl.when(h == z)
            def _():
                for a in range(2):
                    for four in range(16):
                        parts = [
                            t3[a, pl.ds(z * 64 + four * 4 + n, 32, stride=64), :][:, 0:96] for n in range(4)
                        ]
                        row = jnp.concatenate(parts, axis=1)
                        for n in range(3):
                            rows3[four * 3 + n, pl.ds(a, 32, stride=2), :] = row[:, n * 128 : (n + 1) * 128]
        for tile in range(48):
            lane = tile % 24 * 128
            for n in range(2):
                part = rows3[tile, n * 32 : n * 32 + 32, :].astype(bf16)
                out_ref[n * 2 + tile // 24, :, lane : lane + 128] = part

        wait_all(start_all([(out_ref.at[n], target) for n, target in enumerate((out0, out1, out2, out3))], sems))


def sections23(received, c, c_sent, d, kernels):
    f32, bf16 = jnp.float32, jnp.bfloat16
    return kernel_call(
        sections23_body,
        tuple([jax.ShapeDtypeStruct((32, 3072), bf16)] * 4),
        [
            pltpu.VMEM((2, 320, 384), bf16),
            pltpu.VMEM((2240, 96), bf16),
            pltpu.VMEM((192, 5184), bf16),
            pltpu.VMEM((96, 3456), bf16),
            pltpu.VMEM((192, 1152), bf16),
            pltpu.VMEM((96, 1152), bf16),
            pltpu.VMEM((2560, 192), bf16),
            pltpu.VMEM((1600, 192), f32),
            pltpu.VMEM((1600, 576), bf16),
            pltpu.VMEM((960, 192), bf16),
            pltpu.VMEM((960, 1152), f32),
            pltpu.VMEM((2, 1920, 128), f32),
            pltpu.VMEM((3360, 96), f32),
            pltpu.VMEM((3360, 384), bf16),
            pltpu.VMEM((1120, 96), bf16),
            pltpu.VMEM((1120, 1152), f32),
            pltpu.VMEM((2, 2240, 128), f32),
            pltpu.VMEM((48, 64, 128), f32),
            pltpu.VMEM((4, 32, 3072), bf16),
        ],
        *received, c, c_sent, d, *kernels,
        copies=8,
        vmem=44,
    )


def beside_body(near_any, far_any, out_any, near, far, out, sems):
    wait_all(start_all([(near_any, near), (far_any, far)], sems))
    out[:, 0:432] = near[...]
    out[:, 432:864] = far[...]
    wait_all(start_all([(out, out_any)], sems))


def beside(near, far):
    shape, bf16 = (192, 864), jnp.bfloat16
    return kernel_call(
        beside_body,
        jax.ShapeDtypeStruct(shape, bf16),
        [pltpu.VMEM((192, 432), bf16), pltpu.VMEM((192, 432), bf16), pltpu.VMEM(shape, bf16)],
        near, far,
        copies=2,
        cost=15000000,
    )


def blank_body(*refs):
    pass


def blank(some, shapes):
    return kernel_call(blank_body, [jax.ShapeDtypeStruct(shape, jnp.bfloat16) for shape in shapes], [], some, copies=1)


LATER = ((192, 5184), (96, 3456), (192, 1152), (192, 5184), (96, 3456), (192, 1152), (640, 192), (640, 192), (2240, 96))


def sections01(latent, cache_a, cache_b, cache_c, cache_d, k, u):
    u_far = send(u, [((s_, h_ + 2, w_), (s_, h_, w_)) for s_ in (0, 1) for h_ in range(2) for w_ in range(2)])
    k_x, k_z = send(k, square((1,), 0, 1)), send(k, square((1,), 1, 0))
    gathered = lax.all_to_all(
        spread_tiles(latent, cache_a, cache_b), ("ha", "wa"), split_axis=0, concat_axis=0, tiled=True
    )
    ups = beside(u, u_far)
    u_z, u_x, u_d = (send(ups, square((0, 1), dh, dw)) for dh, dw in ((1, 0), (0, 1), (1, 1)))
    partial_sums = conv0(gathered, k)
    partial_sums, k_x, k_z = lax.optimization_barrier((partial_sums, k_x, k_z))
    k_d = send(k_z, square((1,), 0, 1))
    partials = lax.all_to_all(partial_sums, ("ha", "wa"), split_axis=0, concat_axis=0, tiled=True)
    taps = join((ups, u_z, u_x, u_d))
    risen = up0(partials, taps)
    given = send(risen, [((0, h_, w_), (1, h_, w_)) for h_ in range(2) for w_ in range(2)])
    out1 = section1(given, gathered, (k, k_z, k_x, k_d), taps)
    return (out1, *blank(k, LATER))


def before_sections23(latent, cache_a, cache_b, cache_c, cache_d, k, u):
    own = jnp.concatenate([cache_c.reshape(16, 1536), cache_d.reshape(32, 1536)], axis=0)
    bands = [own] + [
        send(own, [((2, h_ + n, w_ ^ dw), (2, h_, w_)) for h_ in range(2) for w_ in range(2)])
        for n in range(3)
        for dw in range(2)
        if n + dw
    ]
    picked = pick(k, u)
    picked_x, picked_z, picked_d = (send(picked, square((2, 3), dh, dw)) for dh, dw in ((0, 1), (1, 0), (1, 1)))
    k2, k3, u23 = merge((picked, picked_z, picked_x, picked_d))
    pairs = [((s_, h_, w_), (s_ ^ 1, h_, w_)) for s_ in (2, 3) for h_ in range(2) for w_ in range(2)]
    rise, fall = [pair for pair in pairs if pair[0][0] == 2], [pair for pair in pairs if pair[0][0] == 3]
    c, d = caches(bands)
    c_sent, k2_sent, k3_sent, u_sent = send(c, rise), send(k2, rise), send(k3, fall), send(u23, pairs)
    return (*blank(k, ((320, 384),)), k2, k3, u23, k2_sent, k3_sent, u_sent, c, c_sent, d)


def relay(latent, cache_a, cache_b, cache_c, cache_d, conv_pack, up_pack):
    s, h, w = (lax.axis_index(axis) for axis in AXES)
    k, u = conv_pack[0].T, up_pack[0]
    out1, k2, k3, u23, k2_sent, k3_sent, u_sent, c, c_sent, d = lax.cond(
        s < 2, sections01, before_sections23, latent, cache_a, cache_b, cache_c, cache_d, k, u
    )
    received = [
        send(out1, [((1, h_, w_), (s_, h_, w_ ^ dw)) for h_ in range(2) for w_ in range(s_ - 1)])
        for dw in range(2)
        for s_ in (2, 3)
    ]
    blocks = sections23(received, c, c_sent, d, (k2, k2_sent, k3, k3_sent, u23, u_sent))

    arrived = [
        send(
            blocks[2 * n + half],
            [((2 + c_, z, x), (2 * c_ + x, 2 * z + n, half)) for c_ in range(2) for z in range(2) for x in range(2)],
        )
        for n in range(2)
        for half in range(2)
    ]
    lower_half = jnp.where(w == 0, arrived[2], arrived[3])
    upper_half = jnp.where(w == 0, arrived[0], arrived[1])
    return jnp.where(h % 2 == 0, upper_half, lower_half)[None]


def solution(mesh):
    in_specs = (
        P(None, "ha", "wa"),
        P(None, "ha", "wa"),
        P(None, "ha", "wa"),
        P(None, "ha", "wa"),
        P(None, "ha", "wa"),
        P("segment", "ha", "wa"),
        P("segment", "wa", "ha"),
    )
    out_specs = P("segment", "ha", "wa")
    sizes = tuple(mesh.shape[axis] for axis in AXES)
    program = relay if sizes == (4, 4, 2) else per_device
    return jax.shard_map(
        program, mesh=mesh, in_specs=in_specs, out_specs=out_specs, check_vma=False
    )
```

```python
from functools import partial

import jax
import jax.numpy as jnp
from jax import lax
from jax.experimental import pallas as pl
from jax.experimental.pallas import tpu as pltpu
from jax.sharding import PartitionSpec as P

WIDE = 384
MID = 192
NARROW = 96


EPSILON = 1e-06


def shortened(array):

    def short(part):
        return part.astype(jnp.bfloat16) if part.dtype == jnp.float32 else part

    return jax.tree.map(short, array)


def passed_along(value, axis, steps):
    count = lax.axis_size(axis)
    initial, last = (max(0, -steps), min(count, count - steps))
    return lax.ppermute(value, axis, [(source, source + steps) for source in range(initial, last)])


def layer_table():
    return ((WIDE, WIDE, MID), (MID, WIDE, MID), (MID, MID, NARROW), (NARROW, NARROW, NARROW))


def round_up(amount):
    return -(-amount // 128) * 128


def volume(target):
    amount = 1
    for extent in target:
        amount = amount * extent
    return amount


def flat_pad(tensor, length):
    leading = tensor.shape[0]
    packed = tensor.reshape(leading, -1)
    return jnp.pad(packed, ((0, 0), (0, length - packed.shape[1])))


def reshaped(packed, target):
    return packed[:, : volume(target)].reshape((packed.shape[0],) + tuple(target))


def add_rows(tensor, from_above, from_below):
    leading, height, width, channels = tensor.shape
    upper = reshaped(from_above, (1, width, channels))
    lower = reshaped(from_below, (1, width, channels))
    return jnp.concatenate([upper, tensor, lower], axis=1)


def add_cols(tensor, from_left, from_right):
    leading, height, width, channels = tensor.shape
    before = reshaped(from_left, (height, 1, channels))
    after = reshaped(from_right, (height, 1, channels))
    return jnp.concatenate([before, tensor, after], axis=2)


def trade_rows(upper_rim, bottom):
    return (
        jax.tree.map(
            lambda part, own: part.astype(own.dtype),
            passed_along(shortened(bottom), "ha", 1),
            bottom,
        ),
        jax.tree.map(
            lambda part, own: part.astype(own.dtype),
            passed_along(shortened(upper_rim), "ha", -1),
            upper_rim,
        ),
    )


def trade_cols(left_rim, right_rim):
    return (
        jax.tree.map(
            lambda part, own: part.astype(own.dtype),
            passed_along(shortened(right_rim), "wa", 1),
            right_rim,
        ),
        jax.tree.map(
            lambda part, own: part.astype(own.dtype),
            passed_along(shortened(left_rim), "wa", -1),
            left_rim,
        ),
    )


def causal_conv(stacked, kernel):
    result = lax.conv_general_dilated(
        stacked[None],
        kernel,
        (1, 1, 1),
        "VALID",
        dimension_numbers=("NDHWC", "DHWIO", "NDHWC"),
        preferred_element_type=jnp.float32,
    )
    return result[0, 0]


def activate(conv_sum):
    inverse = lax.rsqrt(jnp.mean(conv_sum * conv_sum, axis=-1, keepdims=True) + EPSILON)
    return jax.nn.silu(conv_sum * inverse).astype(jnp.bfloat16)


def upsample_conv(hidden_ext, kernel):
    expanded = jnp.repeat(jnp.repeat(hidden_ext, 2, axis=0), 2, axis=1)[1:-1, 1:-1]
    result = lax.conv_general_dilated(
        expanded[None],
        kernel,
        (1, 1),
        "VALID",
        dimension_numbers=("NHWC", "HWIO", "NHWC"),
        preferred_element_type=jnp.float32,
    )
    return result[0].astype(jnp.bfloat16)


def per_device(latent, cache_a, cache_b, cache_c, cache_d, conv_pack, up_pack):
    frames = latent.shape[0]
    tile_rows = latent.shape[1]
    tile_cols = latent.shape[2] // WIDE
    layers = layer_table()
    section = lax.axis_index("segment")
    segments = lax.axis_size("segment")
    final_segment = segments - 1
    input_shapes = [
        (tile_rows << level, tile_cols << level, layers[level][0]) for level in range(4)
    ]
    mid_shapes = [(tile_rows << level, tile_cols << level, layers[level][1]) for level in range(4)]
    out_shapes = [
        (tile_rows << level + 1, tile_cols << level + 1, layers[level][2]) for level in range(4)
    ]
    ext_shapes = [(target[0] + 2, target[1] + 2, target[2]) for target in input_shapes]
    all_shapes = input_shapes + mid_shapes
    row_length = round_up(max((target[1] * target[2] for target in all_shapes)))
    column_length = round_up(max(((target[0] + 2) * target[2] for target in all_shapes)))
    size_input = round_up(max((volume(target) for target in input_shapes)))
    size_middle = round_up(max((volume(target) for target in mid_shapes)))
    size_extended = round_up(max((volume(target) for target in ext_shapes)))
    size_output = round_up(max((volume(target) for target in out_shapes)))
    final_shape = out_shapes[3]
    final_count = volume(final_shape)
    conv_rows, up_rows = (
        lax.all_gather(conv_pack, "ha", axis=1, tiled=True),
        lax.all_gather(up_pack, "ha", axis=2, tiled=True),
    )
    conv_all, up_all = (
        lax.all_gather(conv_rows, "wa", axis=2, tiled=True),
        lax.all_gather(up_rows, "wa", axis=1, tiled=True),
    )

    def conv_kernel(level):
        width_in, width_mid, width_out = layers[level]
        columns = conv_all[0, : 27 * width_in, :: WIDE // width_mid]
        return columns.reshape(3, 3, 3, width_in, columns.shape[1])

    def up_kernel(level):
        width_in, width_mid, width_out = layers[level]
        rows_used = up_all[0, :: WIDE // width_mid, : 9 * width_out]
        return rows_used.reshape(width_mid, 3, 3, width_out).transpose(1, 2, 0, 3)

    conv_kernels = [conv_kernel(level) for level in range(4)]
    up_kernels = [up_kernel(level) for level in range(4)]

    def row_rims(packed, shapes):

        def rows_branch(level, packed):
            tensor = reshaped(packed, shapes[level])
            return (flat_pad(tensor[:, :1], row_length), flat_pad(tensor[:, -1:], row_length))

        upper_rim, bottom = lax.switch(
            section, [partial(rows_branch, level) for level in range(4)], packed
        )
        return trade_rows(upper_rim, bottom)

    def extend(packed, shapes):
        from_above, from_below = row_rims(packed, shapes)

        def cols_branch(level, packed, from_above, from_below):
            tensor = add_rows(reshaped(packed, shapes[level]), from_above, from_below)
            return (
                flat_pad(tensor[:, :, :1], column_length),
                flat_pad(tensor[:, :, -1:], column_length),
            )

        left_rim, right_rim = lax.switch(
            section,
            [partial(cols_branch, level) for level in range(4)],
            packed,
            from_above,
            from_below,
        )
        from_left, from_right = trade_cols(left_rim, right_rim)
        return (from_above, from_below, from_left, from_right)

    def assemble(packed, target, rims):
        tensor = add_rows(reshaped(packed, target), rims[0], rims[1])
        return add_cols(tensor, rims[2], rims[3])

    caches = (cache_a, cache_b, cache_c, cache_d)

    def cache_branch(level):
        return flat_pad(caches[level], size_input)

    cached = lax.switch(section, [partial(cache_branch, level) for level in range(4)])
    cache_rims = extend(cached, input_shapes)

    def store_branch(level, packed, rims):
        return flat_pad(assemble(packed, input_shapes[level], rims), size_extended)

    history = lax.switch(
        section, [partial(store_branch, level) for level in range(4)], cached, cache_rims
    )
    finished = jnp.zeros((frames, final_shape[0], final_shape[1] * final_shape[2]), jnp.bfloat16)
    stream = jnp.zeros((1, size_input), jnp.bfloat16)
    for moment in range(frames + segments - 1):
        if moment == 0:
            incoming = stream
        else:
            incoming = jax.tree.map(
                lambda part, own: part.astype(own.dtype),
                passed_along(shortened(stream), "segment", 1),
                stream,
            )
        frame_id = moment - section
        active = (frame_id >= 0) & (frame_id < frames)
        chosen = jnp.clip(frame_id, 0, frames - 1)
        picked = lax.dynamic_index_in_dim(latent, chosen, 0, keepdims=True)
        current = jnp.where(section == 0, flat_pad(picked, size_input), incoming)
        branch_id = jnp.where(active, section, 4)
        rims = extend(current, input_shapes)

        def conv_branch(level, current, history, rims):
            window = assemble(current, input_shapes[level], rims)
            earlier = reshaped(history, ext_shapes[level])
            hidden = activate(
                causal_conv(jnp.concatenate([earlier, window], axis=0), conv_kernels[level])
            )
            return (flat_pad(hidden[None], size_middle), flat_pad(window, size_extended))

        def spare_conv(current, history, rims):
            return (
                jnp.zeros((1, size_middle), jnp.bfloat16),
                jnp.zeros((1, size_extended), jnp.bfloat16),
            )

        hidden, window = lax.switch(
            branch_id,
            [partial(conv_branch, level) for level in range(4)] + [spare_conv],
            current,
            history,
            rims,
        )
        hidden_rims = extend(hidden, mid_shapes)

        def up_branch(level, hidden, hidden_rims):
            expanded = assemble(hidden, mid_shapes[level], hidden_rims)[0]
            return flat_pad(upsample_conv(expanded, up_kernels[level])[None], size_output)

        def spare_up(hidden, hidden_rims):
            return jnp.zeros((1, size_output), jnp.bfloat16)

        produced = lax.switch(
            branch_id,
            [partial(up_branch, level) for level in range(4)] + [spare_up],
            hidden,
            hidden_rims,
        )
        shifted = jnp.concatenate([history[1:], window], axis=0)
        history = jnp.where(active, shifted, history)
        stream = produced[:, :size_input]
        if moment >= final_segment:
            finished_id = moment - final_segment
            picture = produced[:, :final_count].reshape(
                1, final_shape[0], final_shape[1] * final_shape[2]
            )
            finished = finished.at[finished_id].set(picture[0])
    collected = lax.all_to_all(finished, "segment", split_axis=0, concat_axis=0, tiled=True)
    per_segment = frames // segments
    own_frame = collected[final_segment * per_segment : (final_segment + 1) * per_segment]
    return own_frame


AXES = ("segment", "ha", "wa")
MIB = 1024 * 1024


def place(s, h, w):
    return (s * 4 + h) * 2 + w


def send(value, pairs):
    return lax.ppermute(value, AXES, [(place(*a), place(*b)) for a, b in pairs])


def square(segments, dh, dw):
    return [
        ((s, h, w), (s, h ^ dh, w ^ dw)) for s in segments for h in range(2) for w in range(2)
    ]


def kernel_call(body, out_shape, scratch, *args, copies=0, vmem=16, cost=1000, place=pl.ANY):
    return pl.pallas_call(
        body,
        out_shape=out_shape,
        in_specs=[pl.BlockSpec(memory_space=place)] * len(args),
        out_specs=jax.tree.map(lambda _: pl.BlockSpec(memory_space=pl.ANY), out_shape),
        scratch_shapes=scratch + [pltpu.SemaphoreType.DMA((copies,))],
        compiler_params=pltpu.CompilerParams(vmem_limit_bytes=vmem * MIB),
        cost_estimate=pl.CostEstimate(flops=1000 * cost, bytes_accessed=1000, transcendentals=0),
    )(*args)


def start_all(pairs, sems, first=0):
    copies = [pltpu.make_async_copy(a, b, sems.at[first + n]) for n, (a, b) in enumerate(pairs)]
    for copy in copies:
        copy.start()
    return copies


def wait_all(copies):
    for copy in copies:
        copy.wait()


def dot(a, b):
    return jnp.dot(a, b, preferred_element_type=jnp.float32)


def dot_t(a, b):
    return lax.dot_general(a, b, (((1,), (1,)), ((), ())), preferred_element_type=jnp.float32)


def index_of(shape):
    return lax.broadcasted_iota(jnp.int32, shape, 0)


def silu(v):
    return v / (1.0 + jnp.exp(-v))


def shifts(base, pitch, width):
    n = base.shape[0]
    left, right = pltpu.roll(base, 1, 0), pltpu.roll(base, n - 1, 0)
    if pitch == width:
        column = index_of(base.shape) % pitch
        left = jnp.where(column == 0, 0.0, left)
        right = jnp.where(column == width - 1, 0.0, right)
    return left, base, right


def upsample(p_ref, t_ref, pitch, width, lanes):
    n = p_ref.shape[0]
    blocks = lanes // 128
    column = index_of((n, 128)) % pitch
    for block in range(blocks):

        def tap(dy, dx):
            at = (dy * 3 + dx) * lanes + block * 128
            return p_ref[:, at : at + 128]

        for b in range(2):
            rows = []
            for dy in range(3):
                middle = tap(dy, 1)
                if b == 0:
                    far = pltpu.roll(tap(dy, 0), 1, 0)
                    if pitch == width:
                        far = jnp.where(column == 0, 0.0, far)
                    rows.append(far + middle + tap(dy, 2))
                else:
                    far = pltpu.roll(tap(dy, 2), n - 1, 0)
                    if pitch == width:
                        far = jnp.where(column == width - 1, 0.0, far)
                    rows.append(tap(dy, 0) + middle + far)
            t_ref[block, pl.ds(b, n, stride=2), :] = pltpu.roll(rows[0], pitch, 0) + rows[1] + rows[2]
            t_ref[blocks + block, pl.ds(b, n, stride=2), :] = (
                rows[0] + rows[1] + pltpu.roll(rows[2], n - pitch, 0)
            )


def tiles_body(latent_any, a_any, b_any, out_any, latent, a, b, rows, out, sems):
    wait_all(start_all([(latent_any, latent), (a_any, a), (b_any, b)], sems))

    @pl.when(lax.axis_index("segment") == 0)
    def _():
        for frame in range(4):
            rows[frame * 2 : frame * 2 + 2] = latent[frame].astype(jnp.float32)
        for frame in range(2):
            rows[8 + frame * 2 : 10 + frame * 2] = a[frame].astype(jnp.float32)

    @pl.when(lax.axis_index("segment") > 0)
    def _():
        for frame in range(2):
            rows[frame * 4 : frame * 4 + 4] = b[frame].astype(jnp.float32)
        rows[8:12] = jnp.zeros((4, 768), jnp.float32)

    out[...] = rows[...].astype(jnp.bfloat16)
    wait_all(start_all([(out, out_any.at[n]) for n in range(8)], sems))


def spread_tiles(latent, cache_a, cache_b):
    bf16 = jnp.bfloat16
    return kernel_call(
        tiles_body,
        jax.ShapeDtypeStruct((8, 12, 768), bf16),
        [
            pltpu.VMEM((4, 2, 768), bf16),
            pltpu.VMEM((2, 2, 768), bf16),
            pltpu.VMEM((2, 4, 768), bf16),
            pltpu.VMEM((12, 768), jnp.float32),
            pltpu.VMEM((12, 768), bf16),
        ],
        latent, cache_a, cache_b,
        copies=8,
    )


def conv0_body(g_any, k_any, out_any, g_ref, k_ref, gf, base, xx, acc, buf, out_ref, sems):
    s, h = lax.axis_index("segment"), lax.axis_index("ha")

    @pl.when(s == 0)
    def _():
        coming = start_all([(g_any, g_ref), (k_any, k_ref)], sems)
        base[...] = jnp.zeros_like(base)
        coming[0].wait()
        gf[...] = g_ref[...].astype(jnp.float32)
        for frame in range(6):
            for hh in range(4):
                for ww in range(2):
                    for r in range(2):
                        row = 8 + frame * 2 + r if frame < 2 else (frame - 2) * 2 + r
                        for c in range(2):
                            at = frame * 160 + (1 + 2 * hh + r) * 16 + 2 * ww + c
                            base[at : at + 1, :] = gf[hh * 2 + ww, row : row + 1, c * 384 : (c + 1) * 384]
        for dx, moved in enumerate(shifts(base[...], 16, 4)):
            xx[dx] = moved.astype(jnp.bfloat16)
        coming[1].wait()
        for part in range(4):

            @pl.when(h == part)
            def _():
                total = None
                at, end = part * 2592, part * 2592 + 2592
                while at < end:
                    tap, c0 = divmod(at, 384)
                    c1 = min(384, c0 + end - at)
                    dt, dy, dx = tap // 9, tap // 3 % 3, tap % 3
                    start = dt * 160 + dy * 16
                    k0 = at - part * 2592
                    term = dot_t(xx[dx, start : start + 608, c0:c1], k_ref[:, k0 : k0 + c1 - c0])
                    total = term if total is None else total + term
                    at += c1 - c0
                acc[...] = total

        for frame in range(4):
            for r in range(8):
                to, at = (frame * 8 + r) * 4, frame * 160 + r * 16
                buf[to : to + 4, :] = acc[at : at + 4, :]
        out_ref[0:128, :] = buf[:, 0:128].astype(jnp.bfloat16)
        tail = jnp.concatenate([buf[0:64, 128:192], buf[64:128, 128:192]], axis=1)
        out_ref[128:192, :] = tail.astype(jnp.bfloat16)
        wait_all(start_all([(out_ref, out_any.at[n]) for n in range(8)], sems))


def conv0(gathered, k):
    f32, bf16 = jnp.float32, jnp.bfloat16
    return kernel_call(
        conv0_body,
        jax.ShapeDtypeStruct((8, 192, 128), bf16),
        [
            pltpu.VMEM((8, 12, 768), bf16),
            pltpu.VMEM((192, 2592), bf16),
            pltpu.VMEM((8, 12, 768), f32),
            pltpu.VMEM((960, 384), f32),
            pltpu.VMEM((3, 960, 384), bf16),
            pltpu.VMEM((608, 192), f32),
            pltpu.VMEM((128, 192), f32),
            pltpu.VMEM((192, 128), bf16),
        ],
        gathered, k,
        copies=8,
        cost=20 * 10**6,
    )


def join_body(own, nz, nx, nd, mine_any, other_any, cat, taps, sems):
    s, h = lax.axis_index("segment"), lax.axis_index("ha")

    @pl.when((s < 2) & (h < 2))
    def _():
        sending = []
        for half, (near, far, target) in enumerate(((own, nz, mine_any), (nx, nd, other_any))):
            for z in range(2):

                @pl.when(h == z)
                def _():
                    for first, pieces in ((z, near), (1 - z, far)):
                        for n in range(2):
                            at = (first + 2 * n) * 432
                            cat[:, at : at + 432] = pieces[:, n * 432 : (n + 1) * 432]

            for tap in range(9):
                taps[half, :, tap * 256 : tap * 256 + 192] = cat[:, tap * 192 : (tap + 1) * 192]
                taps[half, :, tap * 256 + 192 : (tap + 1) * 256] = jnp.zeros((192, 64), jnp.bfloat16)
            sending += start_all([(taps.at[half], target)], sems, half)
        wait_all(sending)


def join(pieces):
    bf16 = jnp.bfloat16
    return kernel_call(
        join_body,
        (jax.ShapeDtypeStruct((192, 2304), bf16), jax.ShapeDtypeStruct((192, 2304), bf16)),
        [pltpu.VMEM((192, 1728), bf16), pltpu.VMEM((2, 192, 2304), bf16)],
        *pieces,
        copies=2,
        vmem=62,
        cost=20 * 10**6,
        place=pltpu.VMEM,
    )


def up0_body(*refs):
    y_any, taps_any, out_any = refs[0], refs[1:3], refs[3]
    y, taps, hbuf, hs, p, t, out_ref, sems = refs[4:]
    s, h, w = (lax.axis_index(axis) for axis in AXES)

    @pl.when((s == 0) & (h < 2))
    def _():
        coming = start_all([(y_any, y)], sems)
        rising = start_all([(a, taps.at[n]) for n, a in enumerate(taps_any)], sems, 1)
        wait_all(coming)
        halves = []
        for side in range(2):
            total = y[side].astype(jnp.float32)
            for hh in range(1, 4):
                total = total + y[hh * 2 + side].astype(jnp.float32)
            tail = jnp.concatenate([total[128:192, 0:64], total[128:192, 64:128]], axis=0)
            halves.append(jnp.concatenate([total[0:128], tail], axis=1))
        squares = sum(jnp.sum(half * half, axis=1, keepdims=True) for half in halves)
        inverse = lax.rsqrt(squares / 384.0 + EPSILON)
        active = [silu(half * inverse) for half in halves]
        hs[...] = jnp.zeros_like(hs)
        for k in range(2):
            hbuf[...] = jnp.where(w == k, active[0], active[1])
            for frame in range(4):
                for r in range(8):
                    to, at = frame * 72 + r * 8, (frame * 8 + r) * 4
                    hs[k, to : to + 4, :] = hbuf[at : at + 4, :]
        wait_all(rising)
        p[...] = dot(hs[0].astype(jnp.bfloat16), taps[0]) + dot(hs[1].astype(jnp.bfloat16), taps[1])
        upsample(p, t, 8, 4, 256)
        column = index_of((16, 192))
        out_ref[...] = jnp.zeros_like(out_ref)
        for z in range(2):

            @pl.when(h == z)
            def _():
                for frame in range(4):
                    for r in range(11):
                        y = r + 5 * z
                        at = frame * 144 + (y // 2) * 16
                        to = frame * 192 + (r + 1 - z) * 16
                        for lane, count in ((0, 128), (128, 64)):
                            row = t[y % 2 * 2 + lane // 128, at : at + 16, 0:count]
                            row = jnp.where(column[:, 0:count] < 8, row, 0.0)
                            out_ref[to : to + 16, lane : lane + count] = row.astype(jnp.bfloat16)

        wait_all(start_all([(out_ref, out_any)], sems))


def up0(partials, ups):
    f32, bf16 = jnp.float32, jnp.bfloat16
    return kernel_call(
        up0_body,
        jax.ShapeDtypeStruct((768, 192), bf16),
        [
            pltpu.VMEM((8, 192, 128), bf16),
            pltpu.VMEM((2, 192, 2304), bf16),
            pltpu.VMEM((128, 192), f32),
            pltpu.VMEM((2, 288, 192), f32),
            pltpu.VMEM((288, 2304), f32),
            pltpu.VMEM((4, 576, 128), f32),
            pltpu.VMEM((768, 192), bf16),
        ],
        partials, *ups,
        copies=3,
        vmem=62,
    )


def group_rows(first, second, group):
    at, end = group * 576, group * 576 + 576
    if end <= 2592:
        return first[:, at:end]
    if at >= 2592:
        return second[:, at - 2592 : end - 2592]
    return jnp.concatenate([first[:, at:2592], second[:, 0 : end - 2592]], axis=1)


def section1_body(x_any, g_any, *refs):
    kernels_any, taps_any, out_any = refs[0:4], refs[4:6], refs[6]
    x_ref, g_ref = refs[7:9]
    k_own, k_z, k_x, k_d = refs[9:13]
    gf, full, base, xx, acc, hs, taps, p, t, out_ref, sems = refs[13:]
    s, h, w = (lax.axis_index(axis) for axis in AXES)

    @pl.when((s == 1) & (h < 2))
    def _():
        coming = start_all([(x_any, x_ref), (g_any, g_ref)], sems)
        arriving = start_all(list(zip(kernels_any, (k_own, k_z, k_x, k_d))), sems, 2)
        rising = start_all([(a, taps.at[n]) for n, a in enumerate(taps_any)], sems, 6)
        wait_all(coming)

        @pl.when(w == 0)
        def _():
            gf[...] = g_ref[...].astype(jnp.float32)
            full[...] = jnp.zeros_like(full)
            for frame in range(2):
                for hh in range(4):
                    for ww in range(2):
                        for r in range(4):
                            for c in range(4):
                                row = frame * 4 + r
                                at = frame * 288 + (1 + hh * 4 + r) * 16 + ww * 4 + c
                                full[at : at + 1, :] = gf[hh * 2 + ww, row : row + 1, c * 192 : (c + 1) * 192]
            for frame in range(2):
                start = pl.multiple_of(frame * 288 + h * 96, 32)
                base[frame * 192 : (frame + 1) * 192] = full[pl.ds(start, 192), :]
            base[384:768] = x_ref[0:384].astype(jnp.float32)

        @pl.when(w == 1)
        def _():
            base[...] = x_ref[...].astype(jnp.float32)

        for dx, moved in enumerate(shifts(base[...], 16, 8)):
            xx[:, dx * 192 : (dx + 1) * 192] = moved.astype(jnp.bfloat16)
        wait_all(arriving)
        for z in range(2):

            @pl.when(h == z)
            def _():
                for k, (mine, other) in enumerate(((k_own, k_z), (k_x, k_d))):
                    first, second = (mine, other) if z == 0 else (other, mine)
                    total = None
                    for group in range(9):
                        start = group // 3 * 192 + group % 3 * 16
                        term = dot_t(xx[start : start + 352, :], group_rows(first, second, group))
                        total = term if total is None else total + term
                    acc[k] = total

        squares = sum(jnp.sum(acc[k] * acc[k], axis=1, keepdims=True) for k in range(2))
        inverse = lax.rsqrt(squares / 384.0 + EPSILON)
        index = index_of((352, 192))
        keep = (index % 192 < 160) & (index % 16 < 8)
        for k in range(2):
            hs[k, 0:352] = jnp.where(keep, silu(acc[k] * inverse), 0.0).astype(jnp.bfloat16)
            hs[k, 352:384] = jnp.zeros((32, 192), jnp.bfloat16)
        wait_all(rising)
        p[...] = dot(hs[0], taps[0]) + dot(hs[1], taps[1])
        upsample(p, t, 16, 8, 256)
        out_ref[...] = jnp.zeros_like(out_ref)
        for z in range(2):

            @pl.when(h == z)
            def _():
                for frame in range(2):
                    for r in range(19):
                        y = r + z
                        at = frame * 384 + (y // 2) * 32
                        to = (r + 1 - z) * 16
                        for lane, count in ((0, 128), (128, 64)):
                            row = t[y % 2 * 2 + lane // 128, at : at + 16, 0:count].astype(jnp.bfloat16)
                            lane0 = frame * 192 + lane
                            out_ref[to : to + 16, lane0 : lane0 + count] = row

        wait_all(start_all([(out_ref, out_any)], sems))


def section1(frames, gathered, kernels, ups):
    f32, bf16 = jnp.float32, jnp.bfloat16
    return kernel_call(
        section1_body,
        jax.ShapeDtypeStruct((320, 384), bf16),
        [
            pltpu.VMEM((768, 192), bf16),
            pltpu.VMEM((8, 12, 768), bf16),
            *[pltpu.VMEM((192, 2592), bf16)] * 4,
            pltpu.VMEM((8, 12, 768), f32),
            pltpu.VMEM((576, 192), f32),
            pltpu.VMEM((768, 192), f32),
            pltpu.VMEM((768, 576), bf16),
            pltpu.VMEM((2, 352, 192), f32),
            pltpu.VMEM((2, 384, 192), bf16),
            pltpu.VMEM((2, 192, 2304), bf16),
            pltpu.VMEM((384, 2304), f32),
            pltpu.VMEM((4, 768, 128), f32),
            pltpu.VMEM((320, 384), bf16),
        ],
        frames, gathered, *kernels, *ups,
        copies=8,
        vmem=62,
    )


def pick_body(k_any, u_any, out_any, k, u, out, sems):
    s = lax.axis_index("segment")

    @pl.when(s >= 2)
    def _():
        coming = start_all([(k_any, k), (u_any, u)], sems)
        step = jnp.where(s == 2, 2, 4)
        source = lax.broadcasted_iota(jnp.int32, (96, 192), 1)
        target = lax.broadcasted_iota(jnp.int32, (96, 192), 0)
        picked = ((source == target * step) & (target * step < 192)).astype(jnp.bfloat16)
        wait_all(coming)
        out[:, 0:2592] = dot(picked, k[...]).astype(jnp.bfloat16)
        out[:, 2688:3120] = dot(picked, u[...]).astype(jnp.bfloat16)
        wait_all(start_all([(out, out_any)], sems))


def pick(k, u):
    bf16 = jnp.bfloat16
    return kernel_call(
        pick_body,
        jax.ShapeDtypeStruct((96, 3200), bf16),
        [pltpu.VMEM((192, 2592), bf16), pltpu.VMEM((192, 432), bf16), pltpu.VMEM((96, 3200), bf16)],
        k, u,
        copies=2,
    )


def merge_body(*refs):
    pieces_any, (k2_any, k3_any, up_any) = refs[0:4], refs[4:7]
    pieces = refs[7:11]
    k2, k3, cat, up, sems = refs[11:]
    s, h = lax.axis_index("segment"), lax.axis_index("ha")
    bf16 = jnp.bfloat16

    @pl.when((s >= 2) & (h < 2))
    def _():
        wait_all(start_all(list(zip(pieces_any, pieces)), sems))
        own, nz, nx, nd = pieces
        up[...] = jnp.zeros_like(up)
        for z in range(2):
            for segment, count in ((2, 96), (3, 48)):

                @pl.when((h == z) & (s == segment))
                def _():
                    for part, (a, b) in enumerate(((own, nx), (nz, nd))):
                        at = (part ^ z) * 432
                        cat[0:count, at : at + 432] = a[0:count, 2688:3120]
                        cat[count : 2 * count, at : at + 432] = b[0:count, 2688:3120]
                        if segment == 2:
                            at = (part ^ z) * 2592
                            k2[0:96, at : at + 2592] = a[:, 0:2592]
                            k2[96:192, at : at + 2592] = b[:, 0:2592]
                    if segment == 3:
                        a, b = ((own, nx), (nz, nd))[z]
                        k3[...] = jnp.zeros_like(k3)
                        for tap in range(27):
                            k3[0:48, tap * 128 : tap * 128 + 96] = a[0:48, tap * 96 : tap * 96 + 96]
                            k3[48:96, tap * 128 : tap * 128 + 96] = b[0:48, tap * 96 : tap * 96 + 96]

        for tap in range(9):
            up[:, tap * 128 : tap * 128 + 96] = cat[:, tap * 96 : (tap + 1) * 96]
        wait_all(start_all([(up, up_any), (k2, k2_any), (k3, k3_any)], sems))


def merge(pieces):
    bf16 = jnp.bfloat16
    shapes = ((192, 5184), (96, 3456), (192, 1152))
    return kernel_call(
        merge_body,
        tuple(jax.ShapeDtypeStruct(shape, bf16) for shape in shapes),
        [
            *[pltpu.VMEM((96, 3200), bf16)] * 4,
            pltpu.VMEM((192, 5184), bf16),
            pltpu.VMEM((96, 3456), bf16),
            pltpu.VMEM((192, 864), bf16),
            pltpu.VMEM((192, 1152), bf16),
        ],
        *pieces,
        copies=4,
        vmem=12,
    )


def caches_body(*refs):
    parts, (c_any, d_any) = refs[0:6], refs[6:8]
    bands, wide, c_full, d_full, c, d, sems = refs[8:]
    s, h, w = (lax.axis_index(axis) for axis in AXES)
    f32, bf16 = jnp.float32, jnp.bfloat16

    @pl.when((s == 2) & (h < 2))
    def _():
        pairs = [(a, bands.at[n // 2, n % 2 * 48 : n % 2 * 48 + 48]) for n, a in enumerate(parts)]
        wait_all(start_all(pairs, sems))
        c_full[...] = jnp.zeros_like(c_full)
        d_full[...] = jnp.zeros_like(d_full)
        for band in range(3):
            wide[...] = bands[band].astype(f32)
            for side in range(2):
                swapped = (w + side) % 2
                for frame in range(2):
                    row = side * 48 + frame * 8
                    for column in range(8):
                        at = (frame * 26 + 1 + band * 8) * 16 + swapped * 8 + column
                        lane = column * 192
                        c_full[0, pl.ds(at, 8, stride=16), :] = wide[row : row + 8, lane : lane + 128]
                        tail = jnp.concatenate([wide[row : row + 8, lane + 128 : lane + 192]] * 2, axis=1)
                        c_full[1, pl.ds(at, 8, stride=16), :] = tail
                    row = side * 48 + 16 + frame * 16
                    for column in range(16):
                        at = (frame * 50 + 1 + band * 16) * 32 + swapped * 16 + column
                        lane = column * 96
                        part = wide[row : row + 16, lane : lane + 96]
                        part = jnp.concatenate([part, part[:, 0:32]], axis=1)
                        d_full[pl.ds(at, 16, stride=32), :] = part
        for frame in range(2):
            at = pl.multiple_of((frame * 26 + h * 6) * 16, 32)
            c[frame * 320 : frame * 320 + 320, 0:128] = c_full[0, pl.ds(at, 320), :].astype(bf16)
            c[frame * 320 : frame * 320 + 320, 128:192] = c_full[1, pl.ds(at, 320), 0:64].astype(bf16)
            at = pl.multiple_of((frame * 50 + h * 15) * 32, 32)
            d[frame * 1120 : frame * 1120 + 1120, :] = d_full[pl.ds(at, 1120), 0:96].astype(bf16)
        wait_all(start_all([(c, c_any), (d, d_any)], sems))


def caches(bands):
    f32, bf16 = jnp.float32, jnp.bfloat16
    return kernel_call(
        caches_body,
        (jax.ShapeDtypeStruct((640, 192), bf16), jax.ShapeDtypeStruct((2240, 96), bf16)),
        [
            pltpu.VMEM((3, 96, 1536), bf16),
            pltpu.VMEM((96, 1536), f32),
            pltpu.VMEM((2, 832, 128), f32),
            pltpu.VMEM((3200, 128), f32),
            pltpu.VMEM((640, 192), bf16),
            pltpu.VMEM((2240, 96), bf16),
        ],
        *bands,
        copies=6,
        vmem=16,
        cost=60 * 10**6,
    )


def sections23_body(same2, same3, other2, other3, c_own, c_sent, d_any, k2_own, k2_sent, k3_own, k3_sent, u_own, u_sent,
                    out0, out1, out2, out3, pairs, d_ref, k2, k3, u2, u3, line, base, xx, hs, p, t, base3, xx3, hs3, p3, t3, rows3, out_ref,
                    sems):
    s, h, w = (lax.axis_index(axis) for axis in AXES)
    f32, bf16 = jnp.float32, jnp.bfloat16

    @pl.when((s >= 2) & (h < 2))
    def _():
        frame = (s - 2) * 2 + w
        line[0:640] = jnp.zeros((640, 192), bf16)
        for segment, same, other in ((2, same2, other2), (3, same3, other3)):

            @pl.when(s == segment)
            def _():
                c_any = c_own if segment == 2 else c_sent
                held2, held3 = (k2_own, k3_sent) if segment == 2 else (k2_sent, k3_own)
                up2, up3 = (u_own, u_sent) if segment == 2 else (u_sent, u_own)
                start_all(
                    [
                        (same, pairs.at[w]),
                        (other, pairs.at[1 - w]),
                        (c_any, line.at[640:1280]),
                        (held2, k2),
                        (up2, u2),
                        (d_any, d_ref),
                        (held3, k3),
                        (up3.at[0:96], u3),
                    ],
                    sems,
                )

        coming = [
            pltpu.make_async_copy(a, b, sems.at[n])
            for n, (a, b) in enumerate(
                [
                    (same2, pairs.at[0]),
                    (other2, pairs.at[1]),
                    (c_own, line.at[640:1280]),
                    (k2_own, k2),
                    (u_own, u2),
                    (d_any, d_ref),
                    (k3_own, k3),
                    (u_own.at[0:96], u3),
                ]
            )
        ]
        wait_all(coming[0:3])
        for number in range(2):
            for k in range(2):
                at = 1280 + (2 * number + k) * 320
                line[at : at + 320] = pairs[number, :, k * 192 : (k + 1) * 192]

        base[...] = line[pl.ds(pl.multiple_of(frame * 320, 320), 1600), :].astype(f32)
        for dx, moved in enumerate(shifts(base[...], 16, 16)):
            xx[:, dx * 192 : (dx + 1) * 192] = moved.astype(bf16)
        coming[3].wait()
        for moment in range(3):
            total = None
            for group in range(9):
                start = (group // 3 + moment) * 320 + group % 3 * 16
                term = dot_t(xx[start : start + 288, :], k2[:, group * 576 : (group + 1) * 576])
                total = term if total is None else total + term
            inverse = lax.rsqrt(jnp.sum(total * total, axis=1, keepdims=True) / 192.0 + EPSILON)
            at = moment * 320
            hs[at : at + 288] = silu(total * inverse).astype(bf16)
            hs[moment * 320 + 288 : moment * 320 + 320] = jnp.zeros((32, 192), bf16)
        coming[4].wait()
        p[...] = dot(hs[...], u2[...])
        upsample(p, t, 16, 16, 128)

        for z in range(2):

            @pl.when(h == z)
            def _():
                blank = 0 if z == 0 else 34
                for moment in range(3):
                    to = moment * 1120 + blank * 32
                    base3[to : to + 32] = jnp.zeros((32, 96), f32)
                    for r in range(34):
                        y = r + 2 * z
                        at = moment * 640 + (y // 2) * 32
                        to = moment * 1120 + (r + 1 - z) * 32
                        base3[to : to + 32] = t[y % 2, at : at + 32, 0:96].astype(bf16).astype(f32)

        wait_all(coming[5:8])

        @pl.when(frame == 0)
        def _():
            base3[0:2240] = d_ref[...].astype(f32)

        @pl.when(frame == 1)
        def _():
            base3[0:1120] = d_ref[1120:2240].astype(f32)

        xx3[...] = jnp.zeros_like(xx3)
        for dx, moved in enumerate(shifts(base3[...], 32, 32)):
            xx3[:, dx * 128 : dx * 128 + 96] = moved.astype(bf16)
        total = None
        for group in range(9):
            start = group // 3 * 1120 + group % 3 * 32
            term = dot_t(xx3[start : start + 1056, :], k3[:, group * 384 : (group + 1) * 384])
            total = term if total is None else total + term
        inverse = lax.rsqrt(jnp.sum(total * total, axis=1, keepdims=True) / 96.0 + EPSILON)
        hs3[0:1056] = silu(total * inverse).astype(bf16)
        hs3[1056:1120] = jnp.zeros((64, 96), bf16)
        p3[...] = dot(hs3[...], u3[...])
        upsample(p3, t3, 32, 32, 128)
        for z in range(2):

            @pl.when(h == z)
            def _():
                for a in range(2):
                    for four in range(16):
                        parts = [
                            t3[a, pl.ds(z * 64 + four * 4 + n, 32, stride=64), :][:, 0:96] for n in range(4)
                        ]
                        row = jnp.concatenate(parts, axis=1)
                        for n in range(3):
                            rows3[four * 3 + n, pl.ds(a, 32, stride=2), :] = row[:, n * 128 : (n + 1) * 128]
        for tile in range(48):
            lane = tile % 24 * 128
            for n in range(2):
                part = rows3[tile, n * 32 : n * 32 + 32, :].astype(bf16)
                out_ref[n * 2 + tile // 24, :, lane : lane + 128] = part

        wait_all(start_all([(out_ref.at[n], target) for n, target in enumerate((out0, out1, out2, out3))], sems))


def sections23(received, c, c_sent, d, kernels):
    f32, bf16 = jnp.float32, jnp.bfloat16
    return kernel_call(
        sections23_body,
        tuple([jax.ShapeDtypeStruct((32, 3072), bf16)] * 4),
        [
            pltpu.VMEM((2, 320, 384), bf16),
            pltpu.VMEM((2240, 96), bf16),
            pltpu.VMEM((192, 5184), bf16),
            pltpu.VMEM((96, 3456), bf16),
            pltpu.VMEM((192, 1152), bf16),
            pltpu.VMEM((96, 1152), bf16),
            pltpu.VMEM((2560, 192), bf16),
            pltpu.VMEM((1600, 192), f32),
            pltpu.VMEM((1600, 576), bf16),
            pltpu.VMEM((960, 192), bf16),
            pltpu.VMEM((960, 1152), f32),
            pltpu.VMEM((2, 1920, 128), f32),
            pltpu.VMEM((3360, 96), f32),
            pltpu.VMEM((3360, 384), bf16),
            pltpu.VMEM((1120, 96), bf16),
            pltpu.VMEM((1120, 1152), f32),
            pltpu.VMEM((2, 2240, 128), f32),
            pltpu.VMEM((48, 64, 128), f32),
            pltpu.VMEM((4, 32, 3072), bf16),
        ],
        *received, c, c_sent, d, *kernels,
        copies=8,
        vmem=44,
    )


def beside_body(near_any, far_any, out_any, near, far, out, sems):
    wait_all(start_all([(near_any, near), (far_any, far)], sems))
    out[:, 0:432] = near[...]
    out[:, 432:864] = far[...]
    wait_all(start_all([(out, out_any)], sems))


def beside(near, far):
    shape, bf16 = (192, 864), jnp.bfloat16
    return kernel_call(
        beside_body,
        jax.ShapeDtypeStruct(shape, bf16),
        [pltpu.VMEM((192, 432), bf16), pltpu.VMEM((192, 432), bf16), pltpu.VMEM(shape, bf16)],
        near, far,
        copies=2,
        cost=15000000,
    )


def blank_body(*refs):
    pass


def blank(some, shapes):
    return kernel_call(blank_body, [jax.ShapeDtypeStruct(shape, jnp.bfloat16) for shape in shapes], [], some, copies=1)


LATER = ((192, 5184), (96, 3456), (192, 1152), (192, 5184), (96, 3456), (192, 1152), (640, 192), (640, 192), (2240, 96))


def sections01(latent, cache_a, cache_b, cache_c, cache_d, k, u):
    u_far = send(u, [((s_, h_ + 2, w_), (s_, h_, w_)) for s_ in (0, 1) for h_ in range(2) for w_ in range(2)])
    k_x, k_z = send(k, square((1,), 0, 1)), send(k, square((1,), 1, 0))
    gathered = lax.all_to_all(
        spread_tiles(latent, cache_a, cache_b), ("ha", "wa"), split_axis=0, concat_axis=0, tiled=True
    )
    ups = beside(u, u_far)
    u_z, u_x, u_d = (send(ups, square((0, 1), dh, dw)) for dh, dw in ((1, 0), (0, 1), (1, 1)))
    partial_sums = conv0(gathered, k)
    k_d = send(k_z, square((1,), 0, 1))
    partials = lax.all_to_all(partial_sums, ("ha", "wa"), split_axis=0, concat_axis=0, tiled=True)
    taps = join((ups, u_z, u_x, u_d))
    risen = up0(partials, taps)
    given = send(risen, [((0, h_, w_), (1, h_, w_)) for h_ in range(2) for w_ in range(2)])
    out1 = section1(given, gathered, (k, k_z, k_x, k_d), taps)
    return (out1, *blank(k, LATER))


def before_sections23(latent, cache_a, cache_b, cache_c, cache_d, k, u):
    own = jnp.concatenate([cache_c.reshape(16, 1536), cache_d.reshape(32, 1536)], axis=0)
    bands = [own] + [
        send(own, [((2, h_ + n, w_ ^ dw), (2, h_, w_)) for h_ in range(2) for w_ in range(2)])
        for n in range(3)
        for dw in range(2)
        if n + dw
    ]
    picked = pick(k, u)
    picked_x, picked_z, picked_d = (send(picked, square((2, 3), dh, dw)) for dh, dw in ((0, 1), (1, 0), (1, 1)))
    k2, k3, u23 = merge((picked, picked_z, picked_x, picked_d))
    pairs = [((s_, h_, w_), (s_ ^ 1, h_, w_)) for s_ in (2, 3) for h_ in range(2) for w_ in range(2)]
    rise, fall = [pair for pair in pairs if pair[0][0] == 2], [pair for pair in pairs if pair[0][0] == 3]
    c, d = caches(bands)
    c_sent, k2_sent, k3_sent, u_sent = send(c, rise), send(k2, rise), send(k3, fall), send(u23, pairs)
    return (*blank(k, ((320, 384),)), k2, k3, u23, k2_sent, k3_sent, u_sent, c, c_sent, d)


def relay(latent, cache_a, cache_b, cache_c, cache_d, conv_pack, up_pack):
    s, h, w = (lax.axis_index(axis) for axis in AXES)
    k, u = conv_pack[0].T, up_pack[0]
    out1, k2, k3, u23, k2_sent, k3_sent, u_sent, c, c_sent, d = lax.cond(
        s < 2, sections01, before_sections23, latent, cache_a, cache_b, cache_c, cache_d, k, u
    )
    received = [
        send(out1, [((1, h_, w_), (s_, h_, w_ ^ dw)) for h_ in range(2) for w_ in range(s_ - 1)])
        for dw in range(2)
        for s_ in (2, 3)
    ]
    blocks = sections23(received, c, c_sent, d, (k2, k2_sent, k3, k3_sent, u23, u_sent))

    arrived = [
        send(
            blocks[2 * n + half],
            [((2 + c_, z, x), (2 * c_ + x, 2 * z + n, half)) for c_ in range(2) for z in range(2) for x in range(2)],
        )
        for n in range(2)
        for half in range(2)
    ]
    lower_half = jnp.where(w == 0, arrived[2], arrived[3])
    upper_half = jnp.where(w == 0, arrived[0], arrived[1])
    return jnp.where(h % 2 == 0, upper_half, lower_half)[None]


def solution(mesh):
    in_specs = (
        P(None, "ha", "wa"),
        P(None, "ha", "wa"),
        P(None, "ha", "wa"),
        P(None, "ha", "wa"),
        P(None, "ha", "wa"),
        P("segment", "ha", "wa"),
        P("segment", "wa", "ha"),
    )
    out_specs = P("segment", "ha", "wa")
    sizes = tuple(mesh.shape[axis] for axis in AXES)
    program = relay if sizes == (4, 4, 2) else per_device
    return jax.shard_map(
        program, mesh=mesh, in_specs=in_specs, out_specs=out_specs, check_vma=False
    )
```

```python
from functools import partial

import jax
import jax.numpy as jnp
from jax import lax
from jax.experimental import pallas as pl
from jax.experimental.pallas import tpu as pltpu
from jax.sharding import PartitionSpec as P

WIDE = 384
MID = 192
NARROW = 96


EPSILON = 1e-06


def shortened(array):

    def short(part):
        return part.astype(jnp.bfloat16) if part.dtype == jnp.float32 else part

    return jax.tree.map(short, array)


def passed_along(value, axis, steps):
    count = lax.axis_size(axis)
    initial, last = (max(0, -steps), min(count, count - steps))
    return lax.ppermute(value, axis, [(source, source + steps) for source in range(initial, last)])


def layer_table():
    return ((WIDE, WIDE, MID), (MID, WIDE, MID), (MID, MID, NARROW), (NARROW, NARROW, NARROW))


def round_up(amount):
    return -(-amount // 128) * 128


def volume(target):
    amount = 1
    for extent in target:
        amount = amount * extent
    return amount


def flat_pad(tensor, length):
    leading = tensor.shape[0]
    packed = tensor.reshape(leading, -1)
    return jnp.pad(packed, ((0, 0), (0, length - packed.shape[1])))


def reshaped(packed, target):
    return packed[:, : volume(target)].reshape((packed.shape[0],) + tuple(target))


def add_rows(tensor, from_above, from_below):
    leading, height, width, channels = tensor.shape
    upper = reshaped(from_above, (1, width, channels))
    lower = reshaped(from_below, (1, width, channels))
    return jnp.concatenate([upper, tensor, lower], axis=1)


def add_cols(tensor, from_left, from_right):
    leading, height, width, channels = tensor.shape
    before = reshaped(from_left, (height, 1, channels))
    after = reshaped(from_right, (height, 1, channels))
    return jnp.concatenate([before, tensor, after], axis=2)


def trade_rows(upper_rim, bottom):
    return (
        jax.tree.map(
            lambda part, own: part.astype(own.dtype),
            passed_along(shortened(bottom), "ha", 1),
            bottom,
        ),
        jax.tree.map(
            lambda part, own: part.astype(own.dtype),
            passed_along(shortened(upper_rim), "ha", -1),
            upper_rim,
        ),
    )


def trade_cols(left_rim, right_rim):
    return (
        jax.tree.map(
            lambda part, own: part.astype(own.dtype),
            passed_along(shortened(right_rim), "wa", 1),
            right_rim,
        ),
        jax.tree.map(
            lambda part, own: part.astype(own.dtype),
            passed_along(shortened(left_rim), "wa", -1),
            left_rim,
        ),
    )


def causal_conv(stacked, kernel):
    result = lax.conv_general_dilated(
        stacked[None],
        kernel,
        (1, 1, 1),
        "VALID",
        dimension_numbers=("NDHWC", "DHWIO", "NDHWC"),
        preferred_element_type=jnp.float32,
    )
    return result[0, 0]


def activate(conv_sum):
    inverse = lax.rsqrt(jnp.mean(conv_sum * conv_sum, axis=-1, keepdims=True) + EPSILON)
    return jax.nn.silu(conv_sum * inverse).astype(jnp.bfloat16)


def upsample_conv(hidden_ext, kernel):
    expanded = jnp.repeat(jnp.repeat(hidden_ext, 2, axis=0), 2, axis=1)[1:-1, 1:-1]
    result = lax.conv_general_dilated(
        expanded[None],
        kernel,
        (1, 1),
        "VALID",
        dimension_numbers=("NHWC", "HWIO", "NHWC"),
        preferred_element_type=jnp.float32,
    )
    return result[0].astype(jnp.bfloat16)


def per_device(latent, cache_a, cache_b, cache_c, cache_d, conv_pack, up_pack):
    frames = latent.shape[0]
    tile_rows = latent.shape[1]
    tile_cols = latent.shape[2] // WIDE
    layers = layer_table()
    section = lax.axis_index("segment")
    segments = lax.axis_size("segment")
    final_segment = segments - 1
    input_shapes = [
        (tile_rows << level, tile_cols << level, layers[level][0]) for level in range(4)
    ]
    mid_shapes = [(tile_rows << level, tile_cols << level, layers[level][1]) for level in range(4)]
    out_shapes = [
        (tile_rows << level + 1, tile_cols << level + 1, layers[level][2]) for level in range(4)
    ]
    ext_shapes = [(target[0] + 2, target[1] + 2, target[2]) for target in input_shapes]
    all_shapes = input_shapes + mid_shapes
    row_length = round_up(max((target[1] * target[2] for target in all_shapes)))
    column_length = round_up(max(((target[0] + 2) * target[2] for target in all_shapes)))
    size_input = round_up(max((volume(target) for target in input_shapes)))
    size_middle = round_up(max((volume(target) for target in mid_shapes)))
    size_extended = round_up(max((volume(target) for target in ext_shapes)))
    size_output = round_up(max((volume(target) for target in out_shapes)))
    final_shape = out_shapes[3]
    final_count = volume(final_shape)
    conv_rows, up_rows = (
        lax.all_gather(conv_pack, "ha", axis=1, tiled=True),
        lax.all_gather(up_pack, "ha", axis=2, tiled=True),
    )
    conv_all, up_all = (
        lax.all_gather(conv_rows, "wa", axis=2, tiled=True),
        lax.all_gather(up_rows, "wa", axis=1, tiled=True),
    )

    def conv_kernel(level):
        width_in, width_mid, width_out = layers[level]
        columns = conv_all[0, : 27 * width_in, :: WIDE // width_mid]
        return columns.reshape(3, 3, 3, width_in, columns.shape[1])

    def up_kernel(level):
        width_in, width_mid, width_out = layers[level]
        rows_used = up_all[0, :: WIDE // width_mid, : 9 * width_out]
        return rows_used.reshape(width_mid, 3, 3, width_out).transpose(1, 2, 0, 3)

    conv_kernels = [conv_kernel(level) for level in range(4)]
    up_kernels = [up_kernel(level) for level in range(4)]

    def row_rims(packed, shapes):

        def rows_branch(level, packed):
            tensor = reshaped(packed, shapes[level])
            return (flat_pad(tensor[:, :1], row_length), flat_pad(tensor[:, -1:], row_length))

        upper_rim, bottom = lax.switch(
            section, [partial(rows_branch, level) for level in range(4)], packed
        )
        return trade_rows(upper_rim, bottom)

    def extend(packed, shapes):
        from_above, from_below = row_rims(packed, shapes)

        def cols_branch(level, packed, from_above, from_below):
            tensor = add_rows(reshaped(packed, shapes[level]), from_above, from_below)
            return (
                flat_pad(tensor[:, :, :1], column_length),
                flat_pad(tensor[:, :, -1:], column_length),
            )

        left_rim, right_rim = lax.switch(
            section,
            [partial(cols_branch, level) for level in range(4)],
            packed,
            from_above,
            from_below,
        )
        from_left, from_right = trade_cols(left_rim, right_rim)
        return (from_above, from_below, from_left, from_right)

    def assemble(packed, target, rims):
        tensor = add_rows(reshaped(packed, target), rims[0], rims[1])
        return add_cols(tensor, rims[2], rims[3])

    caches = (cache_a, cache_b, cache_c, cache_d)

    def cache_branch(level):
        return flat_pad(caches[level], size_input)

    cached = lax.switch(section, [partial(cache_branch, level) for level in range(4)])
    cache_rims = extend(cached, input_shapes)

    def store_branch(level, packed, rims):
        return flat_pad(assemble(packed, input_shapes[level], rims), size_extended)

    history = lax.switch(
        section, [partial(store_branch, level) for level in range(4)], cached, cache_rims
    )
    finished = jnp.zeros((frames, final_shape[0], final_shape[1] * final_shape[2]), jnp.bfloat16)
    stream = jnp.zeros((1, size_input), jnp.bfloat16)
    for moment in range(frames + segments - 1):
        if moment == 0:
            incoming = stream
        else:
            incoming = jax.tree.map(
                lambda part, own: part.astype(own.dtype),
                passed_along(shortened(stream), "segment", 1),
                stream,
            )
        frame_id = moment - section
        active = (frame_id >= 0) & (frame_id < frames)
        chosen = jnp.clip(frame_id, 0, frames - 1)
        picked = lax.dynamic_index_in_dim(latent, chosen, 0, keepdims=True)
        current = jnp.where(section == 0, flat_pad(picked, size_input), incoming)
        branch_id = jnp.where(active, section, 4)
        rims = extend(current, input_shapes)

        def conv_branch(level, current, history, rims):
            window = assemble(current, input_shapes[level], rims)
            earlier = reshaped(history, ext_shapes[level])
            hidden = activate(
                causal_conv(jnp.concatenate([earlier, window], axis=0), conv_kernels[level])
            )
            return (flat_pad(hidden[None], size_middle), flat_pad(window, size_extended))

        def spare_conv(current, history, rims):
            return (
                jnp.zeros((1, size_middle), jnp.bfloat16),
                jnp.zeros((1, size_extended), jnp.bfloat16),
            )

        hidden, window = lax.switch(
            branch_id,
            [partial(conv_branch, level) for level in range(4)] + [spare_conv],
            current,
            history,
            rims,
        )
        hidden_rims = extend(hidden, mid_shapes)

        def up_branch(level, hidden, hidden_rims):
            expanded = assemble(hidden, mid_shapes[level], hidden_rims)[0]
            return flat_pad(upsample_conv(expanded, up_kernels[level])[None], size_output)

        def spare_up(hidden, hidden_rims):
            return jnp.zeros((1, size_output), jnp.bfloat16)

        produced = lax.switch(
            branch_id,
            [partial(up_branch, level) for level in range(4)] + [spare_up],
            hidden,
            hidden_rims,
        )
        shifted = jnp.concatenate([history[1:], window], axis=0)
        history = jnp.where(active, shifted, history)
        stream = produced[:, :size_input]
        if moment >= final_segment:
            finished_id = moment - final_segment
            picture = produced[:, :final_count].reshape(
                1, final_shape[0], final_shape[1] * final_shape[2]
            )
            finished = finished.at[finished_id].set(picture[0])
    collected = lax.all_to_all(finished, "segment", split_axis=0, concat_axis=0, tiled=True)
    per_segment = frames // segments
    own_frame = collected[final_segment * per_segment : (final_segment + 1) * per_segment]
    return own_frame


AXES = ("segment", "ha", "wa")
MIB = 1024 * 1024


def place(s, h, w):
    return (s * 4 + h) * 2 + w


def send(value, pairs):
    return lax.ppermute(value, AXES, [(place(*a), place(*b)) for a, b in pairs])


def square(segments, dh, dw):
    return [
        ((s, h, w), (s, h ^ dh, w ^ dw)) for s in segments for h in range(2) for w in range(2)
    ]


def kernel_call(body, out_shape, scratch, *args, copies=0, vmem=16, cost=1000, place=pl.ANY):
    return pl.pallas_call(
        body,
        out_shape=out_shape,
        in_specs=[pl.BlockSpec(memory_space=place)] * len(args),
        out_specs=jax.tree.map(lambda _: pl.BlockSpec(memory_space=pl.ANY), out_shape),
        scratch_shapes=scratch + [pltpu.SemaphoreType.DMA((copies,))],
        compiler_params=pltpu.CompilerParams(vmem_limit_bytes=vmem * MIB),
        cost_estimate=pl.CostEstimate(flops=1000 * cost, bytes_accessed=1000, transcendentals=0),
    )(*args)


def start_all(pairs, sems, first=0):
    copies = [pltpu.make_async_copy(a, b, sems.at[first + n]) for n, (a, b) in enumerate(pairs)]
    for copy in copies:
        copy.start()
    return copies


def wait_all(copies):
    for copy in copies:
        copy.wait()


def dot(a, b):
    return jnp.dot(a, b, preferred_element_type=jnp.float32)


def dot_t(a, b):
    return lax.dot_general(a, b, (((1,), (1,)), ((), ())), preferred_element_type=jnp.float32)


def index_of(shape):
    return lax.broadcasted_iota(jnp.int32, shape, 0)


def silu(v):
    return v / (1.0 + jnp.exp(-v))


def shifts(base, pitch, width):
    n = base.shape[0]
    left, right = pltpu.roll(base, 1, 0), pltpu.roll(base, n - 1, 0)
    if pitch == width:
        column = index_of(base.shape) % pitch
        left = jnp.where(column == 0, 0.0, left)
        right = jnp.where(column == width - 1, 0.0, right)
    return left, base, right


def upsample(p_ref, t_ref, pitch, width, lanes):
    n = p_ref.shape[0]
    blocks = lanes // 128
    column = index_of((n, 128)) % pitch
    for block in range(blocks):

        def tap(dy, dx):
            at = (dy * 3 + dx) * lanes + block * 128
            return p_ref[:, at : at + 128]

        for b in range(2):
            rows = []
            for dy in range(3):
                middle = tap(dy, 1)
                if b == 0:
                    far = pltpu.roll(tap(dy, 0), 1, 0)
                    if pitch == width:
                        far = jnp.where(column == 0, 0.0, far)
                    rows.append(far + middle + tap(dy, 2))
                else:
                    far = pltpu.roll(tap(dy, 2), n - 1, 0)
                    if pitch == width:
                        far = jnp.where(column == width - 1, 0.0, far)
                    rows.append(tap(dy, 0) + middle + far)
            t_ref[block, pl.ds(b, n, stride=2), :] = pltpu.roll(rows[0], pitch, 0) + rows[1] + rows[2]
            t_ref[blocks + block, pl.ds(b, n, stride=2), :] = (
                rows[0] + rows[1] + pltpu.roll(rows[2], n - pitch, 0)
            )


def tiles_body(latent_any, a_any, b_any, out_any, latent, a, b, rows, out, sems):
    wait_all(start_all([(latent_any, latent), (a_any, a), (b_any, b)], sems))

    @pl.when(lax.axis_index("segment") == 0)
    def _():
        for frame in range(4):
            rows[frame * 2 : frame * 2 + 2] = latent[frame].astype(jnp.float32)
        for frame in range(2):
            rows[8 + frame * 2 : 10 + frame * 2] = a[frame].astype(jnp.float32)

    @pl.when(lax.axis_index("segment") > 0)
    def _():
        for frame in range(2):
            rows[frame * 4 : frame * 4 + 4] = b[frame].astype(jnp.float32)
        rows[8:12] = jnp.zeros((4, 768), jnp.float32)

    out[...] = rows[...].astype(jnp.bfloat16)
    wait_all(start_all([(out, out_any.at[n]) for n in range(8)], sems))


def spread_tiles(latent, cache_a, cache_b):
    bf16 = jnp.bfloat16
    return kernel_call(
        tiles_body,
        jax.ShapeDtypeStruct((8, 12, 768), bf16),
        [
            pltpu.VMEM((4, 2, 768), bf16),
            pltpu.VMEM((2, 2, 768), bf16),
            pltpu.VMEM((2, 4, 768), bf16),
            pltpu.VMEM((12, 768), jnp.float32),
            pltpu.VMEM((12, 768), bf16),
        ],
        latent, cache_a, cache_b,
        copies=8,
    )


def conv0_body(g_any, k_any, out_any, g_ref, k_ref, gf, base, xx, acc, buf, out_ref, sems):
    s, h = lax.axis_index("segment"), lax.axis_index("ha")

    @pl.when(s == 0)
    def _():
        coming = start_all([(g_any, g_ref), (k_any, k_ref)], sems)
        base[...] = jnp.zeros_like(base)
        coming[0].wait()
        gf[...] = g_ref[...].astype(jnp.float32)
        for frame in range(6):
            for hh in range(4):
                for ww in range(2):
                    for r in range(2):
                        row = 8 + frame * 2 + r if frame < 2 else (frame - 2) * 2 + r
                        for c in range(2):
                            at = frame * 160 + (1 + 2 * hh + r) * 16 + 2 * ww + c
                            base[at : at + 1, :] = gf[hh * 2 + ww, row : row + 1, c * 384 : (c + 1) * 384]
        for dx, moved in enumerate(shifts(base[...], 16, 4)):
            xx[dx] = moved.astype(jnp.bfloat16)
        coming[1].wait()
        for part in range(4):

            @pl.when(h == part)
            def _():
                for pair in range(2):
                    total = None
                    at, end = part * 2592, part * 2592 + 2592
                    while at < end:
                        tap, c0 = divmod(at, 384)
                        c1 = min(384, c0 + end - at)
                        dt, dy, dx = tap // 9, tap // 3 % 3, tap % 3
                        start = (dt + 2 * pair) * 160 + dy * 16
                        k0 = at - part * 2592
                        term = dot_t(xx[dx, start : start + 288, c0:c1], k_ref[:, k0 : k0 + c1 - c0])
                        total = term if total is None else total + term
                        at += c1 - c0
                    acc[pair * 320 : pair * 320 + 288] = total

        for frame in range(4):
            for r in range(8):
                to, at = (frame * 8 + r) * 4, frame * 160 + r * 16
                buf[to : to + 4, :] = acc[at : at + 4, :]
        out_ref[0:128, :] = buf[:, 0:128].astype(jnp.bfloat16)
        tail = jnp.concatenate([buf[0:64, 128:192], buf[64:128, 128:192]], axis=1)
        out_ref[128:192, :] = tail.astype(jnp.bfloat16)
        wait_all(start_all([(out_ref, out_any.at[n]) for n in range(8)], sems))


def conv0(gathered, k):
    f32, bf16 = jnp.float32, jnp.bfloat16
    return kernel_call(
        conv0_body,
        jax.ShapeDtypeStruct((8, 192, 128), bf16),
        [
            pltpu.VMEM((8, 12, 768), bf16),
            pltpu.VMEM((192, 2592), bf16),
            pltpu.VMEM((8, 12, 768), f32),
            pltpu.VMEM((960, 384), f32),
            pltpu.VMEM((3, 960, 384), bf16),
            pltpu.VMEM((608, 192), f32),
            pltpu.VMEM((128, 192), f32),
            pltpu.VMEM((192, 128), bf16),
        ],
        gathered, k,
        copies=8,
        cost=20 * 10**6,
    )


def join_body(own, nz, nx, nd, mine_any, other_any, cat, taps, sems):
    s, h = lax.axis_index("segment"), lax.axis_index("ha")

    @pl.when((s < 2) & (h < 2))
    def _():
        sending = []
        for half, (near, far, target) in enumerate(((own, nz, mine_any), (nx, nd, other_any))):
            for z in range(2):

                @pl.when(h == z)
                def _():
                    for first, pieces in ((z, near), (1 - z, far)):
                        for n in range(2):
                            at = (first + 2 * n) * 432
                            cat[:, at : at + 432] = pieces[:, n * 432 : (n + 1) * 432]

            for tap in range(9):
                taps[half, :, tap * 256 : tap * 256 + 192] = cat[:, tap * 192 : (tap + 1) * 192]
                taps[half, :, tap * 256 + 192 : (tap + 1) * 256] = jnp.zeros((192, 64), jnp.bfloat16)
            sending += start_all([(taps.at[half], target)], sems, half)
        wait_all(sending)


def join(pieces):
    bf16 = jnp.bfloat16
    return kernel_call(
        join_body,
        (jax.ShapeDtypeStruct((192, 2304), bf16), jax.ShapeDtypeStruct((192, 2304), bf16)),
        [pltpu.VMEM((192, 1728), bf16), pltpu.VMEM((2, 192, 2304), bf16)],
        *pieces,
        copies=2,
        vmem=62,
        cost=20 * 10**6,
        place=pltpu.VMEM,
    )


def up0_body(*refs):
    y_any, taps_any, out_any = refs[0], refs[1:3], refs[3]
    y, taps, hbuf, hs, p, t, out_ref, sems = refs[4:]
    s, h, w = (lax.axis_index(axis) for axis in AXES)

    @pl.when((s == 0) & (h < 2))
    def _():
        coming = start_all([(y_any, y)], sems)
        rising = start_all([(a, taps.at[n]) for n, a in enumerate(taps_any)], sems, 1)
        wait_all(coming)
        halves = []
        for side in range(2):
            total = y[side].astype(jnp.float32)
            for hh in range(1, 4):
                total = total + y[hh * 2 + side].astype(jnp.float32)
            tail = jnp.concatenate([total[128:192, 0:64], total[128:192, 64:128]], axis=0)
            halves.append(jnp.concatenate([total[0:128], tail], axis=1))
        squares = sum(jnp.sum(half * half, axis=1, keepdims=True) for half in halves)
        inverse = lax.rsqrt(squares / 384.0 + EPSILON)
        active = [silu(half * inverse) for half in halves]
        hs[...] = jnp.zeros_like(hs)
        for k in range(2):
            hbuf[...] = jnp.where(w == k, active[0], active[1])
            for frame in range(4):
                for r in range(8):
                    to, at = frame * 72 + r * 8, (frame * 8 + r) * 4
                    hs[k, to : to + 4, :] = hbuf[at : at + 4, :]
        wait_all(rising)
        p[...] = dot(hs[0].astype(jnp.bfloat16), taps[0]) + dot(hs[1].astype(jnp.bfloat16), taps[1])
        upsample(p, t, 8, 4, 256)
        column = index_of((16, 192))
        out_ref[...] = jnp.zeros_like(out_ref)
        for z in range(2):

            @pl.when(h == z)
            def _():
                for frame in range(4):
                    for r in range(11):
                        y = r + 5 * z
                        at = frame * 144 + (y // 2) * 16
                        to = frame * 192 + (r + 1 - z) * 16
                        for lane, count in ((0, 128), (128, 64)):
                            row = t[y % 2 * 2 + lane // 128, at : at + 16, 0:count]
                            row = jnp.where(column[:, 0:count] < 8, row, 0.0)
                            out_ref[to : to + 16, lane : lane + count] = row.astype(jnp.bfloat16)

        wait_all(start_all([(out_ref, out_any)], sems))


def up0(partials, ups):
    f32, bf16 = jnp.float32, jnp.bfloat16
    return kernel_call(
        up0_body,
        jax.ShapeDtypeStruct((768, 192), bf16),
        [
            pltpu.VMEM((8, 192, 128), bf16),
            pltpu.VMEM((2, 192, 2304), bf16),
            pltpu.VMEM((128, 192), f32),
            pltpu.VMEM((2, 288, 192), f32),
            pltpu.VMEM((288, 2304), f32),
            pltpu.VMEM((4, 576, 128), f32),
            pltpu.VMEM((768, 192), bf16),
        ],
        partials, *ups,
        copies=3,
        vmem=62,
    )


def group_rows(first, second, group):
    at, end = group * 576, group * 576 + 576
    if end <= 2592:
        return first[:, at:end]
    if at >= 2592:
        return second[:, at - 2592 : end - 2592]
    return jnp.concatenate([first[:, at:2592], second[:, 0 : end - 2592]], axis=1)


def section1_body(x_any, g_any, *refs):
    kernels_any, taps_any, out_any = refs[0:4], refs[4:6], refs[6]
    x_ref, g_ref = refs[7:9]
    k_own, k_z, k_x, k_d = refs[9:13]
    gf, full, base, xx, acc, hs, taps, p, t, out_ref, sems = refs[13:]
    s, h, w = (lax.axis_index(axis) for axis in AXES)

    @pl.when((s == 1) & (h < 2))
    def _():
        coming = start_all([(x_any, x_ref), (g_any, g_ref)], sems)
        arriving = start_all(list(zip(kernels_any, (k_own, k_z, k_x, k_d))), sems, 2)
        rising = start_all([(a, taps.at[n]) for n, a in enumerate(taps_any)], sems, 6)
        wait_all(coming)

        @pl.when(w == 0)
        def _():
            gf[...] = g_ref[...].astype(jnp.float32)
            full[...] = jnp.zeros_like(full)
            for frame in range(2):
                for hh in range(4):
                    for ww in range(2):
                        for r in range(4):
                            for c in range(4):
                                row = frame * 4 + r
                                at = frame * 288 + (1 + hh * 4 + r) * 16 + ww * 4 + c
                                full[at : at + 1, :] = gf[hh * 2 + ww, row : row + 1, c * 192 : (c + 1) * 192]
            for frame in range(2):
                start = pl.multiple_of(frame * 288 + h * 96, 32)
                base[frame * 192 : (frame + 1) * 192] = full[pl.ds(start, 192), :]
            base[384:768] = x_ref[0:384].astype(jnp.float32)

        @pl.when(w == 1)
        def _():
            base[...] = x_ref[...].astype(jnp.float32)

        for dx, moved in enumerate(shifts(base[...], 16, 8)):
            xx[:, dx * 192 : (dx + 1) * 192] = moved.astype(jnp.bfloat16)
        wait_all(arriving)
        for z in range(2):

            @pl.when(h == z)
            def _():
                for k, (mine, other) in enumerate(((k_own, k_z), (k_x, k_d))):
                    first, second = (mine, other) if z == 0 else (other, mine)
                    total = None
                    for group in range(9):
                        start = group // 3 * 192 + group % 3 * 16
                        term = dot_t(xx[start : start + 352, :], group_rows(first, second, group))
                        total = term if total is None else total + term
                    acc[k] = total

        squares = sum(jnp.sum(acc[k] * acc[k], axis=1, keepdims=True) for k in range(2))
        inverse = lax.rsqrt(squares / 384.0 + EPSILON)
        index = index_of((352, 192))
        keep = (index % 192 < 160) & (index % 16 < 8)
        for k in range(2):
            hs[k, 0:352] = jnp.where(keep, silu(acc[k] * inverse), 0.0).astype(jnp.bfloat16)
            hs[k, 352:384] = jnp.zeros((32, 192), jnp.bfloat16)
        wait_all(rising)
        p[...] = dot(hs[0], taps[0]) + dot(hs[1], taps[1])
        upsample(p, t, 16, 8, 256)
        out_ref[...] = jnp.zeros_like(out_ref)
        for z in range(2):

            @pl.when(h == z)
            def _():
                for frame in range(2):
                    for r in range(19):
                        y = r + z
                        at = frame * 384 + (y // 2) * 32
                        to = (r + 1 - z) * 16
                        for lane, count in ((0, 128), (128, 64)):
                            row = t[y % 2 * 2 + lane // 128, at : at + 16, 0:count].astype(jnp.bfloat16)
                            lane0 = frame * 192 + lane
                            out_ref[to : to + 16, lane0 : lane0 + count] = row

        wait_all(start_all([(out_ref, out_any)], sems))


def section1(frames, gathered, kernels, ups):
    f32, bf16 = jnp.float32, jnp.bfloat16
    return kernel_call(
        section1_body,
        jax.ShapeDtypeStruct((320, 384), bf16),
        [
            pltpu.VMEM((768, 192), bf16),
            pltpu.VMEM((8, 12, 768), bf16),
            *[pltpu.VMEM((192, 2592), bf16)] * 4,
            pltpu.VMEM((8, 12, 768), f32),
            pltpu.VMEM((576, 192), f32),
            pltpu.VMEM((768, 192), f32),
            pltpu.VMEM((768, 576), bf16),
            pltpu.VMEM((2, 352, 192), f32),
            pltpu.VMEM((2, 384, 192), bf16),
            pltpu.VMEM((2, 192, 2304), bf16),
            pltpu.VMEM((384, 2304), f32),
            pltpu.VMEM((4, 768, 128), f32),
            pltpu.VMEM((320, 384), bf16),
        ],
        frames, gathered, *kernels, *ups,
        copies=8,
        vmem=62,
    )


def pick_body(k_any, u_any, out_any, k, u, out, sems):
    s = lax.axis_index("segment")

    @pl.when(s >= 2)
    def _():
        coming = start_all([(k_any, k), (u_any, u)], sems)
        step = jnp.where(s == 2, 2, 4)
        source = lax.broadcasted_iota(jnp.int32, (96, 192), 1)
        target = lax.broadcasted_iota(jnp.int32, (96, 192), 0)
        picked = ((source == target * step) & (target * step < 192)).astype(jnp.bfloat16)
        wait_all(coming)
        out[:, 0:2592] = dot(picked, k[...]).astype(jnp.bfloat16)
        out[:, 2688:3120] = dot(picked, u[...]).astype(jnp.bfloat16)
        wait_all(start_all([(out, out_any)], sems))


def pick(k, u):
    bf16 = jnp.bfloat16
    return kernel_call(
        pick_body,
        jax.ShapeDtypeStruct((96, 3200), bf16),
        [pltpu.VMEM((192, 2592), bf16), pltpu.VMEM((192, 432), bf16), pltpu.VMEM((96, 3200), bf16)],
        k, u,
        copies=2,
    )


def merge_body(*refs):
    pieces_any, (k2_any, k3_any, up_any) = refs[0:4], refs[4:7]
    pieces = refs[7:11]
    k2, k3, cat, up, sems = refs[11:]
    s, h = lax.axis_index("segment"), lax.axis_index("ha")
    bf16 = jnp.bfloat16

    @pl.when((s >= 2) & (h < 2))
    def _():
        wait_all(start_all(list(zip(pieces_any, pieces)), sems))
        own, nz, nx, nd = pieces
        up[...] = jnp.zeros_like(up)
        for z in range(2):
            for segment, count in ((2, 96), (3, 48)):

                @pl.when((h == z) & (s == segment))
                def _():
                    for part, (a, b) in enumerate(((own, nx), (nz, nd))):
                        at = (part ^ z) * 432
                        cat[0:count, at : at + 432] = a[0:count, 2688:3120]
                        cat[count : 2 * count, at : at + 432] = b[0:count, 2688:3120]
                        if segment == 2:
                            at = (part ^ z) * 2592
                            k2[0:96, at : at + 2592] = a[:, 0:2592]
                            k2[96:192, at : at + 2592] = b[:, 0:2592]
                    if segment == 3:
                        a, b = ((own, nx), (nz, nd))[z]
                        k3[...] = jnp.zeros_like(k3)
                        for tap in range(27):
                            k3[0:48, tap * 128 : tap * 128 + 96] = a[0:48, tap * 96 : tap * 96 + 96]
                            k3[48:96, tap * 128 : tap * 128 + 96] = b[0:48, tap * 96 : tap * 96 + 96]

        for tap in range(9):
            up[:, tap * 128 : tap * 128 + 96] = cat[:, tap * 96 : (tap + 1) * 96]
        wait_all(start_all([(up, up_any), (k2, k2_any), (k3, k3_any)], sems))


def merge(pieces):
    bf16 = jnp.bfloat16
    shapes = ((192, 5184), (96, 3456), (192, 1152))
    return kernel_call(
        merge_body,
        tuple(jax.ShapeDtypeStruct(shape, bf16) for shape in shapes),
        [
            *[pltpu.VMEM((96, 3200), bf16)] * 4,
            pltpu.VMEM((192, 5184), bf16),
            pltpu.VMEM((96, 3456), bf16),
            pltpu.VMEM((192, 864), bf16),
            pltpu.VMEM((192, 1152), bf16),
        ],
        *pieces,
        copies=4,
        vmem=12,
    )


def caches_body(*refs):
    parts, (c_any, d_any) = refs[0:6], refs[6:8]
    bands, wide, c_full, d_full, c, d, sems = refs[8:]
    s, h, w = (lax.axis_index(axis) for axis in AXES)
    f32, bf16 = jnp.float32, jnp.bfloat16

    @pl.when((s == 2) & (h < 2))
    def _():
        pairs = [(a, bands.at[n // 2, n % 2 * 48 : n % 2 * 48 + 48]) for n, a in enumerate(parts)]
        wait_all(start_all(pairs, sems))
        c_full[...] = jnp.zeros_like(c_full)
        d_full[...] = jnp.zeros_like(d_full)
        for band in range(3):
            wide[...] = bands[band].astype(f32)
            for side in range(2):
                swapped = (w + side) % 2
                for frame in range(2):
                    row = side * 48 + frame * 8
                    for column in range(8):
                        at = (frame * 26 + 1 + band * 8) * 16 + swapped * 8 + column
                        lane = column * 192
                        c_full[0, pl.ds(at, 8, stride=16), :] = wide[row : row + 8, lane : lane + 128]
                        tail = jnp.concatenate([wide[row : row + 8, lane + 128 : lane + 192]] * 2, axis=1)
                        c_full[1, pl.ds(at, 8, stride=16), :] = tail
                    row = side * 48 + 16 + frame * 16
                    for column in range(16):
                        at = (frame * 50 + 1 + band * 16) * 32 + swapped * 16 + column
                        lane = column * 96
                        part = wide[row : row + 16, lane : lane + 96]
                        part = jnp.concatenate([part, part[:, 0:32]], axis=1)
                        d_full[pl.ds(at, 16, stride=32), :] = part
        for frame in range(2):
            at = pl.multiple_of((frame * 26 + h * 6) * 16, 32)
            c[frame * 320 : frame * 320 + 320, 0:128] = c_full[0, pl.ds(at, 320), :].astype(bf16)
            c[frame * 320 : frame * 320 + 320, 128:192] = c_full[1, pl.ds(at, 320), 0:64].astype(bf16)
            at = pl.multiple_of((frame * 50 + h * 15) * 32, 32)
            d[frame * 1120 : frame * 1120 + 1120, :] = d_full[pl.ds(at, 1120), 0:96].astype(bf16)
        wait_all(start_all([(c, c_any), (d, d_any)], sems))


def caches(bands):
    f32, bf16 = jnp.float32, jnp.bfloat16
    return kernel_call(
        caches_body,
        (jax.ShapeDtypeStruct((640, 192), bf16), jax.ShapeDtypeStruct((2240, 96), bf16)),
        [
            pltpu.VMEM((3, 96, 1536), bf16),
            pltpu.VMEM((96, 1536), f32),
            pltpu.VMEM((2, 832, 128), f32),
            pltpu.VMEM((3200, 128), f32),
            pltpu.VMEM((640, 192), bf16),
            pltpu.VMEM((2240, 96), bf16),
        ],
        *bands,
        copies=6,
        vmem=16,
        cost=60 * 10**6,
    )


def sections23_body(same2, same3, other2, other3, c_own, c_sent, d_any, k2_own, k2_sent, k3_own, k3_sent, u_own, u_sent,
                    out0, out1, out2, out3, pairs, d_ref, k2, k3, u2, u3, line, base, xx, hs, p, t, base3, xx3, hs3, p3, t3, rows3, out_ref,
                    sems):
    s, h, w = (lax.axis_index(axis) for axis in AXES)
    f32, bf16 = jnp.float32, jnp.bfloat16

    @pl.when((s >= 2) & (h < 2))
    def _():
        frame = (s - 2) * 2 + w
        line[0:640] = jnp.zeros((640, 192), bf16)
        for segment, same, other in ((2, same2, other2), (3, same3, other3)):

            @pl.when(s == segment)
            def _():
                c_any = c_own if segment == 2 else c_sent
                held2, held3 = (k2_own, k3_sent) if segment == 2 else (k2_sent, k3_own)
                up2, up3 = (u_own, u_sent) if segment == 2 else (u_sent, u_own)
                start_all(
                    [
                        (same, pairs.at[w]),
                        (other, pairs.at[1 - w]),
                        (c_any, line.at[640:1280]),
                        (held2, k2),
                        (up2, u2),
                        (d_any, d_ref),
                        (held3, k3),
                        (up3.at[0:96], u3),
                    ],
                    sems,
                )

        coming = [
            pltpu.make_async_copy(a, b, sems.at[n])
            for n, (a, b) in enumerate(
                [
                    (same2, pairs.at[0]),
                    (other2, pairs.at[1]),
                    (c_own, line.at[640:1280]),
                    (k2_own, k2),
                    (u_own, u2),
                    (d_any, d_ref),
                    (k3_own, k3),
                    (u_own.at[0:96], u3),
                ]
            )
        ]
        wait_all(coming[0:3])
        for number in range(2):
            for k in range(2):
                at = 1280 + (2 * number + k) * 320
                line[at : at + 320] = pairs[number, :, k * 192 : (k + 1) * 192]

        base[...] = line[pl.ds(pl.multiple_of(frame * 320, 320), 1600), :].astype(f32)
        for dx, moved in enumerate(shifts(base[...], 16, 16)):
            xx[:, dx * 192 : (dx + 1) * 192] = moved.astype(bf16)
        coming[3].wait()
        for moment in range(3):
            total = None
            for group in range(9):
                start = (group // 3 + moment) * 320 + group % 3 * 16
                term = dot_t(xx[start : start + 288, :], k2[:, group * 576 : (group + 1) * 576])
                total = term if total is None else total + term
            inverse = lax.rsqrt(jnp.sum(total * total, axis=1, keepdims=True) / 192.0 + EPSILON)
            at = moment * 320
            hs[at : at + 288] = silu(total * inverse).astype(bf16)
            hs[moment * 320 + 288 : moment * 320 + 320] = jnp.zeros((32, 192), bf16)
        coming[4].wait()
        p[...] = dot(hs[...], u2[...])
        upsample(p, t, 16, 16, 128)

        for z in range(2):

            @pl.when(h == z)
            def _():
                blank = 0 if z == 0 else 34
                for moment in range(3):
                    to = moment * 1120 + blank * 32
                    base3[to : to + 32] = jnp.zeros((32, 96), f32)
                    for r in range(34):
                        y = r + 2 * z
                        at = moment * 640 + (y // 2) * 32
                        to = moment * 1120 + (r + 1 - z) * 32
                        base3[to : to + 32] = t[y % 2, at : at + 32, 0:96].astype(bf16).astype(f32)

        wait_all(coming[5:8])

        @pl.when(frame == 0)
        def _():
            base3[0:2240] = d_ref[...].astype(f32)

        @pl.when(frame == 1)
        def _():
            base3[0:1120] = d_ref[1120:2240].astype(f32)

        xx3[...] = jnp.zeros_like(xx3)
        for dx, moved in enumerate(shifts(base3[...], 32, 32)):
            xx3[:, dx * 128 : dx * 128 + 96] = moved.astype(bf16)
        total = None
        for group in range(9):
            start = group // 3 * 1120 + group % 3 * 32
            term = dot_t(xx3[start : start + 1056, :], k3[:, group * 384 : (group + 1) * 384])
            total = term if total is None else total + term
        inverse = lax.rsqrt(jnp.sum(total * total, axis=1, keepdims=True) / 96.0 + EPSILON)
        hs3[0:1056] = silu(total * inverse).astype(bf16)
        hs3[1056:1120] = jnp.zeros((64, 96), bf16)
        p3[...] = dot(hs3[...], u3[...])
        upsample(p3, t3, 32, 32, 128)
        for z in range(2):

            @pl.when(h == z)
            def _():
                for a in range(2):
                    for four in range(16):
                        parts = [
                            t3[a, pl.ds(z * 64 + four * 4 + n, 32, stride=64), :][:, 0:96] for n in range(4)
                        ]
                        row = jnp.concatenate(parts, axis=1)
                        for n in range(3):
                            rows3[four * 3 + n, pl.ds(a, 32, stride=2), :] = row[:, n * 128 : (n + 1) * 128]
        for tile in range(48):
            lane = tile % 24 * 128
            for n in range(2):
                part = rows3[tile, n * 32 : n * 32 + 32, :].astype(bf16)
                out_ref[n * 2 + tile // 24, :, lane : lane + 128] = part

        wait_all(start_all([(out_ref.at[n], target) for n, target in enumerate((out0, out1, out2, out3))], sems))


def sections23(received, c, c_sent, d, kernels):
    f32, bf16 = jnp.float32, jnp.bfloat16
    return kernel_call(
        sections23_body,
        tuple([jax.ShapeDtypeStruct((32, 3072), bf16)] * 4),
        [
            pltpu.VMEM((2, 320, 384), bf16),
            pltpu.VMEM((2240, 96), bf16),
            pltpu.VMEM((192, 5184), bf16),
            pltpu.VMEM((96, 3456), bf16),
            pltpu.VMEM((192, 1152), bf16),
            pltpu.VMEM((96, 1152), bf16),
            pltpu.VMEM((2560, 192), bf16),
            pltpu.VMEM((1600, 192), f32),
            pltpu.VMEM((1600, 576), bf16),
            pltpu.VMEM((960, 192), bf16),
            pltpu.VMEM((960, 1152), f32),
            pltpu.VMEM((2, 1920, 128), f32),
            pltpu.VMEM((3360, 96), f32),
            pltpu.VMEM((3360, 384), bf16),
            pltpu.VMEM((1120, 96), bf16),
            pltpu.VMEM((1120, 1152), f32),
            pltpu.VMEM((2, 2240, 128), f32),
            pltpu.VMEM((48, 64, 128), f32),
            pltpu.VMEM((4, 32, 3072), bf16),
        ],
        *received, c, c_sent, d, *kernels,
        copies=8,
        vmem=44,
    )


def beside_body(near_any, far_any, out_any, near, far, out, sems):
    wait_all(start_all([(near_any, near), (far_any, far)], sems))
    out[:, 0:432] = near[...]
    out[:, 432:864] = far[...]
    wait_all(start_all([(out, out_any)], sems))


def beside(near, far):
    shape, bf16 = (192, 864), jnp.bfloat16
    return kernel_call(
        beside_body,
        jax.ShapeDtypeStruct(shape, bf16),
        [pltpu.VMEM((192, 432), bf16), pltpu.VMEM((192, 432), bf16), pltpu.VMEM(shape, bf16)],
        near, far,
        copies=2,
        cost=15000000,
    )


def blank_body(*refs):
    pass


def blank(some, shapes):
    return kernel_call(blank_body, [jax.ShapeDtypeStruct(shape, jnp.bfloat16) for shape in shapes], [], some, copies=1)


LATER = ((192, 5184), (96, 3456), (192, 1152), (192, 5184), (96, 3456), (192, 1152), (640, 192), (640, 192), (2240, 96))


def sections01(latent, cache_a, cache_b, cache_c, cache_d, k, u):
    u_far = send(u, [((s_, h_ + 2, w_), (s_, h_, w_)) for s_ in (0, 1) for h_ in range(2) for w_ in range(2)])
    k_x, k_z = send(k, square((1,), 0, 1)), send(k, square((1,), 1, 0))
    gathered = lax.all_to_all(
        spread_tiles(latent, cache_a, cache_b), ("ha", "wa"), split_axis=0, concat_axis=0, tiled=True
    )
    ups = beside(u, u_far)
    u_z, u_x, u_d = (send(ups, square((0, 1), dh, dw)) for dh, dw in ((1, 0), (0, 1), (1, 1)))
    partial_sums = conv0(gathered, k)
    k_d = send(k_z, square((1,), 0, 1))
    partials = lax.all_to_all(partial_sums, ("ha", "wa"), split_axis=0, concat_axis=0, tiled=True)
    taps = join((ups, u_z, u_x, u_d))
    risen = up0(partials, taps)
    given = send(risen, [((0, h_, w_), (1, h_, w_)) for h_ in range(2) for w_ in range(2)])
    out1 = section1(given, gathered, (k, k_z, k_x, k_d), taps)
    return (out1, *blank(k, LATER))


def before_sections23(latent, cache_a, cache_b, cache_c, cache_d, k, u):
    own = jnp.concatenate([cache_c.reshape(16, 1536), cache_d.reshape(32, 1536)], axis=0)
    bands = [own] + [
        send(own, [((2, h_ + n, w_ ^ dw), (2, h_, w_)) for h_ in range(2) for w_ in range(2)])
        for n in range(3)
        for dw in range(2)
        if n + dw
    ]
    picked = pick(k, u)
    picked_x, picked_z, picked_d = (send(picked, square((2, 3), dh, dw)) for dh, dw in ((0, 1), (1, 0), (1, 1)))
    k2, k3, u23 = merge((picked, picked_z, picked_x, picked_d))
    pairs = [((s_, h_, w_), (s_ ^ 1, h_, w_)) for s_ in (2, 3) for h_ in range(2) for w_ in range(2)]
    rise, fall = [pair for pair in pairs if pair[0][0] == 2], [pair for pair in pairs if pair[0][0] == 3]
    c, d = caches(bands)
    c_sent, k2_sent, k3_sent, u_sent = send(c, rise), send(k2, rise), send(k3, fall), send(u23, pairs)
    return (*blank(k, ((320, 384),)), k2, k3, u23, k2_sent, k3_sent, u_sent, c, c_sent, d)


def relay(latent, cache_a, cache_b, cache_c, cache_d, conv_pack, up_pack):
    s, h, w = (lax.axis_index(axis) for axis in AXES)
    k, u = conv_pack[0].T, up_pack[0]
    out1, k2, k3, u23, k2_sent, k3_sent, u_sent, c, c_sent, d = lax.cond(
        s < 2, sections01, before_sections23, latent, cache_a, cache_b, cache_c, cache_d, k, u
    )
    received = [
        send(out1, [((1, h_, w_), (s_, h_, w_ ^ dw)) for h_ in range(2) for w_ in range(s_ - 1)])
        for dw in range(2)
        for s_ in (2, 3)
    ]
    blocks = sections23(received, c, c_sent, d, (k2, k2_sent, k3, k3_sent, u23, u_sent))

    arrived = [
        send(
            blocks[2 * n + half],
            [((2 + c_, z, x), (2 * c_ + x, 2 * z + n, half)) for c_ in range(2) for z in range(2) for x in range(2)],
        )
        for n in range(2)
        for half in range(2)
    ]
    lower_half = jnp.where(w == 0, arrived[2], arrived[3])
    upper_half = jnp.where(w == 0, arrived[0], arrived[1])
    return jnp.where(h % 2 == 0, upper_half, lower_half)[None]


def solution(mesh):
    in_specs = (
        P(None, "ha", "wa"),
        P(None, "ha", "wa"),
        P(None, "ha", "wa"),
        P(None, "ha", "wa"),
        P(None, "ha", "wa"),
        P("segment", "ha", "wa"),
        P("segment", "wa", "ha"),
    )
    out_specs = P("segment", "ha", "wa")
    sizes = tuple(mesh.shape[axis] for axis in AXES)
    program = relay if sizes == (4, 4, 2) else per_device
    return jax.shard_map(
        program, mesh=mesh, in_specs=in_specs, out_specs=out_specs, check_vma=False
    )
```
